256 devices in a mesh: seq: 32 (over z, x_lo, core), head: 8 (over y, x_hi).
Axes of the slice: x: 4 (x_hi: 2, x_lo: 2; x = x_hi * 2 + x_lo), y: 4, z: 8, core: 2. Of those that a mesh axis runs over, the one named last changes fastest.
Arguments:
- queries: bfloat16 [8192, 3072], P('seq', 'head'), may hold values from -6 to 6
- key_states: bfloat16 [8192, 3072], P('seq', 'head'), may hold values from -6 to 6
- value_states: bfloat16 [8192, 3072], P('seq', 'head'), may hold values from -6 to 6
- block_list: int32 [32, 27], P('seq'), may hold values from -1 to 31, as said below
- text_slots: int32 [2], replicated, may hold values from 0 to 31, as said below
- out_weight: bfloat16 [3072, 3072], P('head'), may hold values from -0.15625 to 0.15625
Outputs:
- mixed: bfloat16 [8192, 3072], P('seq', 'head')
The draws below stay inside these ranges and needn't reach their ends.
Inputs may be any that keep to these rules, and one draw needn't show every extreme that they name: `block_list`: video tiles are numbered slab by slab in a grid of 4 x 4 tiles a frame slab, the last slab possibly partial, and occupy the slots that are not text slots in increasing order of their numbers. Row i lists, in a fixed order of the 27 offsets in -1..1 along the three dimensions, the slots of the existing video tiles next to or equal to the video tile in slot i, with -1 where the tile does not exist; rows of text slots are all -1. `text_slots`: the distinct slots of the text tiles in increasing order; the last slot is always one of them; no row of block_list names them.
All inputs are finite; a program needn't handle non-finite values.
Results may differ from the reference program's by a relative error of at most 0.0057.
Values may be sent and summed in bfloat16 or wider, within the bound.
No kernel may reach another device: no remote copies, remote signals or barrier semaphores. Data moves between devices by JAX's collectives and lax.ppermute only.
A program may use at most 128 MiB of HBM per device.

```python
import math
import jax
import jax.numpy as jnp
from jax import lax

HEADS = 24
HD = 128
TILE = 256
WIN = 27
GRID_SIDE = 4
NTEXT = 2
D = 3072
TILES = 32
NVIDEO = 30
TOKENS = 8192


def tile_layout(key):
    others = jax.random.permutation(key, TILES - 1).astype(jnp.int32)[:NTEXT - 1]
    last_slot = jnp.full((1,), TILES - 1, jnp.int32)
    text_part = jnp.sort(jnp.concatenate([others, last_slot])).astype(jnp.int32)
    slot_ids = jnp.arange(TILES, dtype=jnp.int32)
    is_text = jnp.any(slot_ids[:, None] == text_part[None, :], axis=1).astype(jnp.int32)
    slot_order = jnp.argsort(is_text, stable=True).astype(jnp.int32)
    video_ids = jnp.arange(NVIDEO, dtype=jnp.int32)
    slab_index = video_ids // (GRID_SIDE * GRID_SIDE)
    row_index = video_ids // GRID_SIDE % GRID_SIDE
    col_index = video_ids % GRID_SIDE
    offsets = jnp.arange(WIN, dtype=jnp.int32)
    time_step = offsets // 9 - 1
    row_step = offsets // 3 % 3 - 1
    col_step = offsets % 3 - 1
    slab_near = slab_index[:, None] + time_step[None, :]
    row_near = row_index[:, None] + row_step[None, :]
    col_near = col_index[:, None] + col_step[None, :]
    neighbour = slab_near * (GRID_SIDE * GRID_SIDE) + row_near * GRID_SIDE + col_near
    present = (slab_near >= 0) & (row_near >= 0) & (row_near < GRID_SIDE) & (col_near >= 0) & (col_near < GRID_SIDE) & (neighbour < NVIDEO)
    listed = jnp.where(present, slot_order[jnp.clip(neighbour, 0, NVIDEO - 1)], -1)
    slot_table = jnp.full((TILES, WIN), -1, jnp.int32).at[slot_order[:NVIDEO]].set(listed)
    return (slot_table, text_part)


def draw_block_list(key, part):
    slot_table, text_part = tile_layout(key)
    return slot_table.astype(jnp.int32)


def draw_text_slots(key, part):
    slot_table, text_part = tile_layout(key)
    return text_part.astype(jnp.int32)


def draw_queries(key, part):
    key = jax.random.fold_in(key, 11)
    first_key = jax.random.fold_in(key, 0)
    result = jnp.clip(jax.random.normal(first_key, (TOKENS, D), jnp.float32), -6.0, 6.0)
    return result.astype(jnp.bfloat16)


def draw_key_states(key, part):
    key = jax.random.fold_in(key, 12)
    first_key = jax.random.fold_in(key, 0)
    result = jnp.clip(jax.random.normal(first_key, (TOKENS, D), jnp.float32), -6.0, 6.0)
    return result.astype(jnp.bfloat16)


def with_spikes(values, own_key, source, target, blocks, factor):
    owner, partner = [(jnp.arange(values.shape[dim]) // (values.shape[dim] // blocks)).reshape([-1 if axis == dim else 1 for axis in range(values.ndim)]) for dim in (source, target)]
    chosen = jax.random.permutation(own_key, blocks)[partner]
    strong = (owner == chosen) | (owner == (partner + blocks // 2) % blocks)
    return jnp.where(strong, factor * values, values)


def shard_levels(own_key, dims, shards, smallest, largest):
    gain, own = 1.0, jax.random.fold_in(own_key, 6)
    for dim, blocks in shards:
        heights = jnp.exp(jax.random.uniform(jax.random.fold_in(own, dim), (blocks,), jnp.float32, smallest / len(shards), largest / len(shards)))
        gain = gain * jnp.repeat(heights, dims[dim] // blocks).reshape([-1 if axis == dim else 1 for axis in range(len(dims))])
    return gain


def scatter_about(rng, shape, scale, limit, cuts=(), held_as=jnp.bfloat16):
    level = shard_levels(rng, shape, cuts, -0.22, 0.18) if cuts else 1.0
    entries = jax.random.normal(rng, shape, jnp.float32) * scale * level
    return jnp.minimum(jnp.maximum(entries, -limit), limit).astype(held_as)


def noise_with(key, shape, deviation, most, cuts, heavy, held_as=jnp.bfloat16):
    array = deviation * jax.random.normal(key, shape, jnp.float32)
    if cuts:
        array = array * shard_levels(key, shape, cuts, -0.22, 0.18)
    return jnp.clip(with_spikes(array, jax.random.fold_in(key, 3), *heavy), -most, most).astype(held_as)


def setup_inputs(seed: int = 0) -> dict:
    arg_keys = jax.random.split(jax.random.key(seed), 7)
    return {
        "queries": draw_queries(jax.random.fold_in(arg_keys[6], 71), 0),
        "key_states": draw_key_states(jax.random.fold_in(arg_keys[6], 71), 0),
        "value_states": scatter_about(arg_keys[2], (TOKENS, D), 1.0, 6.0, ((0, 32), (1, 8))),
        "block_list": draw_block_list(jax.random.fold_in(arg_keys[6], 71), 0),
        "text_slots": draw_text_slots(jax.random.fold_in(arg_keys[6], 71), 0),
        "out_weight": noise_with(arg_keys[5], (D, D), D ** -0.5, 0.15625, ((0, 8),), (0, 1, 8, 2.0)),
    }


def reference(queries, key_states, value_states, block_list, text_slots, out_weight):
    tile_count = TOKENS // TILE
    score_scale = 1.0 / math.sqrt(HD)
    query_tiles = queries.reshape(tile_count, TILE, HEADS, HD)
    key_tiles = key_states.reshape(tile_count, TILE, HEADS, HD)
    value_tiles = value_states.reshape(tile_count, TILE, HEADS, HD)
    key_lists = jnp.concatenate([block_list, jnp.broadcast_to(text_slots[None, :], (tile_count, NTEXT))], axis=1)

    def one_tile(operands):
        query_tile, listed = operands
        present = listed >= 0
        chosen = jnp.where(present, listed, 0).astype(jnp.int32)
        key_rows = key_tiles[chosen].reshape(-1, HEADS, HD).astype(jnp.float32)
        value_rows = value_tiles[chosen].reshape(-1, HEADS, HD).astype(jnp.float32)
        scores = jnp.einsum('qhd,khd->hqk', query_tile.astype(jnp.float32), key_rows) * score_scale
        wanted = jnp.repeat(present, TILE)
        scores = jnp.where(wanted[None, None, :], scores, -jnp.inf)
        peak = lax.optimization_barrier(jnp.max(scores, axis=-1, keepdims=True))
        weights = jnp.exp(scores - peak)
        total = lax.optimization_barrier(jnp.sum(weights, axis=-1))
        weighted = jnp.einsum('hqk,khd->qhd', weights.astype(jnp.bfloat16).astype(jnp.float32), value_rows)
        return (weighted / total.T[..., None]).astype(jnp.bfloat16)
    attended = lax.map(one_tile, (query_tiles, key_lists)).reshape(TOKENS, D)
    return jnp.dot(attended, out_weight, preferred_element_type=jnp.float32).astype(jnp.bfloat16)
```

```python
import functools
import math

import jax
import jax.numpy as jnp
from jax import lax
from jax.experimental import pallas as pl
from jax.experimental.pallas import tpu as pltpu
from jax.sharding import PartitionSpec as P

HD = 128
TILE = 256
GROUP = 4
PART_ROWS = 16
LOWEST = -1e30
LOG2E = math.log2(math.e)


def write_part(ref, index, outs, sums):
    heads = len(outs)
    for h in range(heads):
        ref[index, h * HD:(h + 1) * HD, :] = outs[h].astype(jnp.bfloat16)
    rows = jnp.concatenate(sums + [jnp.zeros((8 - heads, TILE), jnp.float32)], axis=0)
    high = rows.astype(jnp.bfloat16).astype(jnp.float32)
    middle = (rows - high).astype(jnp.bfloat16).astype(jnp.float32)
    low = rows - high - middle
    block = jnp.concatenate([high, middle], axis=0).astype(jnp.bfloat16)
    last = jnp.concatenate([low, jnp.zeros_like(low)], axis=0).astype(jnp.bfloat16)
    base = heads * HD
    ref[index, base:base + 16, :] = block
    ref[index, base + 16:base + 32, :] = last


def read_sums(ref, index, heads):
    base = heads * HD
    block = ref[index, base:base + 16, :].astype(jnp.float32)
    last = ref[index, base + 16:base + 32, :].astype(jnp.float32)
    return block[0:8] + block[8:16] + last[0:8]


def merged(ref_a, index_a, ref_b, index_b, heads):
    sums_a = read_sums(ref_a, index_a, heads)
    sums_b = read_sums(ref_b, index_b, heads)
    top = jnp.maximum(sums_a, sums_b)
    weight_a = jnp.exp2(sums_a - top)
    weight_b = jnp.exp2(sums_b - top)
    total = weight_a + weight_b
    scale_a = weight_a / total
    scale_b = weight_b / total
    sums = top + jnp.log2(total)
    outs = []
    for h in range(heads):
        part_a = ref_a[index_a, h * HD:(h + 1) * HD, :].astype(jnp.float32)
        part_b = ref_b[index_b, h * HD:(h + 1) * HD, :].astype(jnp.float32)
        outs.append(part_a * scale_a[h:h + 1] + part_b * scale_b[h:h + 1])
    return outs, [sums[h:h + 1] for h in range(heads)]


def attend_kernel(factor, need_ref, q_ref, kv_ref, out_ref, acc_ref, peak_ref, total_ref):
    tiles = q_ref.shape[0]
    heads = q_ref.shape[2] // HD
    keys = kv_ref.shape[0]
    acc_ref[...] = jnp.zeros_like(acc_ref)
    peak_ref[...] = jnp.full_like(peak_ref, LOWEST)
    total_ref[...] = jnp.zeros_like(total_ref)

    def visit(step, carry):
        z = step // tiles
        t = step % tiles

        @pl.when(need_ref[t, z] > 0)
        def _():
            for h in range(heads):
                cols = slice(h * HD, (h + 1) * HD)
                query = q_ref[t, :, cols]
                key = kv_ref[z, 0:TILE, cols]
                value = kv_ref[z, TILE:2 * TILE, cols]
                scores = lax.dot_general(
                    key, query, (((1,), (1,)), ((), ())), preferred_element_type=jnp.float32
                )
                row = t * heads + h
                old = peak_ref[row]
                peak = jnp.maximum(old, jnp.max(scores, axis=0, keepdims=True) * factor)
                weights = jnp.exp2(scores * factor - peak)
                shrink = jnp.exp2(old - peak)
                peak_ref[row] = peak
                total_ref[row] = total_ref[row] * shrink + jnp.sum(weights, axis=0, keepdims=True)
                acc_ref[row] = acc_ref[row] * shrink + lax.dot_general(
                    value,
                    weights.astype(jnp.bfloat16),
                    (((0,), (0,)), ((), ())),
                    preferred_element_type=jnp.float32,
                )

        return carry

    lax.fori_loop(0, keys * tiles, visit, 0)
    for t in range(tiles):
        outs, sums = [], []
        for h in range(heads):
            row = t * heads + h
            total = total_ref[row]
            held = total > 0.0
            safe = jnp.where(held, total, 1.0)
            outs.append(acc_ref[row] / safe)
            sums.append(jnp.where(held, peak_ref[row] + jnp.log2(safe), LOWEST))
        write_part(out_ref, t, outs, sums)


def merge_kernel(mine_ref, other_ref, keep_ref, send_ref):
    heads = mine_ref.shape[1] // HD
    outs, sums = merged(mine_ref, 2, other_ref, 1, heads)
    write_part(send_ref, 0, outs, sums)
    outs, sums = merged(mine_ref, 0, other_ref, 0, heads)
    write_part(keep_ref, 0, outs, sums)


def project_kernel(keep_ref, other_ref, weight_ref, out_ref, held_ref):
    heads = keep_ref.shape[1] // HD
    outs, _ = merged(keep_ref, 0, other_ref, 0, heads)
    for h in range(heads):
        held_ref[h * HD:(h + 1) * HD, :] = outs[h].astype(jnp.bfloat16)
    shares, _, width = out_ref.shape
    attended = held_ref[...].T
    for j in range(shares):
        out_ref[j] = jnp.dot(
            attended, weight_ref[:, j * width:(j + 1) * width], preferred_element_type=jnp.float32
        ).astype(jnp.bfloat16)


def vmem_specs(count):
    return [pl.BlockSpec(memory_space=pltpu.VMEM)] * count


def per_device(seq_size, head_size, queries, key_states, value_states, block_list, text_slots, out_weight):
    width = queries.shape[1]
    heads = width // HD
    planes = seq_size // GROUP
    me = lax.axis_index("seq")
    swap_core = [(s, s ^ 1) for s in range(seq_size)]
    swap_chip = [(s, s ^ 2) for s in range(seq_size)]
    z_groups = [[z * GROUP + d for z in range(planes)] for d in range(GROUP)]

    both = jnp.concatenate([key_states, value_states], axis=0)
    held = lax.all_gather(both, "seq", axis_index_groups=z_groups, axis=0, tiled=False)

    lists = jnp.concatenate([block_list, lax.ppermute(block_list, "seq", swap_core)], axis=0)
    lists = jnp.concatenate([lists, lax.ppermute(lists, "seq", swap_chip)], axis=0)
    tiles = jnp.stack([queries, lax.ppermute(queries, "seq", swap_core)])
    tiles = jnp.concatenate([tiles, lax.ppermute(tiles, "seq", swap_chip)], axis=0)

    lists = jnp.concatenate([lists, jnp.broadcast_to(text_slots[None, :], (GROUP, text_slots.shape[0]))], axis=1)
    slots = jnp.arange(planes, dtype=jnp.int32) * GROUP + me % GROUP
    need = jnp.any(lists[:, None, :] == slots[None, :, None], axis=2).astype(jnp.int32)

    part_rows = width + 2 * PART_ROWS
    part = jax.ShapeDtypeStruct((1, part_rows, TILE), jnp.bfloat16)
    parts = pl.pallas_call(
        functools.partial(attend_kernel, LOG2E / math.sqrt(HD)),
        out_shape=jax.ShapeDtypeStruct((GROUP, part_rows, TILE), jnp.bfloat16),
        in_specs=[pl.BlockSpec(memory_space=pltpu.SMEM)] + vmem_specs(2),
        out_specs=pl.BlockSpec(memory_space=pltpu.VMEM),
        scratch_shapes=[
            pltpu.VMEM((GROUP * heads, HD, TILE), jnp.float32),
            pltpu.VMEM((GROUP * heads, 1, TILE), jnp.float32),
            pltpu.VMEM((GROUP * heads, 1, TILE), jnp.float32),
        ],
        compiler_params=pltpu.CompilerParams(vmem_limit_bytes=32 * 1024 * 1024),
        name="attend",
    )(need, tiles, held)

    other = lax.ppermute(jnp.stack([parts[1], parts[3]]), "seq", swap_core)
    keep, send = pl.pallas_call(
        merge_kernel,
        out_shape=(part, part),
        in_specs=vmem_specs(2),
        out_specs=tuple(vmem_specs(2)),
        compiler_params=pltpu.CompilerParams(vmem_limit_bytes=32 * 1024 * 1024),
        name="merge",
    )(parts, other)
    other = lax.ppermute(send, "seq", swap_chip)
    shares = pl.pallas_call(
        project_kernel,
        out_shape=jax.ShapeDtypeStruct((head_size, TILE, width), jnp.bfloat16),
        in_specs=vmem_specs(3),
        out_specs=pl.BlockSpec(memory_space=pltpu.VMEM),
        scratch_shapes=[pltpu.VMEM((width, TILE), jnp.bfloat16)],
        compiler_params=pltpu.CompilerParams(vmem_limit_bytes=32 * 1024 * 1024),
        name="project",
    )(keep, other, out_weight)
    shares = lax.all_to_all(shares, "head", 0, 0, tiled=False)
    return jnp.sum(shares.astype(jnp.float32), axis=0).astype(jnp.bfloat16)


def solution(mesh):
    return jax.shard_map(
        functools.partial(per_device, mesh.shape["seq"], mesh.shape["head"]),
        mesh=mesh,
        in_specs=(
            P("seq", "head"),
            P("seq", "head"),
            P("seq", "head"),
            P("seq", None),
            P(),
            P("head", None),
        ),
        out_specs=P("seq", "head"),
        check_vma=False,
    )
```

```python
import functools
import math

import jax
import jax.numpy as jnp
from jax import lax
from jax.experimental import pallas as pl
from jax.experimental.pallas import tpu as pltpu
from jax.sharding import PartitionSpec as P

HD = 128
TILE = 256
GROUP = 4
PART_ROWS = 16
LOWEST = -1e30
LOG2E = math.log2(math.e)


def pack_part(ref, index, outs, sums):
    heads = len(outs)
    for h in range(heads):
        ref[index, h * HD:(h + 1) * HD, :] = outs[h].astype(jnp.bfloat16)
    rows = jnp.concatenate(sums + [jnp.zeros((8 - heads, TILE), jnp.float32)], axis=0)
    high = rows.astype(jnp.bfloat16).astype(jnp.float32)
    middle = (rows - high).astype(jnp.bfloat16).astype(jnp.float32)
    low = rows - high - middle
    base = heads * HD
    ref[index, base:base + 16, :] = jnp.concatenate([high, middle], axis=0).astype(jnp.bfloat16)
    ref[index, base + 16:base + 32, :] = jnp.concatenate([low, jnp.zeros_like(low)], axis=0).astype(jnp.bfloat16)


def unpack_sums(ref, index, heads):
    base = heads * HD
    block = ref[index, base:base + 16, :].astype(jnp.float32)
    last = ref[index, base + 16:base + 32, :].astype(jnp.float32)
    return block[0:8] + block[8:16] + last[0:8]


def merged(mine_ref, mine_sum_ref, mine, other_ref, other, heads):
    others = unpack_sums(other_ref, other, heads)
    outs, sums = [], []
    for h in range(heads):
        rows = slice(h * HD, (h + 1) * HD)
        own_sum = mine_sum_ref[mine, h:h + 1, :]
        other_sum = others[h:h + 1]
        top = jnp.maximum(own_sum, other_sum)
        own_weight = jnp.exp2(own_sum - top)
        other_weight = jnp.exp2(other_sum - top)
        total = own_weight + other_weight
        outs.append(
            mine_ref[mine, rows, :] * (own_weight / total)
            + other_ref[other, rows, :].astype(jnp.float32) * (other_weight / total)
        )
        sums.append(top + jnp.log2(total))
    return outs, sums


def visit_shards(factor, need_ref, first, q_refs, shards, acc_ref, peak_ref, total_ref):
    heads = q_refs[0].shape[1] // HD
    for j, (k_ref, v_ref) in enumerate(shards):
        for t, q_ref in enumerate(q_refs):

            @pl.when(need_ref[t, first + j] > 0)
            def _():
                for h in range(heads):
                    cols = slice(h * HD, (h + 1) * HD)
                    scores = lax.dot_general(
                        k_ref[:, cols],
                        q_ref[0:TILE, cols],
                        (((1,), (1,)), ((), ())),
                        preferred_element_type=jnp.float32,
                    )
                    row = t * heads + h
                    old = peak_ref[row]
                    peak = jnp.maximum(old, jnp.max(scores, axis=0, keepdims=True) * factor)
                    weights = jnp.exp2(scores * factor - peak)
                    shrink = jnp.exp2(old - peak)
                    peak_ref[row] = peak
                    total_ref[row] = total_ref[row] * shrink + jnp.sum(weights, axis=0, keepdims=True)
                    acc_ref[row] = acc_ref[row] * shrink + lax.dot_general(
                        v_ref[:, cols],
                        weights.astype(jnp.bfloat16),
                        (((0,), (0,)), ((), ())),
                        preferred_element_type=jnp.float32,
                    )


def open_kernel(factor, count, need_ref, *refs):
    q_refs, kv_refs, (acc_ref, peak_ref, total_ref) = refs[:GROUP], refs[GROUP:-3], refs[-3:]
    acc_ref[...] = jnp.zeros_like(acc_ref)
    peak_ref[...] = jnp.full_like(peak_ref, LOWEST)
    total_ref[...] = jnp.zeros_like(total_ref)
    shards = list(zip(kv_refs[:count], kv_refs[count:]))
    visit_shards(factor, need_ref, 0, q_refs, shards, acc_ref, peak_ref, total_ref)


def more_kernel(factor, first, count, need_ref, *refs):
    q_refs, kv_refs = refs[:GROUP], refs[GROUP:GROUP + 2 * count]
    held, state = refs[GROUP + 2 * count:-3], refs[-3:]
    for source, target in zip(held, state):
        target[...] = source[...]
    shards = list(zip(kv_refs[:count], kv_refs[count:]))
    visit_shards(factor, need_ref, first, q_refs, shards, *state)


def close_kernel(factor, first, need_ref, *refs):
    q_refs, kv_refs = refs[:GROUP], refs[GROUP:GROUP + 2]
    held = refs[GROUP + 2:GROUP + 5]
    keep_ref, keep_sum_ref, send_ref, acc_ref, peak_ref, total_ref = refs[GROUP + 5:]
    heads = q_refs[0].shape[1] // HD
    for source, target in zip(held, (acc_ref, peak_ref, total_ref)):
        target[...] = source[...]
    visit_shards(factor, need_ref, first, q_refs, [kv_refs], acc_ref, peak_ref, total_ref)
    for t in range(GROUP):
        outs, sums = [], []
        for h in range(heads):
            row = t * heads + h
            total = total_ref[row]
            present = total > 0.0
            safe = jnp.where(present, total, 1.0)
            outs.append(acc_ref[row] * (1.0 / safe))
            sums.append(jnp.where(present, peak_ref[row] + jnp.log2(safe), LOWEST))
        if t % 2:
            pack_part(send_ref, t // 2, outs, sums)
        else:
            for h in range(heads):
                keep_ref[t // 2, h * HD:(h + 1) * HD, :] = outs[h]
                keep_sum_ref[t // 2, h:h + 1, :] = sums[h]


def merge_kernel(mine_ref, mine_sum_ref, other_ref, keep_ref, keep_sum_ref, send_ref):
    heads = mine_ref.shape[1] // HD
    outs, sums = merged(mine_ref, mine_sum_ref, 1, other_ref, 1, heads)
    pack_part(send_ref, 0, outs, sums)
    outs, sums = merged(mine_ref, mine_sum_ref, 0, other_ref, 0, heads)
    for h in range(heads):
        keep_ref[0, h * HD:(h + 1) * HD, :] = outs[h]
        keep_sum_ref[0, h:h + 1, :] = sums[h]


def project_kernel(mine_ref, mine_sum_ref, other_ref, weight_ref, out_ref, held_ref):
    heads = mine_ref.shape[1] // HD
    outs, _ = merged(mine_ref, mine_sum_ref, 0, other_ref, 0, heads)
    for h in range(heads):
        held_ref[:, h * HD:(h + 1) * HD] = outs[h].T.astype(jnp.bfloat16)
    shares, _, width = out_ref.shape
    attended = held_ref[...]
    for j in range(shares):
        out_ref[j] = jnp.dot(
            attended, weight_ref[:, j * width:(j + 1) * width], preferred_element_type=jnp.float32
        ).astype(jnp.bfloat16)


def vmem_specs(count):
    return [pl.BlockSpec(memory_space=pltpu.VMEM)] * count


def attend_cost(blocks):
    return pl.CostEstimate(
        flops=blocks * 4 * TILE * TILE * HD, bytes_accessed=4 << 20, transcendentals=blocks * TILE * TILE
    )


PARAMS = pltpu.CompilerParams(vmem_limit_bytes=32 * 1024 * 1024)


def per_device(seq_size, head_size, queries, key_states, value_states, block_list, text_slots, out_weight):
    width = queries.shape[1]
    heads = width // HD
    planes = seq_size // GROUP
    me = lax.axis_index("seq")
    up = [(s, (s + GROUP) % seq_size) for s in range(seq_size)]
    down = [(s, (s - GROUP) % seq_size) for s in range(seq_size)]

    k_up, k_down, v_up, v_down = [key_states], [key_states], [value_states], [value_states]
    half = planes // 2
    for step in range(half):
        k_up.append(lax.ppermute(k_up[-1], "seq", up))
        if step < half - 1:
            k_down.append(lax.ppermute(k_down[-1], "seq", down))
            v_up.append(lax.ppermute(v_up[-1], "seq", up))
        v_down.append(lax.ppermute(v_down[-1], "seq", down))
        if step == 0:
            listed = jnp.pad(
                block_list.astype(jnp.bfloat16), ((0, PART_ROWS - 1), (0, width - block_list.shape[1]))
            )
            packed = jnp.concatenate([queries, listed], axis=0)
            tiles = [packed] + [
                lax.ppermute(packed, "seq", [(s, s ^ k) for s in range(seq_size)]) for k in range(1, GROUP)
            ]
            lists = jnp.concatenate([t[TILE:TILE + 1, :block_list.shape[1]] for t in tiles], axis=0)
            lists = jnp.concatenate(
                [lists.astype(jnp.int32), jnp.broadcast_to(text_slots[None, :], (GROUP, text_slots.shape[0]))],
                axis=1,
            )
            order = [0] + [sign * i for i in range(1, half) for sign in (-1, 1)] + [half]
            slots = (me + GROUP * jnp.asarray(order, jnp.int32)) % seq_size
            need = jnp.any(lists[:, None, :] == slots[None, :, None], axis=2).astype(jnp.int32)

    rows = GROUP * heads
    state = (
        jax.ShapeDtypeStruct((rows, HD, TILE), jnp.float32),
        jax.ShapeDtypeStruct((rows, 1, TILE), jnp.float32),
        jax.ShapeDtypeStruct((rows, 1, TILE), jnp.float32),
    )
    factor = LOG2E / math.sqrt(HD)
    smem = [pl.BlockSpec(memory_space=pltpu.SMEM)]

    def shards(pairs):
        return [k for k, _ in pairs] + [v for _, v in pairs]

    first = [(key_states, value_states), (k_up[1], v_up[1]), (k_down[1], v_down[1])]
    held = pl.pallas_call(
        functools.partial(open_kernel, factor, 3),
        out_shape=state,
        in_specs=smem + vmem_specs(GROUP + 6),
        out_specs=tuple(vmem_specs(3)),
        compiler_params=PARAMS,
        cost_estimate=attend_cost(27),
        name="attend_near",
    )(need, *tiles, *shards(first))
    second = [pair for i in range(2, half) for pair in ((k_up[i], v_up[i]), (k_down[i], v_down[i]))]
    held = pl.pallas_call(
        functools.partial(more_kernel, factor, 3, len(second)),
        out_shape=state,
        in_specs=smem + vmem_specs(GROUP + 2 * len(second) + 3),
        out_specs=tuple(vmem_specs(3)),
        compiler_params=PARAMS,
        cost_estimate=attend_cost(18),
        name="attend_far",
    )(need, *tiles, *shards(second), *held)
    keep, keep_sum, send = pl.pallas_call(
        functools.partial(close_kernel, factor, planes - 1),
        out_shape=(
            jax.ShapeDtypeStruct((2, width, TILE), jnp.float32),
            jax.ShapeDtypeStruct((2, 8, TILE), jnp.float32),
            jax.ShapeDtypeStruct((2, width + 2 * PART_ROWS, TILE), jnp.bfloat16),
        ),
        in_specs=smem + vmem_specs(GROUP + 5),
        out_specs=tuple(vmem_specs(3)),
        scratch_shapes=[pltpu.VMEM(s.shape, s.dtype) for s in state],
        compiler_params=PARAMS,
        cost_estimate=attend_cost(9),
        name="attend_last",
    )(need, *tiles, k_up[half], v_down[half], *held)

    other = lax.ppermute(send, "seq", [(s, s ^ 1) for s in range(seq_size)])
    keep, keep_sum, send = pl.pallas_call(
        merge_kernel,
        out_shape=(
            jax.ShapeDtypeStruct((1, width, TILE), jnp.float32),
            jax.ShapeDtypeStruct((1, 8, TILE), jnp.float32),
            jax.ShapeDtypeStruct((1, width + 2 * PART_ROWS, TILE), jnp.bfloat16),
        ),
        in_specs=vmem_specs(3),
        out_specs=tuple(vmem_specs(3)),
        compiler_params=PARAMS,
        name="merge",
    )(keep, keep_sum, other)
    other = lax.ppermute(send, "seq", [(s, s ^ 2) for s in range(seq_size)])
    shares = pl.pallas_call(
        project_kernel,
        out_shape=jax.ShapeDtypeStruct((head_size, TILE, width), jnp.bfloat16),
        in_specs=vmem_specs(4),
        out_specs=pl.BlockSpec(memory_space=pltpu.VMEM),
        scratch_shapes=[pltpu.VMEM((TILE, width), jnp.bfloat16)],
        compiler_params=PARAMS,
        name="project",
    )(keep, keep_sum, other, out_weight)
    shares = lax.all_to_all(shares, "head", 0, 0, tiled=False)
    return jnp.sum(shares.astype(jnp.float32), axis=0).astype(jnp.bfloat16)


def solution(mesh):
    return jax.shard_map(
        functools.partial(per_device, mesh.shape["seq"], mesh.shape["head"]),
        mesh=mesh,
        in_specs=(
            P("seq", "head"),
            P("seq", "head"),
            P("seq", "head"),
            P("seq", None),
            P(),
            P("head", None),
        ),
        out_specs=P("seq", "head"),
        check_vma=False,
    )
```

```python
import functools
import math

import jax
import jax.numpy as jnp
from jax import lax
from jax.experimental import pallas as pl
from jax.experimental.pallas import tpu as pltpu
from jax.sharding import PartitionSpec as P

HD = 128
TILE = 256
GROUP = 4
PART_ROWS = 16
LOWEST = -1e30
LOG2E = math.log2(math.e)


def pack_part(ref, index, outs, sums):
    heads = len(outs)
    for h in range(heads):
        ref[index, h * HD:(h + 1) * HD, :] = outs[h].astype(jnp.bfloat16)
    rows = jnp.concatenate(sums + [jnp.zeros((8 - heads, TILE), jnp.float32)], axis=0)
    high = rows.astype(jnp.bfloat16).astype(jnp.float32)
    middle = (rows - high).astype(jnp.bfloat16).astype(jnp.float32)
    low = rows - high - middle
    base = heads * HD
    ref[index, base:base + 16, :] = jnp.concatenate([high, middle], axis=0).astype(jnp.bfloat16)
    ref[index, base + 16:base + 32, :] = jnp.concatenate([low, jnp.zeros_like(low)], axis=0).astype(jnp.bfloat16)


def unpack_sums(ref, index, heads):
    base = heads * HD
    block = ref[index, base:base + 16, :].astype(jnp.float32)
    last = ref[index, base + 16:base + 32, :].astype(jnp.float32)
    return block[0:8] + block[8:16] + last[0:8]


def merged(mine_ref, mine_sum_ref, mine, other_ref, other, heads):
    others = unpack_sums(other_ref, other, heads)
    outs, sums = [], []
    for h in range(heads):
        rows = slice(h * HD, (h + 1) * HD)
        own_sum = mine_sum_ref[mine, h:h + 1, :]
        other_sum = others[h:h + 1]
        top = jnp.maximum(own_sum, other_sum)
        own_weight = jnp.exp2(own_sum - top)
        other_weight = jnp.exp2(other_sum - top)
        total = own_weight + other_weight
        outs.append(
            mine_ref[mine, rows, :] * (own_weight / total)
            + other_ref[other, rows, :].astype(jnp.float32) * (other_weight / total)
        )
        sums.append(top + jnp.log2(total))
    return outs, sums


def transpose_values(v_refs, vt_ref, first):
    for j, v_ref in enumerate(v_refs):
        for h in range(v_ref.shape[1] // HD):
            vt_ref[first + j, h] = v_ref[:, h * HD:(h + 1) * HD].T


def visit_group(factor, need_ref, first, q_ref, k_refs, vt_ref, vt_first, state):
    acc_ref, peak_ref, total_ref = state
    heads = q_ref.shape[2] // HD

    def visit(t, carry):
        wanted = [need_ref[t, first + j] for j in range(len(k_refs))]

        @pl.when(sum(wanted[1:], wanted[0]) > 0)
        def _():
            shift = [jnp.where(w > 0, 0.0, LOWEST) for w in wanted]

            def scores_of(h):
                cols = slice(h * HD, (h + 1) * HD)
                return [
                    lax.dot_general(
                        k_ref[:, cols],
                        q_ref[t, :, cols],
                        (((1,), (1,)), ((), ())),
                        preferred_element_type=jnp.float32,
                    )
                    for k_ref in k_refs
                ]

            following = scores_of(0)
            for h in range(heads):
                scores = following
                if h + 1 < heads:
                    following = scores_of(h + 1)
                row = t * heads + h
                old = peak_ref[row]
                peak = old
                for part, low in zip(scores, shift):
                    peak = jnp.maximum(peak, jnp.max(part, axis=0, keepdims=True) * factor + low)
                weights = [jnp.exp2(part * factor - (peak - low)) for part, low in zip(scores, shift)]
                shrink = jnp.exp2(old - peak)
                sums = [jnp.sum(w, axis=0, keepdims=True) for w in weights]
                dots = [
                    jnp.dot(vt_ref[vt_first + j, h], w.astype(jnp.bfloat16), preferred_element_type=jnp.float32)
                    for j, w in enumerate(weights)
                ]
                peak_ref[row] = peak
                total_ref[row] = total_ref[row] * shrink + sum(sums[1:], sums[0])
                acc_ref[row] = acc_ref[row] * shrink + sum(dots[1:], dots[0])

        return carry

    lax.fori_loop(0, q_ref.shape[0], visit, 0)


def near_kernel(factor, count, need_ref, *refs):
    q_refs, k_refs, v_refs = refs[:GROUP], refs[GROUP:GROUP + count], refs[GROUP + count:GROUP + 2 * count]
    stacked_ref, acc_ref, peak_ref, total_ref, vt_ref = refs[GROUP + 2 * count:]
    acc_ref[...] = jnp.zeros_like(acc_ref)
    peak_ref[...] = jnp.full_like(peak_ref, LOWEST)
    total_ref[...] = jnp.zeros_like(total_ref)
    for t, q_ref in enumerate(q_refs):
        stacked_ref[t] = q_ref[0:TILE, :]
    transpose_values(v_refs, vt_ref, 0)
    visit_group(factor, need_ref, 0, stacked_ref, k_refs, vt_ref, 0, (acc_ref, peak_ref, total_ref))


def far_kernel(factor, groups, need_ref, stacked_ref, *refs):
    count = sum(groups)
    k_refs, v_refs = refs[:count], refs[count:2 * count]
    held = refs[2 * count:2 * count + 3]
    keep_ref, keep_sum_ref, send_ref, acc_ref, peak_ref, total_ref, vt_ref = refs[2 * count + 3:]
    heads = stacked_ref.shape[2] // HD
    for source, target in zip(held, (acc_ref, peak_ref, total_ref)):
        target[...] = source[...]
    transpose_values(v_refs, vt_ref, 0)
    begin = 0
    for size in groups:
        visit_group(
            factor,
            need_ref,
            GROUP - 1 + begin,
            stacked_ref,
            k_refs[begin:begin + size],
            vt_ref,
            begin,
            (acc_ref, peak_ref, total_ref),
        )
        begin += size
    for t in range(GROUP):
        outs, sums = [], []
        for h in range(heads):
            row = t * heads + h
            total = total_ref[row]
            present = total > 0.0
            safe = jnp.where(present, total, 1.0)
            outs.append(acc_ref[row] * (1.0 / safe))
            sums.append(jnp.where(present, peak_ref[row] + jnp.log2(safe), LOWEST))
        if t % 2:
            pack_part(send_ref, t // 2, outs, sums)
        else:
            for h in range(heads):
                keep_ref[t // 2, h * HD:(h + 1) * HD, :] = outs[h]
                keep_sum_ref[t // 2, h:h + 1, :] = sums[h]


def merge_kernel(mine_ref, mine_sum_ref, other_ref, keep_ref, keep_sum_ref, send_ref):
    heads = mine_ref.shape[1] // HD
    outs, sums = merged(mine_ref, mine_sum_ref, 1, other_ref, 1, heads)
    pack_part(send_ref, 0, outs, sums)
    outs, sums = merged(mine_ref, mine_sum_ref, 0, other_ref, 0, heads)
    for h in range(heads):
        keep_ref[0, h * HD:(h + 1) * HD, :] = outs[h]
        keep_sum_ref[0, h:h + 1, :] = sums[h]


def project_kernel(mine_ref, mine_sum_ref, other_ref, weight_ref, out_ref, held_ref):
    heads = mine_ref.shape[1] // HD
    outs, _ = merged(mine_ref, mine_sum_ref, 0, other_ref, 0, heads)
    for h in range(heads):
        held_ref[:, h * HD:(h + 1) * HD] = outs[h].T.astype(jnp.bfloat16)
    shares, _, width = out_ref.shape
    attended = held_ref[...]
    for j in range(shares):
        out_ref[j] = jnp.dot(
            attended, weight_ref[:, j * width:(j + 1) * width], preferred_element_type=jnp.float32
        ).astype(jnp.bfloat16)


def vmem_specs(count):
    return [pl.BlockSpec(memory_space=pltpu.VMEM)] * count


def attend_cost(blocks):
    return pl.CostEstimate(
        flops=blocks * 4 * TILE * TILE * HD, bytes_accessed=4 << 20, transcendentals=blocks * TILE * TILE
    )


PARAMS = pltpu.CompilerParams(vmem_limit_bytes=32 * 1024 * 1024)


def per_device(seq_size, head_size, queries, key_states, value_states, block_list, text_slots, out_weight):
    width = queries.shape[1]
    heads = width // HD
    planes = seq_size // GROUP
    me = lax.axis_index("seq")
    up = [(s, (s + GROUP) % seq_size) for s in range(seq_size)]
    down = [(s, (s - GROUP) % seq_size) for s in range(seq_size)]

    k_up, k_down, v_up, v_down = [key_states], [key_states], [value_states], [value_states]
    half = planes // 2
    for step in range(half):
        k_up.append(lax.ppermute(k_up[-1], "seq", up))
        if step < half - 1:
            k_down.append(lax.ppermute(k_down[-1], "seq", down))
            v_up.append(lax.ppermute(v_up[-1], "seq", up))
        v_down.append(lax.ppermute(v_down[-1], "seq", down))
        if step == 0:
            listed = jnp.pad(
                block_list.astype(jnp.bfloat16), ((0, PART_ROWS - 1), (0, width - block_list.shape[1]))
            )
            packed = jnp.concatenate([queries, listed], axis=0)
            tiles = [packed] + [
                lax.ppermute(packed, "seq", [(s, s ^ k) for s in range(seq_size)]) for k in range(1, GROUP)
            ]
            lists = jnp.concatenate([t[TILE:TILE + 1, :block_list.shape[1]] for t in tiles], axis=0)
            lists = jnp.concatenate(
                [lists.astype(jnp.int32), jnp.broadcast_to(text_slots[None, :], (GROUP, text_slots.shape[0]))],
                axis=1,
            )
            order = [0, -1, 1, -3, 3, 4, -2, 2]
            slots = (me + GROUP * jnp.asarray(order, jnp.int32)) % seq_size
            need = jnp.any(lists[:, None, :] == slots[None, :, None], axis=2).astype(jnp.int32)

    rows = GROUP * heads
    state = (
        jax.ShapeDtypeStruct((rows, HD, TILE), jnp.float32),
        jax.ShapeDtypeStruct((rows, 1, TILE), jnp.float32),
        jax.ShapeDtypeStruct((rows, 1, TILE), jnp.float32),
    )
    factor = LOG2E / math.sqrt(HD)
    smem = [pl.BlockSpec(memory_space=pltpu.SMEM)]

    def shards(pairs):
        return [k for k, _ in pairs] + [v for _, v in pairs]

    def vt_scratch(count):
        return pltpu.VMEM((count, heads, HD, TILE), jnp.bfloat16)

    near = [(key_states, value_states), (k_up[1], v_up[1]), (k_down[1], v_down[1])]
    stacked = jax.ShapeDtypeStruct((GROUP, TILE, width), jnp.bfloat16)
    stacked, *held = pl.pallas_call(
        functools.partial(near_kernel, factor, len(near)),
        out_shape=(stacked,) + state,
        in_specs=smem + vmem_specs(GROUP + 2 * len(near)),
        out_specs=tuple(vmem_specs(4)),
        scratch_shapes=[vt_scratch(len(near))],
        compiler_params=PARAMS,
        cost_estimate=attend_cost(27),
        name="attend_near",
    )(need, *tiles, *shards(near))
    far = [(k_up[3], v_up[3]), (k_down[3], v_down[3]), (k_up[4], v_down[4]), (k_up[2], v_up[2]), (k_down[2], v_down[2])]
    keep, keep_sum, send = pl.pallas_call(
        functools.partial(far_kernel, factor, (3, 2)),
        out_shape=(
            jax.ShapeDtypeStruct((2, width, TILE), jnp.float32),
            jax.ShapeDtypeStruct((2, 8, TILE), jnp.float32),
            jax.ShapeDtypeStruct((2, width + 2 * PART_ROWS, TILE), jnp.bfloat16),
        ),
        in_specs=smem + vmem_specs(1 + 2 * len(far) + 3),
        out_specs=tuple(vmem_specs(3)),
        scratch_shapes=[pltpu.VMEM(s.shape, s.dtype) for s in state] + [vt_scratch(len(far))],
        compiler_params=PARAMS,
        cost_estimate=attend_cost(27),
        name="attend_far",
    )(need, stacked, *shards(far), *held)

    other = lax.ppermute(send, "seq", [(s, s ^ 1) for s in range(seq_size)])
    keep, keep_sum, send = pl.pallas_call(
        merge_kernel,
        out_shape=(
            jax.ShapeDtypeStruct((1, width, TILE), jnp.float32),
            jax.ShapeDtypeStruct((1, 8, TILE), jnp.float32),
            jax.ShapeDtypeStruct((1, width + 2 * PART_ROWS, TILE), jnp.bfloat16),
        ),
        in_specs=vmem_specs(3),
        out_specs=tuple(vmem_specs(3)),
        compiler_params=PARAMS,
        name="merge",
    )(keep, keep_sum, other)
    other = lax.ppermute(send, "seq", [(s, s ^ 2) for s in range(seq_size)])
    shares = pl.pallas_call(
        project_kernel,
        out_shape=jax.ShapeDtypeStruct((head_size, TILE, width), jnp.bfloat16),
        in_specs=vmem_specs(4),
        out_specs=pl.BlockSpec(memory_space=pltpu.VMEM),
        scratch_shapes=[pltpu.VMEM((TILE, width), jnp.bfloat16)],
        compiler_params=PARAMS,
        name="project",
    )(keep, keep_sum, other, out_weight)
    shares = lax.all_to_all(shares, "head", 0, 0, tiled=False)
    return jnp.sum(shares.astype(jnp.float32), axis=0).astype(jnp.bfloat16)


def solution(mesh):
    return jax.shard_map(
        functools.partial(per_device, mesh.shape["seq"], mesh.shape["head"]),
        mesh=mesh,
        in_specs=(
            P("seq", "head"),
            P("seq", "head"),
            P("seq", "head"),
            P("seq", None),
            P(),
            P("head", None),
        ),
        out_specs=P("seq", "head"),
        check_vma=False,
    )
```

```python
import functools
import math

import jax
import jax.numpy as jnp
from jax import lax
from jax.experimental import pallas as pl
from jax.experimental.pallas import tpu as pltpu
from jax.sharding import PartitionSpec as P

HD = 128
TILE = 256
GROUP = 4
PART_ROWS = 16
LOWEST = -1e30
LOG2E = math.log2(math.e)


def pack_part(ref, index, outs, sums):
    heads = len(outs)
    for h in range(heads):
        ref[index, h * HD:(h + 1) * HD, :] = outs[h].astype(jnp.bfloat16)
    rows = jnp.concatenate(sums + [jnp.zeros((8 - heads, TILE), jnp.float32)], axis=0)
    high = rows.astype(jnp.bfloat16).astype(jnp.float32)
    middle = (rows - high).astype(jnp.bfloat16).astype(jnp.float32)
    low = rows - high - middle
    base = heads * HD
    ref[index, base:base + 16, :] = jnp.concatenate([high, middle], axis=0).astype(jnp.bfloat16)
    ref[index, base + 16:base + 32, :] = jnp.concatenate([low, jnp.zeros_like(low)], axis=0).astype(jnp.bfloat16)


def unpack_sums(ref, index, heads):
    base = heads * HD
    block = ref[index, base:base + 16, :].astype(jnp.float32)
    last = ref[index, base + 16:base + 32, :].astype(jnp.float32)
    return block[0:8] + block[8:16] + last[0:8]


def merged(mine_ref, mine_sum_ref, mine, other_ref, other, heads):
    others = unpack_sums(other_ref, other, heads)
    outs, sums = [], []
    for h in range(heads):
        rows = slice(h * HD, (h + 1) * HD)
        own_sum = mine_sum_ref[mine, h:h + 1, :]
        other_sum = others[h:h + 1]
        top = jnp.maximum(own_sum, other_sum)
        own_weight = jnp.exp2(own_sum - top)
        other_weight = jnp.exp2(other_sum - top)
        total = own_weight + other_weight
        outs.append(
            mine_ref[mine, rows, :] * (own_weight / total)
            + other_ref[other, rows, :].astype(jnp.float32) * (other_weight / total)
        )
        sums.append(top + jnp.log2(total))
    return outs, sums


def load_shards(need_ref, first, shards, k_ref, vt_ref):
    for j, (key, value) in enumerate(shards):
        wanted = need_ref[0, first + j]
        for t in range(1, need_ref.shape[0]):
            wanted = wanted + need_ref[t, first + j]

        @pl.when(wanted > 0)
        def _():
            k_ref[j] = key[...]
            for h in range(vt_ref.shape[1]):
                vt_ref[j, h] = value[:, h * HD:(h + 1) * HD].T


def visit_shards(factor, need_ref, first, count, q_ref, k_ref, vt_ref, state):
    acc_ref, peak_ref, total_ref = state
    heads = vt_ref.shape[1]

    def take(t, picks):
        def scores_of(h):
            cols = slice(h * HD, (h + 1) * HD)
            return [
                lax.dot_general(
                    k_ref[j, :, cols],
                    q_ref[t, :, cols],
                    (((1,), (1,)), ((), ())),
                    preferred_element_type=jnp.float32,
                )
                for j in picks
            ]

        following = scores_of(0)
        for h in range(heads):
            scores = following
            if h + 1 < heads:
                following = scores_of(h + 1)
            row = t * heads + h
            old = peak_ref[row]
            tops = [jnp.max(part, axis=0, keepdims=True) for part in scores]
            peak = jnp.maximum(old, functools.reduce(jnp.maximum, tops) * factor)
            weights = [jnp.exp2(part * factor - peak) for part in scores]
            shrink = jnp.exp2(old - peak)
            sums = [jnp.sum(w, axis=0, keepdims=True) for w in weights]
            dots = [
                jnp.dot(vt_ref[j, h], w.astype(jnp.bfloat16), preferred_element_type=jnp.float32)
                for j, w in zip(picks, weights)
            ]
            peak_ref[row] = peak
            total_ref[row] = total_ref[row] * shrink + sum(sums[1:], sums[0])
            acc_ref[row] = acc_ref[row] * shrink + sum(dots[1:], dots[0])

    def visit(t, carry):
        picks = [jnp.int32(0)] * count
        seen = jnp.int32(0)
        for j in range(count):
            wanted = need_ref[t, first + j]
            for i in range(j + 1):
                picks[i] = jnp.where((wanted > 0) & (seen == i), j, picks[i])
            seen = seen + wanted

        if count >= 3:

            @pl.when(seen >= 3)
            def _():
                take(t, picks[:3])

        if count >= 2:

            @pl.when(seen == 2)
            def _():
                take(t, picks[:2])

        @pl.when((seen == 1) | (seen == 4))
        def _():
            take(t, [jnp.where(seen == 4, picks[-1], picks[0])])

        return carry

    lax.fori_loop(0, q_ref.shape[0], visit, 0)


def near_kernel(factor, need_ref, *refs):
    q_refs, (own_ref, k_low, k_high, v_low, v_high) = refs[:GROUP], refs[GROUP:GROUP + 5]
    stacked_ref, acc_ref, peak_ref, total_ref, k_ref, vt_ref = refs[GROUP + 5:]
    acc_ref[...] = jnp.zeros_like(acc_ref)
    peak_ref[...] = jnp.full_like(peak_ref, LOWEST)
    total_ref[...] = jnp.zeros_like(total_ref)
    for t, q_ref in enumerate(q_refs):
        stacked_ref[t] = q_ref[0:TILE, :]
    shards = [(own_ref.at[0:TILE], own_ref.at[TILE:2 * TILE]), (k_low, v_low), (k_high, v_high)]
    load_shards(need_ref, 0, shards, k_ref, vt_ref)
    visit_shards(factor, need_ref, 0, 3, stacked_ref, k_ref, vt_ref, (acc_ref, peak_ref, total_ref))


def far_kernel(factor, first, count, need_ref, stacked_ref, *refs):
    shards = list(zip(refs[:count], refs[count:2 * count]))
    held, state = refs[2 * count:2 * count + 3], refs[2 * count + 3:2 * count + 6]
    k_ref, vt_ref = refs[2 * count + 6:]
    for source, target in zip(held, state):
        target[...] = source[...]
    load_shards(need_ref, first, shards, k_ref, vt_ref)
    visit_shards(factor, need_ref, first, count, stacked_ref, k_ref, vt_ref, state)


def last_kernel(factor, first, need_ref, stacked_ref, *refs):
    shards = [refs[:2]]
    keep_ref, keep_sum_ref, send_ref, *state, k_ref, vt_ref = refs[5:]
    heads = vt_ref.shape[1]
    for source, target in zip(refs[2:5], state):
        target[...] = source[...]
    load_shards(need_ref, first, shards, k_ref, vt_ref)
    visit_shards(factor, need_ref, first, 1, stacked_ref, k_ref, vt_ref, state)
    acc_ref, peak_ref, total_ref = state
    for t in range(GROUP):
        outs, sums = [], []
        for h in range(heads):
            row = t * heads + h
            total = total_ref[row]
            present = total > 0.0
            safe = jnp.where(present, total, 1.0)
            outs.append(acc_ref[row] * (1.0 / safe))
            sums.append(jnp.where(present, peak_ref[row] + jnp.log2(safe), LOWEST))
        if t % 2:
            pack_part(send_ref, t // 2, outs, sums)
        else:
            for h in range(heads):
                keep_ref[t // 2, h * HD:(h + 1) * HD, :] = outs[h]
                keep_sum_ref[t // 2, h:h + 1, :] = sums[h]


def relay_kernel(k_ref, v_ref, after_ref, k_out_ref, v_out_ref):
    k_out_ref[...] = k_ref[...]
    v_out_ref[...] = v_ref[...]


def merge_kernel(mine_ref, mine_sum_ref, other_ref, keep_ref, keep_sum_ref, send_ref):
    heads = mine_ref.shape[1] // HD
    outs, sums = merged(mine_ref, mine_sum_ref, 1, other_ref, 1, heads)
    pack_part(send_ref, 0, outs, sums)
    outs, sums = merged(mine_ref, mine_sum_ref, 0, other_ref, 0, heads)
    for h in range(heads):
        keep_ref[0, h * HD:(h + 1) * HD, :] = outs[h]
        keep_sum_ref[0, h:h + 1, :] = sums[h]


def project_kernel(mine_ref, mine_sum_ref, other_ref, weight_ref, out_ref, held_ref):
    heads = mine_ref.shape[1] // HD
    outs, _ = merged(mine_ref, mine_sum_ref, 0, other_ref, 0, heads)
    for h in range(heads):
        held_ref[:, h * HD:(h + 1) * HD] = outs[h].T.astype(jnp.bfloat16)
    shares, _, width = out_ref.shape
    attended = held_ref[...]
    for j in range(shares):
        out_ref[j] = jnp.dot(
            attended, weight_ref[:, j * width:(j + 1) * width], preferred_element_type=jnp.float32
        ).astype(jnp.bfloat16)


def vmem_specs(count):
    return [pl.BlockSpec(memory_space=pltpu.VMEM)] * count


def attend_cost(blocks):
    return pl.CostEstimate(
        flops=blocks * 4 * TILE * TILE * HD, bytes_accessed=4 << 20, transcendentals=blocks * TILE * TILE
    )


PARAMS = pltpu.CompilerParams(vmem_limit_bytes=32 * 1024 * 1024)


def per_device(seq_size, head_size, queries, key_states, value_states, block_list, text_slots, out_weight):
    width = queries.shape[1]
    heads = width // HD
    planes = seq_size // GROUP
    me = lax.axis_index("seq")
    up = [(s, (s + GROUP) % seq_size) for s in range(seq_size)]
    down = [(s, (s - GROUP) % seq_size) for s in range(seq_size)]

    k_up, k_down, v_up, v_down = [key_states], [key_states], [value_states], [value_states]
    half = planes // 2
    for step in range(half - 1):
        k_up.append(lax.ppermute(k_up[-1], "seq", up))
        k_down.append(lax.ppermute(k_down[-1], "seq", down))
        v_up.append(lax.ppermute(v_up[-1], "seq", up))
        v_down.append(lax.ppermute(v_down[-1], "seq", down))

    listed = jnp.pad(block_list.astype(jnp.bfloat16), ((0, PART_ROWS - 1), (0, width - block_list.shape[1])))
    packed = jnp.concatenate([queries, listed], axis=0)
    tiles = [packed] + [
        lax.ppermute(packed, "seq", [(s, s ^ k) for s in range(seq_size)]) for k in range(1, GROUP)
    ]
    lists = jnp.concatenate([t[TILE:TILE + 1, :block_list.shape[1]] for t in tiles], axis=0)
    lists = jnp.concatenate(
        [lists.astype(jnp.int32), jnp.broadcast_to(text_slots[None, :], (GROUP, text_slots.shape[0]))], axis=1
    )
    order = [0, -1, 1, -3, 3, -2, 2, 4]
    slots = (me + GROUP * jnp.asarray(order, jnp.int32)) % seq_size
    need = jnp.any(lists[:, None, :] == slots[None, :, None], axis=2).astype(jnp.int32)

    rows = GROUP * heads
    state = (
        jax.ShapeDtypeStruct((rows, HD, TILE), jnp.float32),
        jax.ShapeDtypeStruct((rows, 1, TILE), jnp.float32),
        jax.ShapeDtypeStruct((rows, 1, TILE), jnp.float32),
    )
    factor = LOG2E / math.sqrt(HD)
    smem = [pl.BlockSpec(memory_space=pltpu.SMEM)]

    def scratch(count):
        return [
            pltpu.VMEM((count, TILE, width), jnp.bfloat16),
            pltpu.VMEM((count, heads, HD, TILE), jnp.bfloat16),
        ]

    own = jnp.concatenate([key_states, value_states], axis=0)
    stacked, *held = pl.pallas_call(
        functools.partial(near_kernel, factor),
        out_shape=(jax.ShapeDtypeStruct((GROUP, TILE, width), jnp.bfloat16),) + state,
        in_specs=smem + vmem_specs(GROUP + 5),
        out_specs=tuple(vmem_specs(4)),
        scratch_shapes=scratch(3),
        compiler_params=PARAMS,
        cost_estimate=attend_cost(27),
        name="attend_near",
    )(need, *tiles, own, k_up[1], k_down[1], v_up[1], v_down[1])
    shard = jax.ShapeDtypeStruct(key_states.shape, key_states.dtype)
    k_last, v_last = pl.pallas_call(
        relay_kernel,
        out_shape=(shard, shard),
        in_specs=vmem_specs(3),
        out_specs=tuple(vmem_specs(2)),
        compiler_params=PARAMS,
        name="relay",
    )(k_up[-1], v_down[-1], held[2])
    k_last = lax.ppermute(k_last, "seq", up)
    v_last = lax.ppermute(v_last, "seq", down)
    held = pl.pallas_call(
        functools.partial(far_kernel, factor, 3, 4),
        out_shape=state,
        in_specs=smem + vmem_specs(12),
        out_specs=tuple(vmem_specs(3)),
        scratch_shapes=scratch(4),
        compiler_params=PARAMS,
        cost_estimate=attend_cost(24),
        name="attend_far",
    )(need, stacked, k_up[3], k_down[3], k_up[2], k_down[2], v_up[3], v_down[3], v_up[2], v_down[2], *held)
    keep, keep_sum, send = pl.pallas_call(
        functools.partial(last_kernel, factor, 7),
        out_shape=(
            jax.ShapeDtypeStruct((2, width, TILE), jnp.float32),
            jax.ShapeDtypeStruct((2, 8, TILE), jnp.float32),
            jax.ShapeDtypeStruct((2, width + 2 * PART_ROWS, TILE), jnp.bfloat16),
        ),
        in_specs=smem + vmem_specs(6),
        out_specs=tuple(vmem_specs(3)),
        scratch_shapes=[pltpu.VMEM(s.shape, s.dtype) for s in state] + scratch(1),
        compiler_params=PARAMS,
        cost_estimate=attend_cost(12),
        name="attend_last",
    )(need, stacked, k_last, v_last, *held)

    other = lax.ppermute(send, "seq", [(s, s ^ 1) for s in range(seq_size)])
    keep, keep_sum, send = pl.pallas_call(
        merge_kernel,
        out_shape=(
            jax.ShapeDtypeStruct((1, width, TILE), jnp.float32),
            jax.ShapeDtypeStruct((1, 8, TILE), jnp.float32),
            jax.ShapeDtypeStruct((1, width + 2 * PART_ROWS, TILE), jnp.bfloat16),
        ),
        in_specs=vmem_specs(3),
        out_specs=tuple(vmem_specs(3)),
        compiler_params=PARAMS,
        name="merge",
    )(keep, keep_sum, other)
    other = lax.ppermute(send, "seq", [(s, s ^ 2) for s in range(seq_size)])
    shares = pl.pallas_call(
        project_kernel,
        out_shape=jax.ShapeDtypeStruct((head_size, TILE, width), jnp.bfloat16),
        in_specs=vmem_specs(4),
        out_specs=pl.BlockSpec(memory_space=pltpu.VMEM),
        scratch_shapes=[pltpu.VMEM((TILE, width), jnp.bfloat16)],
        compiler_params=PARAMS,
        name="project",
    )(keep, keep_sum, other, out_weight)
    shares = lax.all_to_all(shares, "head", 0, 0, tiled=False)
    return jnp.sum(shares.astype(jnp.float32), axis=0).astype(jnp.bfloat16)


def solution(mesh):
    return jax.shard_map(
        functools.partial(per_device, mesh.shape["seq"], mesh.shape["head"]),
        mesh=mesh,
        in_specs=(
            P("seq", "head"),
            P("seq", "head"),
            P("seq", "head"),
            P("seq", None),
            P(),
            P("head", None),
        ),
        out_specs=P("seq", "head"),
        check_vma=False,
    )
```

```python
import functools
import math

import jax
import jax.numpy as jnp
from jax import lax
from jax.experimental import pallas as pl
from jax.experimental.pallas import tpu as pltpu
from jax.sharding import PartitionSpec as P

HD = 128
TILE = 256
GROUP = 4
PART_ROWS = 16
LOWEST = -1e30
LOG2E = math.log2(math.e)


def pack_part(ref, index, outs, sums):
    heads = len(outs)
    for h in range(heads):
        ref[index, h * HD:(h + 1) * HD, :] = outs[h].astype(jnp.bfloat16)
    rows = jnp.concatenate(sums + [jnp.zeros((8 - heads, TILE), jnp.float32)], axis=0)
    high = rows.astype(jnp.bfloat16).astype(jnp.float32)
    middle = (rows - high).astype(jnp.bfloat16).astype(jnp.float32)
    low = rows - high - middle
    base = heads * HD
    ref[index, base:base + 16, :] = jnp.concatenate([high, middle], axis=0).astype(jnp.bfloat16)
    ref[index, base + 16:base + 32, :] = jnp.concatenate([low, jnp.zeros_like(low)], axis=0).astype(jnp.bfloat16)


def unpack_sums(ref, index, heads):
    base = heads * HD
    block = ref[index, base:base + 16, :].astype(jnp.float32)
    last = ref[index, base + 16:base + 32, :].astype(jnp.float32)
    return block[0:8] + block[8:16] + last[0:8]


def merged(mine_ref, mine_sum_ref, mine, other_ref, other, heads):
    others = unpack_sums(other_ref, other, heads)
    outs, sums = [], []
    for h in range(heads):
        rows = slice(h * HD, (h + 1) * HD)
        own_sum = mine_sum_ref[mine, h:h + 1, :]
        other_sum = others[h:h + 1]
        top = jnp.maximum(own_sum, other_sum)
        own_weight = jnp.exp2(own_sum - top)
        other_weight = jnp.exp2(other_sum - top)
        total = own_weight + other_weight
        outs.append(
            mine_ref[mine, rows, :] * (own_weight / total)
            + other_ref[other, rows, :].astype(jnp.float32) * (other_weight / total)
        )
        sums.append(top + jnp.log2(total))
    return outs, sums


def halves(ref):
    return ref.at[0:TILE], ref.at[TILE:2 * TILE]


def load_shards(need_ref, first, shards, k_ref, vt_ref):
    for j, (key, value) in enumerate(shards):
        wanted = need_ref[0, first + j]
        for t in range(1, need_ref.shape[0]):
            wanted = wanted + need_ref[t, first + j]

        @pl.when(wanted > 0)
        def _():
            k_ref[j] = key[...]
            for h in range(vt_ref.shape[1]):
                vt_ref[j, h] = value[:, h * HD:(h + 1) * HD].T


def visit_shards(factor, need_ref, first, count, q_ref, k_ref, vt_ref, state):
    acc_ref, peak_ref, total_ref = state
    heads = vt_ref.shape[1]

    def take(t, picks):
        def scores_of(h):
            cols = slice(h * HD, (h + 1) * HD)
            return [
                lax.dot_general(
                    k_ref[j, :, cols],
                    q_ref[t, :, cols],
                    (((1,), (1,)), ((), ())),
                    preferred_element_type=jnp.float32,
                )
                for j in picks
            ]

        following = scores_of(0)
        for h in range(heads):
            scores = following
            if h + 1 < heads:
                following = scores_of(h + 1)
            row = t * heads + h
            old = peak_ref[row]
            tops = [jnp.max(part, axis=0, keepdims=True) for part in scores]
            peak = jnp.maximum(old, functools.reduce(jnp.maximum, tops) * factor)
            weights = [jnp.exp2(part * factor - peak) for part in scores]
            shrink = jnp.exp2(old - peak)
            sums = [jnp.sum(w, axis=0, keepdims=True) for w in weights]
            dots = [
                jnp.dot(vt_ref[j, h], w.astype(jnp.bfloat16), preferred_element_type=jnp.float32)
                for j, w in zip(picks, weights)
            ]
            peak_ref[row] = peak
            total_ref[row] = total_ref[row] * shrink + sum(sums[1:], sums[0])
            acc_ref[row] = acc_ref[row] * shrink + sum(dots[1:], dots[0])

    def visit(t, carry):
        picks = [jnp.int32(0)] * count
        seen = jnp.int32(0)
        for j in range(count):
            wanted = need_ref[t, first + j]
            for i in range(j + 1):
                picks[i] = jnp.where((wanted > 0) & (seen == i), j, picks[i])
            seen = seen + wanted

        if count >= 3:

            @pl.when(seen >= 3)
            def _():
                take(t, picks[:3])

        if count >= 2:

            @pl.when(seen == 2)
            def _():
                take(t, picks[:2])

        @pl.when((seen == 1) | (seen == 4))
        def _():
            take(t, [jnp.where(seen == 4, picks[-1], picks[0])])

        return carry

    lax.fori_loop(0, q_ref.shape[0], visit, 0)


def near_kernel(factor, need_ref, *refs):
    q_refs, kv_refs = refs[:GROUP], refs[GROUP:GROUP + 3]
    stacked_ref, acc_ref, peak_ref, total_ref, k_ref, vt_ref = refs[GROUP + 3:]
    acc_ref[...] = jnp.zeros_like(acc_ref)
    peak_ref[...] = jnp.full_like(peak_ref, LOWEST)
    total_ref[...] = jnp.zeros_like(total_ref)
    for t, q_ref in enumerate(q_refs):
        stacked_ref[t] = q_ref[0:TILE, :]
    load_shards(need_ref, 0, [halves(ref) for ref in kv_refs], k_ref, vt_ref)
    visit_shards(factor, need_ref, 0, 3, stacked_ref, k_ref, vt_ref, (acc_ref, peak_ref, total_ref))


def far_kernel(factor, first, count, need_ref, stacked_ref, *refs):
    shards = [halves(ref) for ref in refs[:count]]
    held, state = refs[count:count + 3], refs[count + 3:count + 6]
    k_ref, vt_ref = refs[count + 6:]
    for source, target in zip(held, state):
        target[...] = source[...]
    load_shards(need_ref, first, shards, k_ref, vt_ref)
    visit_shards(factor, need_ref, first, count, stacked_ref, k_ref, vt_ref, state)


def last_kernel(factor, first, need_ref, stacked_ref, *refs):
    shards = [refs[:2]]
    keep_ref, keep_sum_ref, send_ref, *state, k_ref, vt_ref = refs[5:]
    heads = vt_ref.shape[1]
    for source, target in zip(refs[2:5], state):
        target[...] = source[...]
    load_shards(need_ref, first, shards, k_ref, vt_ref)
    visit_shards(factor, need_ref, first, 1, stacked_ref, k_ref, vt_ref, state)
    acc_ref, peak_ref, total_ref = state
    for t in range(GROUP):
        outs, sums = [], []
        for h in range(heads):
            row = t * heads + h
            total = total_ref[row]
            present = total > 0.0
            safe = jnp.where(present, total, 1.0)
            outs.append(acc_ref[row] * (1.0 / safe))
            sums.append(jnp.where(present, peak_ref[row] + jnp.log2(safe), LOWEST))
        if t % 2:
            pack_part(send_ref, t // 2, outs, sums)
        else:
            for h in range(heads):
                keep_ref[t // 2, h * HD:(h + 1) * HD, :] = outs[h]
                keep_sum_ref[t // 2, h:h + 1, :] = sums[h]


def relay_kernel(low_ref, high_ref, after_ref, k_out_ref, v_out_ref):
    k_out_ref[...] = low_ref[0:TILE]
    v_out_ref[...] = high_ref[TILE:2 * TILE]


def merge_kernel(mine_ref, mine_sum_ref, other_ref, keep_ref, keep_sum_ref, send_ref):
    heads = mine_ref.shape[1] // HD
    outs, sums = merged(mine_ref, mine_sum_ref, 1, other_ref, 1, heads)
    pack_part(send_ref, 0, outs, sums)
    outs, sums = merged(mine_ref, mine_sum_ref, 0, other_ref, 0, heads)
    for h in range(heads):
        keep_ref[0, h * HD:(h + 1) * HD, :] = outs[h]
        keep_sum_ref[0, h:h + 1, :] = sums[h]


def project_kernel(mine_ref, mine_sum_ref, other_ref, weight_ref, out_ref, held_ref):
    heads = mine_ref.shape[1] // HD
    outs, _ = merged(mine_ref, mine_sum_ref, 0, other_ref, 0, heads)
    for h in range(heads):
        held_ref[:, h * HD:(h + 1) * HD] = outs[h].T.astype(jnp.bfloat16)
    shares, _, width = out_ref.shape
    attended = held_ref[...]
    for j in range(shares):
        out_ref[j] = jnp.dot(
            attended, weight_ref[:, j * width:(j + 1) * width], preferred_element_type=jnp.float32
        ).astype(jnp.bfloat16)


def vmem_specs(count):
    return [pl.BlockSpec(memory_space=pltpu.VMEM)] * count


def attend_cost(blocks):
    return pl.CostEstimate(
        flops=blocks * 4 * TILE * TILE * HD, bytes_accessed=4 << 20, transcendentals=blocks * TILE * TILE
    )


PARAMS = pltpu.CompilerParams(vmem_limit_bytes=32 * 1024 * 1024)


def per_device(seq_size, head_size, queries, key_states, value_states, block_list, text_slots, out_weight):
    width = queries.shape[1]
    heads = width // HD
    planes = seq_size // GROUP
    me = lax.axis_index("seq")
    up = [(s, (s + GROUP) % seq_size) for s in range(seq_size)]
    down = [(s, (s - GROUP) % seq_size) for s in range(seq_size)]

    own = jnp.concatenate([key_states, value_states], axis=0)
    kv_up, kv_down = [own], [own]
    half = planes // 2
    for step in range(half - 1):
        kv_up.append(lax.ppermute(kv_up[-1], "seq", up))
        kv_down.append(lax.ppermute(kv_down[-1], "seq", down))

    listed = jnp.pad(block_list.astype(jnp.bfloat16), ((0, PART_ROWS - 1), (0, width - block_list.shape[1])))
    packed = jnp.concatenate([queries, listed], axis=0)
    tiles = [packed] + [
        lax.ppermute(packed, "seq", [(s, s ^ k) for s in range(seq_size)]) for k in range(1, GROUP)
    ]
    lists = jnp.concatenate([t[TILE:TILE + 1, :block_list.shape[1]] for t in tiles], axis=0)
    lists = jnp.concatenate(
        [lists.astype(jnp.int32), jnp.broadcast_to(text_slots[None, :], (GROUP, text_slots.shape[0]))], axis=1
    )
    order = [0, -1, 1, -3, 3, -2, 2, 4]
    slots = (me + GROUP * jnp.asarray(order, jnp.int32)) % seq_size
    need = jnp.any(lists[:, None, :] == slots[None, :, None], axis=2).astype(jnp.int32)

    rows = GROUP * heads
    state = (
        jax.ShapeDtypeStruct((rows, HD, TILE), jnp.float32),
        jax.ShapeDtypeStruct((rows, 1, TILE), jnp.float32),
        jax.ShapeDtypeStruct((rows, 1, TILE), jnp.float32),
    )
    factor = LOG2E / math.sqrt(HD)
    smem = [pl.BlockSpec(memory_space=pltpu.SMEM)]

    def scratch(count):
        return [
            pltpu.VMEM((count, TILE, width), jnp.bfloat16),
            pltpu.VMEM((count, heads, HD, TILE), jnp.bfloat16),
        ]

    stacked, *held = pl.pallas_call(
        functools.partial(near_kernel, factor),
        out_shape=(jax.ShapeDtypeStruct((GROUP, TILE, width), jnp.bfloat16),) + state,
        in_specs=smem + vmem_specs(GROUP + 3),
        out_specs=tuple(vmem_specs(4)),
        scratch_shapes=scratch(3),
        compiler_params=PARAMS,
        cost_estimate=attend_cost(27),
        name="attend_near",
    )(need, *tiles, own, kv_up[1], kv_down[1])
    shard = jax.ShapeDtypeStruct(key_states.shape, key_states.dtype)
    k_last, v_last = pl.pallas_call(
        relay_kernel,
        out_shape=(shard, shard),
        in_specs=vmem_specs(3),
        out_specs=tuple(vmem_specs(2)),
        compiler_params=PARAMS,
        name="relay",
    )(kv_up[-1], kv_down[-1], held[2])
    k_last = lax.ppermute(k_last, "seq", up)
    v_last = lax.ppermute(v_last, "seq", down)
    held = pl.pallas_call(
        functools.partial(far_kernel, factor, 3, 4),
        out_shape=state,
        in_specs=smem + vmem_specs(8),
        out_specs=tuple(vmem_specs(3)),
        scratch_shapes=scratch(4),
        compiler_params=PARAMS,
        cost_estimate=attend_cost(24),
        name="attend_far",
    )(need, stacked, kv_up[3], kv_down[3], kv_up[2], kv_down[2], *held)
    keep, keep_sum, send = pl.pallas_call(
        functools.partial(last_kernel, factor, 7),
        out_shape=(
            jax.ShapeDtypeStruct((2, width, TILE), jnp.float32),
            jax.ShapeDtypeStruct((2, 8, TILE), jnp.float32),
            jax.ShapeDtypeStruct((2, width + 2 * PART_ROWS, TILE), jnp.bfloat16),
        ),
        in_specs=smem + vmem_specs(6),
        out_specs=tuple(vmem_specs(3)),
        scratch_shapes=[pltpu.VMEM(s.shape, s.dtype) for s in state] + scratch(1),
        compiler_params=PARAMS,
        cost_estimate=attend_cost(12),
        name="attend_last",
    )(need, stacked, k_last, v_last, *held)

    other = lax.ppermute(send, "seq", [(s, s ^ 1) for s in range(seq_size)])
    keep, keep_sum, send = pl.pallas_call(
        merge_kernel,
        out_shape=(
            jax.ShapeDtypeStruct((1, width, TILE), jnp.float32),
            jax.ShapeDtypeStruct((1, 8, TILE), jnp.float32),
            jax.ShapeDtypeStruct((1, width + 2 * PART_ROWS, TILE), jnp.bfloat16),
        ),
        in_specs=vmem_specs(3),
        out_specs=tuple(vmem_specs(3)),
        compiler_params=PARAMS,
        name="merge",
    )(keep, keep_sum, other)
    other = lax.ppermute(send, "seq", [(s, s ^ 2) for s in range(seq_size)])
    shares = pl.pallas_call(
        project_kernel,
        out_shape=jax.ShapeDtypeStruct((head_size, TILE, width), jnp.bfloat16),
        in_specs=vmem_specs(4),
        out_specs=pl.BlockSpec(memory_space=pltpu.VMEM),
        scratch_shapes=[pltpu.VMEM((TILE, width), jnp.bfloat16)],
        compiler_params=PARAMS,
        name="project",
    )(keep, keep_sum, other, out_weight)
    shares = lax.all_to_all(shares, "head", 0, 0, tiled=False)
    return jnp.sum(shares.astype(jnp.float32), axis=0).astype(jnp.bfloat16)


def solution(mesh):
    return jax.shard_map(
        functools.partial(per_device, mesh.shape["seq"], mesh.shape["head"]),
        mesh=mesh,
        in_specs=(
            P("seq", "head"),
            P("seq", "head"),
            P("seq", "head"),
            P("seq", None),
            P(),
            P("head", None),
        ),
        out_specs=P("seq", "head"),
        check_vma=False,
    )
```

```python
import functools
import math

import jax
import jax.numpy as jnp
from jax import lax
from jax.experimental import pallas as pl
from jax.experimental.pallas import tpu as pltpu
from jax.sharding import PartitionSpec as P

HD = 128
TILE = 256
GROUP = 4
PART_ROWS = 16
LOWEST = -1e30
LOG2E = math.log2(math.e)


def pack_part(ref, index, outs, sums):
    heads = len(outs)
    for h in range(heads):
        ref[index, h * HD:(h + 1) * HD, :] = outs[h].astype(jnp.bfloat16)
    rows = jnp.concatenate(sums + [jnp.zeros((8 - heads, TILE), jnp.float32)], axis=0)
    high = rows.astype(jnp.bfloat16).astype(jnp.float32)
    middle = (rows - high).astype(jnp.bfloat16).astype(jnp.float32)
    low = rows - high - middle
    base = heads * HD
    ref[index, base:base + 16, :] = jnp.concatenate([high, middle], axis=0).astype(jnp.bfloat16)
    ref[index, base + 16:base + 32, :] = jnp.concatenate([low, jnp.zeros_like(low)], axis=0).astype(jnp.bfloat16)


def unpack_sums(ref, index, heads):
    base = heads * HD
    block = ref[index, base:base + 16, :].astype(jnp.float32)
    last = ref[index, base + 16:base + 32, :].astype(jnp.float32)
    return block[0:8] + block[8:16] + last[0:8]


def merged(mine_ref, mine_sum_ref, mine, other_ref, other, heads):
    others = unpack_sums(other_ref, other, heads)
    outs, sums = [], []
    for h in range(heads):
        rows = slice(h * HD, (h + 1) * HD)
        own_sum = mine_sum_ref[mine, h:h + 1, :]
        other_sum = others[h:h + 1]
        top = jnp.maximum(own_sum, other_sum)
        own_weight = jnp.exp2(own_sum - top)
        other_weight = jnp.exp2(other_sum - top)
        total = own_weight + other_weight
        outs.append(
            mine_ref[mine, rows, :] * (own_weight / total)
            + other_ref[other, rows, :].astype(jnp.float32) * (other_weight / total)
        )
        sums.append(top + jnp.log2(total))
    return outs, sums


def load_shards(need_ref, first, shards, k_ref, vt_ref):
    for j, (key, value) in enumerate(shards):
        wanted = need_ref[0, first + j]
        for t in range(1, need_ref.shape[0]):
            wanted = wanted + need_ref[t, first + j]

        @pl.when(wanted > 0)
        def _():
            k_ref[j] = key[...]
            for h in range(vt_ref.shape[1]):
                vt_ref[j, h] = value[:, h * HD:(h + 1) * HD].T


def visit_shards(factor, need_ref, first, count, q_ref, k_ref, vt_ref, state):
    acc_ref, peak_ref, total_ref = state
    heads = vt_ref.shape[1]

    def take(t, picks):
        def scores_of(h):
            cols = slice(h * HD, (h + 1) * HD)
            return [
                lax.dot_general(
                    k_ref[j, :, cols],
                    q_ref[t, :, cols],
                    (((1,), (1,)), ((), ())),
                    preferred_element_type=jnp.float32,
                )
                for j in picks
            ]

        following = scores_of(0)
        for h in range(heads):
            scores = following
            if h + 1 < heads:
                following = scores_of(h + 1)
            row = t * heads + h
            old = peak_ref[row]
            tops = [jnp.max(part, axis=0, keepdims=True) for part in scores]
            peak = jnp.maximum(old, functools.reduce(jnp.maximum, tops) * factor)
            weights = [jnp.exp2(part * factor - peak) for part in scores]
            shrink = jnp.exp2(old - peak)
            sums = [jnp.sum(w, axis=0, keepdims=True) for w in weights]
            dots = [
                jnp.dot(vt_ref[j, h], w.astype(jnp.bfloat16), preferred_element_type=jnp.float32)
                for j, w in zip(picks, weights)
            ]
            peak_ref[row] = peak
            total_ref[row] = total_ref[row] * shrink + sum(sums[1:], sums[0])
            acc_ref[row] = acc_ref[row] * shrink + sum(dots[1:], dots[0])

    def visit(t, carry):
        picks = [jnp.int32(0)] * count
        seen = jnp.int32(0)
        for j in range(count):
            wanted = need_ref[t, first + j]
            for i in range(j + 1):
                picks[i] = jnp.where((wanted > 0) & (seen == i), j, picks[i])
            seen = seen + wanted

        if count >= 3:

            @pl.when(seen >= 3)
            def _():
                take(t, picks[:3])

        if count >= 2:

            @pl.when(seen == 2)
            def _():
                take(t, picks[:2])

        @pl.when((seen == 1) | (seen == 4))
        def _():
            take(t, [jnp.where(seen == 4, picks[-1], picks[0])])

        return carry

    lax.fori_loop(0, q_ref.shape[0], visit, 0)


def list_wanted(seq_size, order, place_ref, q_refs, need_ref):
    slots = [lax.rem(place_ref[0] + (GROUP * plane + seq_size), seq_size) for plane in order]
    for t, q_ref in enumerate(q_refs):
        row = q_ref[TILE:TILE + PART_ROWS, 0:HD].astype(jnp.float32)
        bits = jnp.zeros_like(row)
        for j, slot in enumerate(slots):
            bits = bits + jnp.where(row == slot.astype(jnp.float32), float(1 << j), 0.0)
        code = jnp.sum(bits).astype(jnp.int32)
        for j, slot in enumerate(slots):
            wanted = (code >> j) & 1
            for i in range(1, place_ref.shape[0]):
                wanted = jnp.where(slot == place_ref[i], 1, wanted)
            need_ref[t, j] = wanted


def near_kernel(factor, seq_size, order, place_ref, *refs):
    q_refs, (own_ref, k_low, k_high, v_low, v_high) = refs[:GROUP], refs[GROUP:GROUP + 5]
    need_ref, stacked_ref, acc_ref, peak_ref, total_ref, k_ref, vt_ref = refs[GROUP + 5:]
    list_wanted(seq_size, order, place_ref, q_refs, need_ref)
    acc_ref[...] = jnp.zeros_like(acc_ref)
    peak_ref[...] = jnp.full_like(peak_ref, LOWEST)
    total_ref[...] = jnp.zeros_like(total_ref)
    for t, q_ref in enumerate(q_refs):
        stacked_ref[t] = q_ref[0:TILE, :]
    shards = [(own_ref.at[0:TILE], own_ref.at[TILE:2 * TILE]), (k_low, v_low), (k_high, v_high)]
    load_shards(need_ref, 0, shards, k_ref, vt_ref)
    visit_shards(factor, need_ref, 0, 3, stacked_ref, k_ref, vt_ref, (acc_ref, peak_ref, total_ref))


def far_kernel(factor, first, count, need_ref, stacked_ref, *refs):
    shards = list(zip(refs[:count], refs[count:2 * count]))
    held, state = refs[2 * count:2 * count + 3], refs[2 * count + 3:2 * count + 6]
    k_ref, vt_ref = refs[2 * count + 6:]
    for source, target in zip(held, state):
        target[...] = source[...]
    load_shards(need_ref, first, shards, k_ref, vt_ref)
    visit_shards(factor, need_ref, first, count, stacked_ref, k_ref, vt_ref, state)


def last_kernel(factor, first, need_ref, stacked_ref, *refs):
    shards = [refs[:2]]
    keep_ref, keep_sum_ref, send_ref, *state, k_ref, vt_ref = refs[5:]
    heads = vt_ref.shape[1]
    for source, target in zip(refs[2:5], state):
        target[...] = source[...]
    load_shards(need_ref, first, shards, k_ref, vt_ref)
    visit_shards(factor, need_ref, first, 1, stacked_ref, k_ref, vt_ref, state)
    acc_ref, peak_ref, total_ref = state
    for t in range(GROUP):
        outs, sums = [], []
        for h in range(heads):
            row = t * heads + h
            total = total_ref[row]
            present = total > 0.0
            safe = jnp.where(present, total, 1.0)
            outs.append(acc_ref[row] * (1.0 / safe))
            sums.append(jnp.where(present, peak_ref[row] + jnp.log2(safe), LOWEST))
        if t % 2:
            pack_part(send_ref, t // 2, outs, sums)
        else:
            for h in range(heads):
                keep_ref[t // 2, h * HD:(h + 1) * HD, :] = outs[h]
                keep_sum_ref[t // 2, h:h + 1, :] = sums[h]


def relay_kernel(k_ref, v_ref, after_ref, k_out_ref, v_out_ref):
    k_out_ref[...] = k_ref[...]
    v_out_ref[...] = v_ref[...]


def merge_kernel(mine_ref, mine_sum_ref, other_ref, keep_ref, keep_sum_ref, send_ref):
    heads = mine_ref.shape[1] // HD
    outs, sums = merged(mine_ref, mine_sum_ref, 1, other_ref, 1, heads)
    pack_part(send_ref, 0, outs, sums)
    outs, sums = merged(mine_ref, mine_sum_ref, 0, other_ref, 0, heads)
    for h in range(heads):
        keep_ref[0, h * HD:(h + 1) * HD, :] = outs[h]
        keep_sum_ref[0, h:h + 1, :] = sums[h]


def project_kernel(mine_ref, mine_sum_ref, other_ref, weight_ref, out_ref, held_ref):
    heads = mine_ref.shape[1] // HD
    outs, _ = merged(mine_ref, mine_sum_ref, 0, other_ref, 0, heads)
    for h in range(heads):
        held_ref[:, h * HD:(h + 1) * HD] = outs[h].T.astype(jnp.bfloat16)
    shares, _, width = out_ref.shape
    attended = held_ref[...]
    for j in range(shares):
        out_ref[j] = jnp.dot(
            attended, weight_ref[:, j * width:(j + 1) * width], preferred_element_type=jnp.float32
        ).astype(jnp.bfloat16)


def vmem_specs(count):
    return [pl.BlockSpec(memory_space=pltpu.VMEM)] * count


def attend_cost(blocks):
    return pl.CostEstimate(
        flops=blocks * 4 * TILE * TILE * HD, bytes_accessed=4 << 20, transcendentals=blocks * TILE * TILE
    )


PARAMS = pltpu.CompilerParams(vmem_limit_bytes=32 * 1024 * 1024)


def per_device(seq_size, head_size, queries, key_states, value_states, block_list, text_slots, out_weight):
    width = queries.shape[1]
    heads = width // HD
    planes = seq_size // GROUP
    me = lax.axis_index("seq")
    up = [(s, (s + GROUP) % seq_size) for s in range(seq_size)]
    down = [(s, (s - GROUP) % seq_size) for s in range(seq_size)]

    k_up, k_down, v_up, v_down = [key_states], [key_states], [value_states], [value_states]
    half = planes // 2
    for step in range(half - 1):
        k_up.append(lax.ppermute(k_up[-1], "seq", up))
        k_down.append(lax.ppermute(k_down[-1], "seq", down))
        v_up.append(lax.ppermute(v_up[-1], "seq", up))
        v_down.append(lax.ppermute(v_down[-1], "seq", down))

    listed = jnp.pad(
        block_list, ((0, PART_ROWS - 1), (0, width - block_list.shape[1])), constant_values=-1
    )
    packed = jnp.concatenate([queries, listed.astype(jnp.bfloat16)], axis=0)
    tiles = [packed] + [
        lax.ppermute(packed, "seq", [(s, s ^ k) for s in range(seq_size)]) for k in range(1, GROUP)
    ]
    order = (0, -1, 1, -3, 3, -2, 2, 4)
    place = jnp.concatenate([me.astype(jnp.int32)[None], text_slots])

    rows = GROUP * heads
    state = (
        jax.ShapeDtypeStruct((rows, HD, TILE), jnp.float32),
        jax.ShapeDtypeStruct((rows, 1, TILE), jnp.float32),
        jax.ShapeDtypeStruct((rows, 1, TILE), jnp.float32),
    )
    factor = LOG2E / math.sqrt(HD)
    smem = [pl.BlockSpec(memory_space=pltpu.SMEM)]

    def scratch(count):
        return [
            pltpu.VMEM((count, TILE, width), jnp.bfloat16),
            pltpu.VMEM((count, heads, HD, TILE), jnp.bfloat16),
        ]

    own = jnp.concatenate([key_states, value_states], axis=0)
    need, stacked, *held = pl.pallas_call(
        functools.partial(near_kernel, factor, seq_size, order),
        out_shape=(
            jax.ShapeDtypeStruct((GROUP, len(order)), jnp.int32),
            jax.ShapeDtypeStruct((GROUP, TILE, width), jnp.bfloat16),
        )
        + state,
        in_specs=smem + vmem_specs(GROUP + 5),
        out_specs=tuple(smem + vmem_specs(4)),
        scratch_shapes=scratch(3),
        compiler_params=PARAMS,
        cost_estimate=attend_cost(27),
        name="attend_near",
    )(place, *tiles, own, k_up[1], k_down[1], v_up[1], v_down[1])
    shard = jax.ShapeDtypeStruct(key_states.shape, key_states.dtype)
    k_last, v_last = pl.pallas_call(
        relay_kernel,
        out_shape=(shard, shard),
        in_specs=vmem_specs(3),
        out_specs=tuple(vmem_specs(2)),
        compiler_params=PARAMS,
        name="relay",
    )(k_up[-1], v_down[-1], held[2])
    k_last = lax.ppermute(k_last, "seq", up)
    v_last = lax.ppermute(v_last, "seq", down)
    held = pl.pallas_call(
        functools.partial(far_kernel, factor, 3, 4),
        out_shape=state,
        in_specs=smem + vmem_specs(12),
        out_specs=tuple(vmem_specs(3)),
        scratch_shapes=scratch(4),
        compiler_params=PARAMS,
        cost_estimate=attend_cost(24),
        name="attend_far",
    )(need, stacked, k_up[3], k_down[3], k_up[2], k_down[2], v_up[3], v_down[3], v_up[2], v_down[2], *held)
    keep, keep_sum, send = pl.pallas_call(
        functools.partial(last_kernel, factor, 7),
        out_shape=(
            jax.ShapeDtypeStruct((2, width, TILE), jnp.float32),
            jax.ShapeDtypeStruct((2, 8, TILE), jnp.float32),
            jax.ShapeDtypeStruct((2, width + 2 * PART_ROWS, TILE), jnp.bfloat16),
        ),
        in_specs=smem + vmem_specs(6),
        out_specs=tuple(vmem_specs(3)),
        scratch_shapes=[pltpu.VMEM(s.shape, s.dtype) for s in state] + scratch(1),
        compiler_params=PARAMS,
        cost_estimate=attend_cost(12),
        name="attend_last",
    )(need, stacked, k_last, v_last, *held)

    other = lax.ppermute(send, "seq", [(s, s ^ 1) for s in range(seq_size)])
    keep, keep_sum, send = pl.pallas_call(
        merge_kernel,
        out_shape=(
            jax.ShapeDtypeStruct((1, width, TILE), jnp.float32),
            jax.ShapeDtypeStruct((1, 8, TILE), jnp.float32),
            jax.ShapeDtypeStruct((1, width + 2 * PART_ROWS, TILE), jnp.bfloat16),
        ),
        in_specs=vmem_specs(3),
        out_specs=tuple(vmem_specs(3)),
        compiler_params=PARAMS,
        name="merge",
    )(keep, keep_sum, other)
    other = lax.ppermute(send, "seq", [(s, s ^ 2) for s in range(seq_size)])
    shares = pl.pallas_call(
        project_kernel,
        out_shape=jax.ShapeDtypeStruct((head_size, TILE, width), jnp.bfloat16),
        in_specs=vmem_specs(4),
        out_specs=pl.BlockSpec(memory_space=pltpu.VMEM),
        scratch_shapes=[pltpu.VMEM((TILE, width), jnp.bfloat16)],
        compiler_params=PARAMS,
        name="project",
    )(keep, keep_sum, other, out_weight)
    shares = lax.all_to_all(shares, "head", 0, 0, tiled=False)
    return jnp.sum(shares.astype(jnp.float32), axis=0).astype(jnp.bfloat16)


def solution(mesh):
    return jax.shard_map(
        functools.partial(per_device, mesh.shape["seq"], mesh.shape["head"]),
        mesh=mesh,
        in_specs=(
            P("seq", "head"),
            P("seq", "head"),
            P("seq", "head"),
            P("seq", None),
            P(),
            P("head", None),
        ),
        out_specs=P("seq", "head"),
        check_vma=False,
    )
```

```python
import functools
import math

import jax
import jax.numpy as jnp
from jax import lax
from jax.experimental import pallas as pl
from jax.experimental.pallas import tpu as pltpu
from jax.sharding import PartitionSpec as P

HD = 128
TILE = 256
GROUP = 4
PART_ROWS = 16
LOWEST = -1e30
LOG2E = math.log2(math.e)


def pack_part(ref, index, outs, sums):
    heads = len(outs)
    for h in range(heads):
        ref[index, h * HD:(h + 1) * HD, :] = outs[h].astype(jnp.bfloat16)
    rows = jnp.concatenate(sums + [jnp.zeros((8 - heads, TILE), jnp.float32)], axis=0)
    high = rows.astype(jnp.bfloat16).astype(jnp.float32)
    middle = (rows - high).astype(jnp.bfloat16).astype(jnp.float32)
    low = rows - high - middle
    base = heads * HD
    ref[index, base:base + 16, :] = jnp.concatenate([high, middle], axis=0).astype(jnp.bfloat16)
    ref[index, base + 16:base + 32, :] = jnp.concatenate([low, jnp.zeros_like(low)], axis=0).astype(jnp.bfloat16)


def unpack_sums(ref, index, heads):
    base = heads * HD
    block = ref[index, base:base + 16, :].astype(jnp.float32)
    last = ref[index, base + 16:base + 32, :].astype(jnp.float32)
    return block[0:8] + block[8:16] + last[0:8]


def merged(mine_ref, mine_sum_ref, mine, other_ref, other, heads):
    others = unpack_sums(other_ref, other, heads)
    outs, sums = [], []
    for h in range(heads):
        rows = slice(h * HD, (h + 1) * HD)
        own_sum = mine_sum_ref[mine, h:h + 1, :]
        other_sum = others[h:h + 1]
        top = jnp.maximum(own_sum, other_sum)
        own_weight = jnp.exp2(own_sum - top)
        other_weight = jnp.exp2(other_sum - top)
        total = own_weight + other_weight
        outs.append(
            mine_ref[mine, rows, :] * (own_weight / total)
            + other_ref[other, rows, :].astype(jnp.float32) * (other_weight / total)
        )
        sums.append(top + jnp.log2(total))
    return outs, sums


def load_shards(need_ref, first, shards, k_ref, vt_ref):
    for j, (key, value) in enumerate(shards):
        wanted = need_ref[0, first + j]
        for t in range(1, need_ref.shape[0]):
            wanted = wanted + need_ref[t, first + j]

        @pl.when(wanted > 0)
        def _():
            k_ref[j] = key[...]
            for h in range(vt_ref.shape[1]):
                vt_ref[j, h] = value[:, h * HD:(h + 1) * HD].T


def visit_shards(factor, need_ref, first, count, q_ref, k_ref, vt_ref, state):
    acc_ref, peak_ref, total_ref = state
    heads = vt_ref.shape[1]

    def take(t, picks):
        def scores_of(h):
            cols = slice(h * HD, (h + 1) * HD)
            return [
                lax.dot_general(
                    k_ref[j, :, cols],
                    q_ref[t, :, cols],
                    (((1,), (1,)), ((), ())),
                    preferred_element_type=jnp.float32,
                )
                for j in picks
            ]

        following = scores_of(0)
        for h in range(heads):
            scores = following
            if h + 1 < heads:
                following = scores_of(h + 1)
            row = t * heads + h
            old = peak_ref[row]
            tops = [jnp.max(part, axis=0, keepdims=True) for part in scores]
            peak = jnp.maximum(old, functools.reduce(jnp.maximum, tops) * factor)
            weights = [jnp.exp2(part * factor - peak) for part in scores]
            shrink = jnp.exp2(old - peak)
            sums = [jnp.sum(w, axis=0, keepdims=True) for w in weights]
            dots = [
                jnp.dot(vt_ref[j, h], w.astype(jnp.bfloat16), preferred_element_type=jnp.float32)
                for j, w in zip(picks, weights)
            ]
            peak_ref[row] = peak
            total_ref[row] = total_ref[row] * shrink + sum(sums[1:], sums[0])
            acc_ref[row] = acc_ref[row] * shrink + sum(dots[1:], dots[0])

    def visit(t, carry):
        picks = [jnp.int32(0)] * count
        seen = jnp.int32(0)
        for j in range(count):
            wanted = need_ref[t, first + j]
            for i in range(j + 1):
                picks[i] = jnp.where((wanted > 0) & (seen == i), j, picks[i])
            seen = seen + wanted

        @pl.when(seen >= 3)
        def _():
            take(t, picks[:3])

        @pl.when((seen == 2) | (seen == 5))
        def _():
            take(t, [jnp.where(seen == 5, late, early) for late, early in zip(picks[-2:], picks[:2])])

        @pl.when((seen == 1) | (seen == 4))
        def _():
            take(t, [jnp.where(seen == 4, picks[min(3, count - 1)], picks[0])])

        return carry

    lax.fori_loop(0, q_ref.shape[0], visit, 0)


def list_wanted(seq_size, order, place_ref, q_refs, need_ref):
    slots = [lax.rem(place_ref[0] + (GROUP * plane + seq_size), seq_size) for plane in order]
    for t, q_ref in enumerate(q_refs):
        row = q_ref[TILE:TILE + PART_ROWS, 0:HD].astype(jnp.float32)
        bits = jnp.zeros_like(row)
        for j, slot in enumerate(slots):
            bits = bits + jnp.where(row == slot.astype(jnp.float32), float(1 << j), 0.0)
        code = jnp.sum(bits).astype(jnp.int32)
        for j, slot in enumerate(slots):
            wanted = (code >> j) & 1
            for i in range(1, place_ref.shape[0]):
                wanted = jnp.where(slot == place_ref[i], 1, wanted)
            need_ref[t, j] = wanted


def near_kernel(factor, seq_size, order, place_ref, *refs):
    q_refs, (own_ref, k_low, k_high, v_low, v_high) = refs[:GROUP], refs[GROUP:GROUP + 5]
    need_ref, stacked_ref, acc_ref, peak_ref, total_ref, k_ref, vt_ref = refs[GROUP + 5:]
    list_wanted(seq_size, order, place_ref, q_refs, need_ref)
    acc_ref[...] = jnp.zeros_like(acc_ref)
    peak_ref[...] = jnp.full_like(peak_ref, LOWEST)
    total_ref[...] = jnp.zeros_like(total_ref)
    for t, q_ref in enumerate(q_refs):
        stacked_ref[t] = q_ref[0:TILE, :]
    shards = [(own_ref.at[0:TILE], own_ref.at[TILE:2 * TILE]), (k_low, v_low), (k_high, v_high)]
    load_shards(need_ref, 0, shards, k_ref, vt_ref)
    visit_shards(factor, need_ref, 0, 3, stacked_ref, k_ref, vt_ref, (acc_ref, peak_ref, total_ref))


def far_kernel(factor, first, count, need_ref, stacked_ref, *refs):
    shards = list(zip(refs[:count], refs[count:2 * count]))
    held = refs[2 * count:2 * count + 3]
    keep_ref, keep_sum_ref, send_ref, *state, k_ref, vt_ref = refs[2 * count + 3:]
    heads = vt_ref.shape[1]
    for source, target in zip(held, state):
        target[...] = source[...]
    load_shards(need_ref, first, shards, k_ref, vt_ref)
    visit_shards(factor, need_ref, first, count, stacked_ref, k_ref, vt_ref, state)
    acc_ref, peak_ref, total_ref = state
    for t in range(GROUP):
        outs, sums = [], []
        for h in range(heads):
            row = t * heads + h
            total = total_ref[row]
            present = total > 0.0
            safe = jnp.where(present, total, 1.0)
            outs.append(acc_ref[row] * (1.0 / safe))
            sums.append(jnp.where(present, peak_ref[row] + jnp.log2(safe), LOWEST))
        if t % 2:
            pack_part(send_ref, t // 2, outs, sums)
        else:
            for h in range(heads):
                keep_ref[t // 2, h * HD:(h + 1) * HD, :] = outs[h]
                keep_sum_ref[t // 2, h:h + 1, :] = sums[h]


def merge_kernel(mine_ref, mine_sum_ref, other_ref, keep_ref, keep_sum_ref, send_ref):
    heads = mine_ref.shape[1] // HD
    outs, sums = merged(mine_ref, mine_sum_ref, 1, other_ref, 1, heads)
    pack_part(send_ref, 0, outs, sums)
    outs, sums = merged(mine_ref, mine_sum_ref, 0, other_ref, 0, heads)
    for h in range(heads):
        keep_ref[0, h * HD:(h + 1) * HD, :] = outs[h]
        keep_sum_ref[0, h:h + 1, :] = sums[h]


def project_kernel(mine_ref, mine_sum_ref, other_ref, weight_ref, out_ref, held_ref):
    heads = mine_ref.shape[1] // HD
    outs, _ = merged(mine_ref, mine_sum_ref, 0, other_ref, 0, heads)
    for h in range(heads):
        held_ref[:, h * HD:(h + 1) * HD] = outs[h].T.astype(jnp.bfloat16)
    shares, _, width = out_ref.shape
    attended = held_ref[...]
    for j in range(shares):
        out_ref[j] = jnp.dot(
            attended, weight_ref[:, j * width:(j + 1) * width], preferred_element_type=jnp.float32
        ).astype(jnp.bfloat16)


def vmem_specs(count):
    return [pl.BlockSpec(memory_space=pltpu.VMEM)] * count


def attend_cost(blocks):
    return pl.CostEstimate(
        flops=blocks * 4 * TILE * TILE * HD, bytes_accessed=4 << 20, transcendentals=blocks * TILE * TILE
    )


PARAMS = pltpu.CompilerParams(vmem_limit_bytes=32 * 1024 * 1024)


def per_device(seq_size, head_size, queries, key_states, value_states, block_list, text_slots, out_weight):
    width = queries.shape[1]
    heads = width // HD
    planes = seq_size // GROUP
    me = lax.axis_index("seq")
    up = [(s, (s + GROUP) % seq_size) for s in range(seq_size)]
    down = [(s, (s - GROUP) % seq_size) for s in range(seq_size)]

    k_up, k_down, v_up, v_down = [key_states], [key_states], [value_states], [value_states]
    half = planes // 2
    for step in range(half):
        k_up.append(lax.ppermute(k_up[-1], "seq", up))
        if step < half - 1:
            k_down.append(lax.ppermute(k_down[-1], "seq", down))
            v_up.append(lax.ppermute(v_up[-1], "seq", up))
        v_down.append(lax.ppermute(v_down[-1], "seq", down))

    listed = jnp.pad(
        block_list, ((0, PART_ROWS - 1), (0, width - block_list.shape[1])), constant_values=-1
    )
    packed = jnp.concatenate([queries, listed.astype(jnp.bfloat16)], axis=0)
    tiles = [packed] + [
        lax.ppermute(packed, "seq", [(s, s ^ k) for s in range(seq_size)]) for k in range(1, GROUP)
    ]
    order = (0, -1, 1, -3, 3, 4, -2, 2)
    place = jnp.concatenate([me.astype(jnp.int32)[None], text_slots])

    rows = GROUP * heads
    state = (
        jax.ShapeDtypeStruct((rows, HD, TILE), jnp.float32),
        jax.ShapeDtypeStruct((rows, 1, TILE), jnp.float32),
        jax.ShapeDtypeStruct((rows, 1, TILE), jnp.float32),
    )
    factor = LOG2E / math.sqrt(HD)
    smem = [pl.BlockSpec(memory_space=pltpu.SMEM)]

    def scratch(count):
        return [
            pltpu.VMEM((count, TILE, width), jnp.bfloat16),
            pltpu.VMEM((count, heads, HD, TILE), jnp.bfloat16),
        ]

    own = jnp.concatenate([key_states, value_states], axis=0)
    need, stacked, *held = pl.pallas_call(
        functools.partial(near_kernel, factor, seq_size, order),
        out_shape=(
            jax.ShapeDtypeStruct((GROUP, len(order)), jnp.int32),
            jax.ShapeDtypeStruct((GROUP, TILE, width), jnp.bfloat16),
        )
        + state,
        in_specs=smem + vmem_specs(GROUP + 5),
        out_specs=tuple(smem + vmem_specs(4)),
        scratch_shapes=scratch(3),
        compiler_params=PARAMS,
        cost_estimate=attend_cost(27),
        name="attend_near",
    )(place, *tiles, own, k_up[1], k_down[1], v_up[1], v_down[1])
    far = [(k_up[3], v_up[3]), (k_down[3], v_down[3]), (k_up[4], v_down[4]), (k_up[2], v_up[2]), (k_down[2], v_down[2])]
    keep, keep_sum, send = pl.pallas_call(
        functools.partial(far_kernel, factor, 3, len(far)),
        out_shape=(
            jax.ShapeDtypeStruct((2, width, TILE), jnp.float32),
            jax.ShapeDtypeStruct((2, 8, TILE), jnp.float32),
            jax.ShapeDtypeStruct((2, width + 2 * PART_ROWS, TILE), jnp.bfloat16),
        ),
        in_specs=smem + vmem_specs(1 + 2 * len(far) + 3),
        out_specs=tuple(vmem_specs(3)),
        scratch_shapes=[pltpu.VMEM(s.shape, s.dtype) for s in state] + scratch(len(far)),
        compiler_params=PARAMS,
        cost_estimate=attend_cost(27),
        name="attend_far",
    )(need, stacked, *[k for k, _ in far], *[v for _, v in far], *held)

    other = lax.ppermute(send, "seq", [(s, s ^ 1) for s in range(seq_size)])
    keep, keep_sum, send = pl.pallas_call(
        merge_kernel,
        out_shape=(
            jax.ShapeDtypeStruct((1, width, TILE), jnp.float32),
            jax.ShapeDtypeStruct((1, 8, TILE), jnp.float32),
            jax.ShapeDtypeStruct((1, width + 2 * PART_ROWS, TILE), jnp.bfloat16),
        ),
        in_specs=vmem_specs(3),
        out_specs=tuple(vmem_specs(3)),
        compiler_params=PARAMS,
        name="merge",
    )(keep, keep_sum, other)
    other = lax.ppermute(send, "seq", [(s, s ^ 2) for s in range(seq_size)])
    shares = pl.pallas_call(
        project_kernel,
        out_shape=jax.ShapeDtypeStruct((head_size, TILE, width), jnp.bfloat16),
        in_specs=vmem_specs(4),
        out_specs=pl.BlockSpec(memory_space=pltpu.VMEM),
        scratch_shapes=[pltpu.VMEM((TILE, width), jnp.bfloat16)],
        compiler_params=PARAMS,
        name="project",
    )(keep, keep_sum, other, out_weight)
    shares = lax.all_to_all(shares, "head", 0, 0, tiled=False)
    return jnp.sum(shares.astype(jnp.float32), axis=0).astype(jnp.bfloat16)


def solution(mesh):
    return jax.shard_map(
        functools.partial(per_device, mesh.shape["seq"], mesh.shape["head"]),
        mesh=mesh,
        in_specs=(
            P("seq", "head"),
            P("seq", "head"),
            P("seq", "head"),
            P("seq", None),
            P(),
            P("head", None),
        ),
        out_specs=P("seq", "head"),
        check_vma=False,
    )
```

```python
import functools
import math

import jax
import jax.numpy as jnp
from jax import lax
from jax.experimental import pallas as pl
from jax.experimental.pallas import tpu as pltpu
from jax.sharding import PartitionSpec as P

HD = 128
TILE = 256
GROUP = 4
PART_ROWS = 16
LOWEST = -1e30
LOG2E = math.log2(math.e)


def pack_part(ref, index, outs, sums):
    heads = len(outs)
    for h in range(heads):
        ref[index, h * HD:(h + 1) * HD, :] = outs[h].astype(jnp.bfloat16)
    rows = jnp.concatenate(sums + [jnp.zeros((8 - heads, TILE), jnp.float32)], axis=0)
    high = rows.astype(jnp.bfloat16).astype(jnp.float32)
    middle = (rows - high).astype(jnp.bfloat16).astype(jnp.float32)
    low = rows - high - middle
    base = heads * HD
    ref[index, base:base + 16, :] = jnp.concatenate([high, middle], axis=0).astype(jnp.bfloat16)
    ref[index, base + 16:base + 32, :] = jnp.concatenate([low, jnp.zeros_like(low)], axis=0).astype(jnp.bfloat16)


def unpack_sums(ref, index, heads):
    base = heads * HD
    block = ref[index, base:base + 16, :].astype(jnp.float32)
    last = ref[index, base + 16:base + 32, :].astype(jnp.float32)
    return block[0:8] + block[8:16] + last[0:8]


def merged(mine_ref, mine_sum_ref, mine, other_ref, other, heads):
    others = unpack_sums(other_ref, other, heads)
    outs, sums = [], []
    for h in range(heads):
        rows = slice(h * HD, (h + 1) * HD)
        own_sum = mine_sum_ref[mine, h:h + 1, :]
        other_sum = others[h:h + 1]
        top = jnp.maximum(own_sum, other_sum)
        own_weight = jnp.exp2(own_sum - top)
        other_weight = jnp.exp2(other_sum - top)
        total = own_weight + other_weight
        outs.append(
            mine_ref[mine, rows, :] * (own_weight / total)
            + other_ref[other, rows, :].astype(jnp.float32) * (other_weight / total)
        )
        sums.append(top + jnp.log2(total))
    return outs, sums


def load_shards(need_ref, first, shards, k_ref, vt_ref):
    for j, (key, value) in enumerate(shards):
        wanted = need_ref[0, first + j]
        for t in range(1, need_ref.shape[0]):
            wanted = wanted + need_ref[t, first + j]

        @pl.when(wanted > 0)
        def _():
            k_ref[j] = key[...]
            for h in range(vt_ref.shape[1]):
                vt_ref[j, h] = value[:, h * HD:(h + 1) * HD].T


def visit_shards(factor, need_ref, first, count, q_ref, k_ref, vt_ref, state):
    acc_ref, peak_ref, total_ref = state
    heads = vt_ref.shape[1]

    def take(t, picks):
        def scores_of(h):
            cols = slice(h * HD, (h + 1) * HD)
            return [
                lax.dot_general(
                    k_ref[j, :, cols],
                    q_ref[t, :, cols],
                    (((1,), (1,)), ((), ())),
                    preferred_element_type=jnp.float32,
                )
                for j in picks
            ]

        following = scores_of(0)
        for h in range(heads):
            scores = following
            if h + 1 < heads:
                following = scores_of(h + 1)
            row = t * heads + h
            old = peak_ref[row]
            tops = [jnp.max(part, axis=0, keepdims=True) for part in scores]
            peak = jnp.maximum(old, functools.reduce(jnp.maximum, tops) * factor)
            weights = [jnp.exp2(part * factor - peak) for part in scores]
            shrink = jnp.exp2(old - peak)
            sums = [jnp.sum(w, axis=0, keepdims=True) for w in weights]
            dots = [
                jnp.dot(vt_ref[j, h], w.astype(jnp.bfloat16), preferred_element_type=jnp.float32)
                for j, w in zip(picks, weights)
            ]
            peak_ref[row] = peak
            total_ref[row] = total_ref[row] * shrink + sum(sums[1:], sums[0])
            acc_ref[row] = acc_ref[row] * shrink + sum(dots[1:], dots[0])

    def visit(t, carry):
        picks = [jnp.int32(0)] * count
        seen = jnp.int32(0)
        for j in range(count):
            wanted = need_ref[t, first + j]
            for i in range(j + 1):
                picks[i] = jnp.where((wanted > 0) & (seen == i), j, picks[i])
            seen = seen + wanted

        @pl.when(seen >= 3)
        def _():
            take(t, picks[:3])

        @pl.when((seen == 2) | (seen == 5))
        def _():
            take(t, [jnp.where(seen == 5, late, early) for late, early in zip(picks[-2:], picks[:2])])

        @pl.when((seen == 1) | (seen == 4))
        def _():
            take(t, [jnp.where(seen == 4, picks[min(3, count - 1)], picks[0])])

        return carry

    lax.fori_loop(0, q_ref.shape[0], visit, 0)


def list_wanted(seq_size, order, place_ref, q_refs, need_ref):
    slots = [lax.rem(place_ref[0] + (GROUP * plane + seq_size), seq_size) for plane in order]
    for t, q_ref in enumerate(q_refs):
        row = q_ref[TILE:TILE + PART_ROWS, 0:HD].astype(jnp.float32)
        bits = jnp.zeros_like(row)
        for j, slot in enumerate(slots):
            bits = bits + jnp.where(row == slot.astype(jnp.float32), float(1 << j), 0.0)
        code = jnp.sum(bits).astype(jnp.int32)
        for j, slot in enumerate(slots):
            wanted = (code >> j) & 1
            for i in range(1, place_ref.shape[0]):
                wanted = jnp.where(slot == place_ref[i], 1, wanted)
            need_ref[t, j] = wanted


def near_kernel(factor, seq_size, order, place_ref, *refs):
    q_refs, (own_ref, k_low, k_high, v_low, v_high) = refs[:GROUP], refs[GROUP:GROUP + 5]
    need_ref, stacked_ref, acc_ref, peak_ref, total_ref, k_ref, vt_ref = refs[GROUP + 5:]
    list_wanted(seq_size, order, place_ref, q_refs, need_ref)
    acc_ref[...] = jnp.zeros_like(acc_ref)
    peak_ref[...] = jnp.full_like(peak_ref, LOWEST)
    total_ref[...] = jnp.zeros_like(total_ref)
    for t, q_ref in enumerate(q_refs):
        stacked_ref[t] = q_ref[0:TILE, :]
    shards = [(own_ref.at[0:TILE], own_ref.at[TILE:2 * TILE]), (k_low, v_low), (k_high, v_high)]
    load_shards(need_ref, 0, shards, k_ref, vt_ref)
    visit_shards(factor, need_ref, 0, 3, stacked_ref, k_ref, vt_ref, (acc_ref, peak_ref, total_ref))


def far_kernel(factor, first, count, need_ref, stacked_ref, *refs):
    shards = list(zip(refs[:count], refs[count:2 * count]))
    held = refs[2 * count:2 * count + 3]
    keep_ref, keep_sum_ref, send_ref, *state, k_ref, vt_ref = refs[2 * count + 3:]
    heads = vt_ref.shape[1]
    for source, target in zip(held, state):
        target[...] = source[...]
    load_shards(need_ref, first, shards, k_ref, vt_ref)
    visit_shards(factor, need_ref, first, count, stacked_ref, k_ref, vt_ref, state)
    acc_ref, peak_ref, total_ref = state
    for t in range(GROUP):
        outs, sums = [], []
        for h in range(heads):
            row = t * heads + h
            total = total_ref[row]
            present = total > 0.0
            safe = jnp.where(present, total, 1.0)
            outs.append(acc_ref[row] * (1.0 / safe))
            sums.append(jnp.where(present, peak_ref[row] + jnp.log2(safe), LOWEST))
        if t % 2:
            pack_part(send_ref, t // 2, outs, sums)
        else:
            for h in range(heads):
                keep_ref[t // 2, h * HD:(h + 1) * HD, :] = outs[h]
                keep_sum_ref[t // 2, h:h + 1, :] = sums[h]


def merge_kernel(mine_ref, mine_sum_ref, other_ref, keep_ref, keep_sum_ref, send_ref):
    heads = mine_ref.shape[1] // HD
    outs, sums = merged(mine_ref, mine_sum_ref, 1, other_ref, 1, heads)
    pack_part(send_ref, 0, outs, sums)
    outs, sums = merged(mine_ref, mine_sum_ref, 0, other_ref, 0, heads)
    for h in range(heads):
        keep_ref[0, h * HD:(h + 1) * HD, :] = outs[h]
        keep_sum_ref[0, h:h + 1, :] = sums[h]


def finish_kernel(mine_ref, mine_sum_ref, other_ref, out_ref):
    heads = mine_ref.shape[1] // HD
    outs, _ = merged(mine_ref, mine_sum_ref, 0, other_ref, 0, heads)
    for h in range(heads):
        out_ref[:, h * HD:(h + 1) * HD] = outs[h].T.astype(jnp.bfloat16)


def pick_kernel(side_ref, weight_ref, out_ref):
    width = weight_ref.shape[0]
    for j in range(out_ref.shape[1] // width):
        begin = pl.multiple_of((2 * j + 1 - side_ref[0]) * width, HD)
        out_ref[:, j * width:(j + 1) * width] = weight_ref[:, pl.ds(begin, width)]


def project_kernel(side_ref, mine_ref, other_ref, weight_ref, other_weight_ref, out_ref):
    shares, _, width = out_ref.shape
    for j in range(shares):
        begin = pl.multiple_of((2 * j + side_ref[0]) * width, HD)
        mixed = jnp.dot(mine_ref[...], weight_ref[:, pl.ds(begin, width)], preferred_element_type=jnp.float32)
        mixed = mixed + jnp.dot(
            other_ref[...], other_weight_ref[:, j * width:(j + 1) * width], preferred_element_type=jnp.float32
        )
        out_ref[j] = mixed.astype(jnp.bfloat16)


def vmem_specs(count):
    return [pl.BlockSpec(memory_space=pltpu.VMEM)] * count


def attend_cost(blocks):
    return pl.CostEstimate(
        flops=blocks * 4 * TILE * TILE * HD, bytes_accessed=4 << 20, transcendentals=blocks * TILE * TILE
    )


PARAMS = pltpu.CompilerParams(vmem_limit_bytes=32 * 1024 * 1024)


def per_device(seq_size, head_size, queries, key_states, value_states, block_list, text_slots, out_weight):
    width = queries.shape[1]
    heads = width // HD
    planes = seq_size // GROUP
    me = lax.axis_index("seq")
    up = [(s, (s + GROUP) % seq_size) for s in range(seq_size)]
    down = [(s, (s - GROUP) % seq_size) for s in range(seq_size)]

    k_up, k_down, v_up, v_down = [key_states], [key_states], [value_states], [value_states]
    half = planes // 2
    for step in range(half):
        k_up.append(lax.ppermute(k_up[-1], "seq", up))
        if step < half - 1:
            k_down.append(lax.ppermute(k_down[-1], "seq", down))
            v_up.append(lax.ppermute(v_up[-1], "seq", up))
        v_down.append(lax.ppermute(v_down[-1], "seq", down))

    side = lax.axis_index("head") % 2
    picked = pl.pallas_call(
        pick_kernel,
        out_shape=jax.ShapeDtypeStruct((width, head_size // 2 * width), out_weight.dtype),
        in_specs=[pl.BlockSpec(memory_space=pltpu.SMEM)] + vmem_specs(1),
        out_specs=pl.BlockSpec(memory_space=pltpu.VMEM),
        compiler_params=PARAMS,
        name="pick",
    )(side[None], out_weight)
    other_weight = lax.ppermute(picked, "head", [(h, h ^ 1) for h in range(head_size)])

    listed = jnp.pad(
        block_list, ((0, PART_ROWS - 1), (0, width - block_list.shape[1])), constant_values=-1
    )
    packed = jnp.concatenate([queries, listed.astype(jnp.bfloat16)], axis=0)
    tiles = [packed] + [
        lax.ppermute(packed, "seq", [(s, s ^ k) for s in range(seq_size)]) for k in range(1, GROUP)
    ]
    order = (0, -1, 1, -3, 3, 4, -2, 2)
    place = jnp.concatenate([me.astype(jnp.int32)[None], text_slots])

    rows = GROUP * heads
    state = (
        jax.ShapeDtypeStruct((rows, HD, TILE), jnp.float32),
        jax.ShapeDtypeStruct((rows, 1, TILE), jnp.float32),
        jax.ShapeDtypeStruct((rows, 1, TILE), jnp.float32),
    )
    factor = LOG2E / math.sqrt(HD)
    smem = [pl.BlockSpec(memory_space=pltpu.SMEM)]

    def scratch(count):
        return [
            pltpu.VMEM((count, TILE, width), jnp.bfloat16),
            pltpu.VMEM((count, heads, HD, TILE), jnp.bfloat16),
        ]

    own = jnp.concatenate([key_states, value_states], axis=0)
    need, stacked, *held = pl.pallas_call(
        functools.partial(near_kernel, factor, seq_size, order),
        out_shape=(
            jax.ShapeDtypeStruct((GROUP, len(order)), jnp.int32),
            jax.ShapeDtypeStruct((GROUP, TILE, width), jnp.bfloat16),
        )
        + state,
        in_specs=smem + vmem_specs(GROUP + 5),
        out_specs=tuple(smem + vmem_specs(4)),
        scratch_shapes=scratch(3),
        compiler_params=PARAMS,
        cost_estimate=attend_cost(27),
        name="attend_near",
    )(place, *tiles, own, k_up[1], k_down[1], v_up[1], v_down[1])
    far = [(k_up[3], v_up[3]), (k_down[3], v_down[3]), (k_up[4], v_down[4]), (k_up[2], v_up[2]), (k_down[2], v_down[2])]
    keep, keep_sum, send = pl.pallas_call(
        functools.partial(far_kernel, factor, 3, len(far)),
        out_shape=(
            jax.ShapeDtypeStruct((2, width, TILE), jnp.float32),
            jax.ShapeDtypeStruct((2, 8, TILE), jnp.float32),
            jax.ShapeDtypeStruct((2, width + 2 * PART_ROWS, TILE), jnp.bfloat16),
        ),
        in_specs=smem + vmem_specs(1 + 2 * len(far) + 3),
        out_specs=tuple(vmem_specs(3)),
        scratch_shapes=[pltpu.VMEM(s.shape, s.dtype) for s in state] + scratch(len(far)),
        compiler_params=PARAMS,
        cost_estimate=attend_cost(27),
        name="attend_far",
    )(need, stacked, *[k for k, _ in far], *[v for _, v in far], *held)

    other = lax.ppermute(send, "seq", [(s, s ^ 1) for s in range(seq_size)])
    keep, keep_sum, send = pl.pallas_call(
        merge_kernel,
        out_shape=(
            jax.ShapeDtypeStruct((1, width, TILE), jnp.float32),
            jax.ShapeDtypeStruct((1, 8, TILE), jnp.float32),
            jax.ShapeDtypeStruct((1, width + 2 * PART_ROWS, TILE), jnp.bfloat16),
        ),
        in_specs=vmem_specs(3),
        out_specs=tuple(vmem_specs(3)),
        compiler_params=PARAMS,
        name="merge",
    )(keep, keep_sum, other)
    other = lax.ppermute(send, "seq", [(s, s ^ 2) for s in range(seq_size)])
    attended = pl.pallas_call(
        finish_kernel,
        out_shape=jax.ShapeDtypeStruct((TILE, width), jnp.bfloat16),
        in_specs=vmem_specs(3),
        out_specs=pl.BlockSpec(memory_space=pltpu.VMEM),
        compiler_params=PARAMS,
        name="finish",
    )(keep, keep_sum, other)
    swap_side = [(h, h ^ 1) for h in range(head_size)]
    shares = pl.pallas_call(
        project_kernel,
        out_shape=jax.ShapeDtypeStruct((head_size // 2, TILE, width), jnp.bfloat16),
        in_specs=smem + vmem_specs(4),
        out_specs=pl.BlockSpec(memory_space=pltpu.VMEM),
        compiler_params=PARAMS,
        name="project",
    )(side[None], attended, lax.ppermute(attended, "head", swap_side), out_weight, other_weight)
    sides = [list(range(k, head_size, 2)) for k in range(2)]
    shares = lax.all_to_all(shares, "head", 0, 0, axis_index_groups=sides, tiled=True)
    return jnp.sum(shares.astype(jnp.float32), axis=0).astype(jnp.bfloat16)


def solution(mesh):
    return jax.shard_map(
        functools.partial(per_device, mesh.shape["seq"], mesh.shape["head"]),
        mesh=mesh,
        in_specs=(
            P("seq", "head"),
            P("seq", "head"),
            P("seq", "head"),
            P("seq", None),
            P(),
            P("head", None),
        ),
        out_specs=P("seq", "head"),
        check_vma=False,
    )
```

```python
import functools
import math

import jax
import jax.numpy as jnp
from jax import lax
from jax.experimental import pallas as pl
from jax.experimental.pallas import tpu as pltpu
from jax.sharding import PartitionSpec as P

HD = 128
TILE = 256
GROUP = 4
PART_ROWS = 16
LOWEST = -1e30
LOG2E = math.log2(math.e)


def pack_part(ref, index, outs, sums):
    heads = len(outs)
    for h in range(heads):
        ref[index, h * HD:(h + 1) * HD, :] = outs[h].astype(jnp.bfloat16)
    rows = jnp.concatenate(sums + [jnp.zeros((8 - heads, TILE), jnp.float32)], axis=0)
    high = rows.astype(jnp.bfloat16).astype(jnp.float32)
    middle = (rows - high).astype(jnp.bfloat16).astype(jnp.float32)
    low = rows - high - middle
    base = heads * HD
    ref[index, base:base + 16, :] = jnp.concatenate([high, middle], axis=0).astype(jnp.bfloat16)
    ref[index, base + 16:base + 32, :] = jnp.concatenate([low, jnp.zeros_like(low)], axis=0).astype(jnp.bfloat16)


def unpack_sums(ref, index, heads):
    base = heads * HD
    block = ref[index, base:base + 16, :].astype(jnp.float32)
    last = ref[index, base + 16:base + 32, :].astype(jnp.float32)
    return block[0:8] + block[8:16] + last[0:8]


def merged(mine_ref, mine_sum_ref, mine, other_ref, other, heads):
    others = unpack_sums(other_ref, other, heads)
    outs, sums = [], []
    for h in range(heads):
        rows = slice(h * HD, (h + 1) * HD)
        own_sum = mine_sum_ref[mine, h:h + 1, :]
        other_sum = others[h:h + 1]
        top = jnp.maximum(own_sum, other_sum)
        own_weight = jnp.exp2(own_sum - top)
        other_weight = jnp.exp2(other_sum - top)
        total = own_weight + other_weight
        outs.append(
            mine_ref[mine, rows, :] * (own_weight / total)
            + other_ref[other, rows, :].astype(jnp.float32) * (other_weight / total)
        )
        sums.append(top + jnp.log2(total))
    return outs, sums


def load_shards(need_ref, first, shards, k_ref, vt_ref):
    for j, (key, value) in enumerate(shards):
        wanted = need_ref[0, first + j]
        for t in range(1, need_ref.shape[0]):
            wanted = wanted + need_ref[t, first + j]

        @pl.when(wanted > 0)
        def _():
            k_ref[j] = key[...]
            for h in range(vt_ref.shape[1]):
                vt_ref[j, h] = value[:, h * HD:(h + 1) * HD].T


def visit_shards(factor, need_ref, first, count, q_ref, k_ref, vt_ref, state):
    acc_ref, peak_ref, total_ref = state
    heads = vt_ref.shape[1]

    def take(t, picks):
        def scores_of(h):
            cols = slice(h * HD, (h + 1) * HD)
            return [
                lax.dot_general(
                    k_ref[j, :, cols],
                    q_ref[t, :, cols],
                    (((1,), (1,)), ((), ())),
                    preferred_element_type=jnp.float32,
                )
                for j in picks
            ]

        following = scores_of(0)
        for h in range(heads):
            scores = following
            if h + 1 < heads:
                following = scores_of(h + 1)
            row = t * heads + h
            old = peak_ref[row]
            tops = [jnp.max(part, axis=0, keepdims=True) for part in scores]
            peak = jnp.maximum(old, functools.reduce(jnp.maximum, tops) * factor)
            weights = [jnp.exp2(part * factor - peak) for part in scores]
            shrink = jnp.exp2(old - peak)
            sums = [jnp.sum(w, axis=0, keepdims=True) for w in weights]
            dots = [
                jnp.dot(vt_ref[j, h], w.astype(jnp.bfloat16), preferred_element_type=jnp.float32)
                for j, w in zip(picks, weights)
            ]
            peak_ref[row] = peak
            total_ref[row] = total_ref[row] * shrink + sum(sums[1:], sums[0])
            acc_ref[row] = acc_ref[row] * shrink + sum(dots[1:], dots[0])

    def visit(t, carry):
        picks = [jnp.int32(0)] * count
        seen = jnp.int32(0)
        for j in range(count):
            wanted = need_ref[t, first + j]
            for i in range(j + 1):
                picks[i] = jnp.where((wanted > 0) & (seen == i), j, picks[i])
            seen = seen + wanted

        @pl.when(seen >= 3)
        def _():
            take(t, picks[:3])

        @pl.when((seen == 2) | (seen == 5))
        def _():
            take(t, [jnp.where(seen == 5, late, early) for late, early in zip(picks[-2:], picks[:2])])

        @pl.when((seen == 1) | (seen == 4))
        def _():
            take(t, [jnp.where(seen == 4, picks[min(3, count - 1)], picks[0])])

        return carry

    lax.fori_loop(0, q_ref.shape[0], visit, 0)


def list_wanted(seq_size, order, place_ref, q_refs, need_ref):
    slots = [lax.rem(place_ref[0] + (GROUP * plane + seq_size), seq_size) for plane in order]
    for t, q_ref in enumerate(q_refs):
        row = q_ref[TILE:TILE + PART_ROWS, 0:HD].astype(jnp.float32)
        bits = jnp.zeros_like(row)
        for j, slot in enumerate(slots):
            bits = bits + jnp.where(row == slot.astype(jnp.float32), float(1 << j), 0.0)
        code = jnp.sum(bits).astype(jnp.int32)
        for j, slot in enumerate(slots):
            wanted = (code >> j) & 1
            for i in range(1, place_ref.shape[0]):
                wanted = jnp.where(slot == place_ref[i], 1, wanted)
            need_ref[t, j] = wanted


def near_kernel(factor, seq_size, order, place_ref, *refs):
    q_refs, (own_ref, k_low, k_high, v_low, v_high) = refs[:GROUP], refs[GROUP:GROUP + 5]
    need_ref, stacked_ref, acc_ref, peak_ref, total_ref, k_ref, vt_ref = refs[GROUP + 5:]
    list_wanted(seq_size, order, place_ref, q_refs, need_ref)
    acc_ref[...] = jnp.zeros_like(acc_ref)
    peak_ref[...] = jnp.full_like(peak_ref, LOWEST)
    total_ref[...] = jnp.zeros_like(total_ref)
    for t, q_ref in enumerate(q_refs):
        stacked_ref[t] = q_ref[0:TILE, :]
    shards = [(own_ref.at[0:TILE], own_ref.at[TILE:2 * TILE]), (k_low, v_low), (k_high, v_high)]
    load_shards(need_ref, 0, shards, k_ref, vt_ref)
    visit_shards(factor, need_ref, 0, 3, stacked_ref, k_ref, vt_ref, (acc_ref, peak_ref, total_ref))


def far_kernel(factor, first, count, need_ref, stacked_ref, *refs):
    shards = list(zip(refs[:count], refs[count:2 * count]))
    held = refs[2 * count:2 * count + 3]
    keep_ref, keep_sum_ref, send_ref, *state, k_ref, vt_ref = refs[2 * count + 3:]
    heads = vt_ref.shape[1]
    for source, target in zip(held, state):
        target[...] = source[...]
    load_shards(need_ref, first, shards, k_ref, vt_ref)
    visit_shards(factor, need_ref, first, count, stacked_ref, k_ref, vt_ref, state)
    acc_ref, peak_ref, total_ref = state
    for t in range(GROUP):
        outs, sums = [], []
        for h in range(heads):
            row = t * heads + h
            total = total_ref[row]
            present = total > 0.0
            safe = jnp.where(present, total, 1.0)
            outs.append(acc_ref[row] * (1.0 / safe))
            sums.append(jnp.where(present, peak_ref[row] + jnp.log2(safe), LOWEST))
        if t % 2:
            pack_part(send_ref, t // 2, outs, sums)
        else:
            for h in range(heads):
                keep_ref[t // 2, h * HD:(h + 1) * HD, :] = outs[h]
                keep_sum_ref[t // 2, h:h + 1, :] = sums[h]


def merge_kernel(mine_ref, mine_sum_ref, other_ref, keep_ref, keep_sum_ref, send_ref):
    heads = mine_ref.shape[1] // HD
    outs, sums = merged(mine_ref, mine_sum_ref, 1, other_ref, 1, heads)
    pack_part(send_ref, 0, outs, sums)
    outs, sums = merged(mine_ref, mine_sum_ref, 0, other_ref, 0, heads)
    for h in range(heads):
        keep_ref[0, h * HD:(h + 1) * HD, :] = outs[h]
        keep_sum_ref[0, h:h + 1, :] = sums[h]


def finish_kernel(mine_ref, mine_sum_ref, other_ref, out_ref):
    heads = mine_ref.shape[1] // HD
    outs, _ = merged(mine_ref, mine_sum_ref, 0, other_ref, 0, heads)
    for h in range(heads):
        out_ref[:, h * HD:(h + 1) * HD] = outs[h].T.astype(jnp.bfloat16)


def pick_kernel(side_ref, weight_ref, out_ref):
    width = weight_ref.shape[0]
    for j in range(out_ref.shape[1] // width):
        begin = pl.multiple_of((2 * j + 1 - side_ref[0]) * width, HD)
        out_ref[:, j * width:(j + 1) * width] = weight_ref[:, pl.ds(begin, width)]


def project_kernel(side_ref, mine_ref, other_ref, weight_ref, other_weight_ref, out_ref):
    shares, _, width = out_ref.shape
    for j in range(shares):
        begin = pl.multiple_of((2 * j + side_ref[0]) * width, HD)
        mixed = jnp.dot(mine_ref[...], weight_ref[:, pl.ds(begin, width)], preferred_element_type=jnp.float32)
        mixed = mixed + jnp.dot(
            other_ref[...], other_weight_ref[:, j * width:(j + 1) * width], preferred_element_type=jnp.float32
        )
        out_ref[j] = mixed.astype(jnp.bfloat16)


def vmem_specs(count):
    return [pl.BlockSpec(memory_space=pltpu.VMEM)] * count


def attend_cost(blocks):
    return pl.CostEstimate(
        flops=blocks * 4 * TILE * TILE * HD, bytes_accessed=4 << 20, transcendentals=blocks * TILE * TILE
    )


PARAMS = pltpu.CompilerParams(vmem_limit_bytes=16 * 1024 * 1024)


def per_device(seq_size, head_size, queries, key_states, value_states, block_list, text_slots, out_weight):
    width = queries.shape[1]
    heads = width // HD
    planes = seq_size // GROUP
    me = lax.axis_index("seq")
    up = [(s, (s + GROUP) % seq_size) for s in range(seq_size)]
    down = [(s, (s - GROUP) % seq_size) for s in range(seq_size)]

    k_up, k_down, v_up, v_down = [key_states], [key_states], [value_states], [value_states]
    half = planes // 2
    for step in range(half):
        k_up.append(lax.ppermute(k_up[-1], "seq", up))
        if step < half - 1:
            k_down.append(lax.ppermute(k_down[-1], "seq", down))
            v_up.append(lax.ppermute(v_up[-1], "seq", up))
        v_down.append(lax.ppermute(v_down[-1], "seq", down))

    side = lax.axis_index("head") % 2
    picked = pl.pallas_call(
        pick_kernel,
        out_shape=jax.ShapeDtypeStruct((width, head_size // 2 * width), out_weight.dtype),
        in_specs=[pl.BlockSpec(memory_space=pltpu.SMEM)] + vmem_specs(1),
        out_specs=pl.BlockSpec(memory_space=pltpu.VMEM),
        compiler_params=PARAMS,
        name="pick",
    )(side[None], out_weight)
    other_weight = lax.ppermute(picked, "head", [(h, h ^ 1) for h in range(head_size)])

    listed = jnp.pad(
        block_list, ((0, PART_ROWS - 1), (0, width - block_list.shape[1])), constant_values=-1
    )
    packed = jnp.concatenate([queries, listed.astype(jnp.bfloat16)], axis=0)
    tiles = [packed] + [
        lax.ppermute(packed, "seq", [(s, s ^ k) for s in range(seq_size)]) for k in range(1, GROUP)
    ]
    order = (0, -1, 1, -3, 3, 4, -2, 2)
    place = jnp.concatenate([me.astype(jnp.int32)[None], text_slots])

    rows = GROUP * heads
    state = (
        jax.ShapeDtypeStruct((rows, HD, TILE), jnp.float32),
        jax.ShapeDtypeStruct((rows, 1, TILE), jnp.float32),
        jax.ShapeDtypeStruct((rows, 1, TILE), jnp.float32),
    )
    factor = LOG2E / math.sqrt(HD)
    smem = [pl.BlockSpec(memory_space=pltpu.SMEM)]

    def scratch(count):
        return [
            pltpu.VMEM((count, TILE, width), jnp.bfloat16),
            pltpu.VMEM((count, heads, HD, TILE), jnp.bfloat16),
        ]

    own = jnp.concatenate([key_states, value_states], axis=0)
    need, stacked, *held = pl.pallas_call(
        functools.partial(near_kernel, factor, seq_size, order),
        out_shape=(
            jax.ShapeDtypeStruct((GROUP, len(order)), jnp.int32),
            jax.ShapeDtypeStruct((GROUP, TILE, width), jnp.bfloat16),
        )
        + state,
        in_specs=smem + vmem_specs(GROUP + 5),
        out_specs=tuple(smem + vmem_specs(4)),
        scratch_shapes=scratch(3),
        compiler_params=PARAMS,
        cost_estimate=attend_cost(27),
        name="attend_near",
    )(place, *tiles, own, k_up[1], k_down[1], v_up[1], v_down[1])
    far = [(k_up[3], v_up[3]), (k_down[3], v_down[3]), (k_up[4], v_down[4]), (k_up[2], v_up[2]), (k_down[2], v_down[2])]
    keep, keep_sum, send = pl.pallas_call(
        functools.partial(far_kernel, factor, 3, len(far)),
        out_shape=(
            jax.ShapeDtypeStruct((2, width, TILE), jnp.float32),
            jax.ShapeDtypeStruct((2, 8, TILE), jnp.float32),
            jax.ShapeDtypeStruct((2, width + 2 * PART_ROWS, TILE), jnp.bfloat16),
        ),
        in_specs=smem + vmem_specs(1 + 2 * len(far) + 3),
        out_specs=tuple(vmem_specs(3)),
        scratch_shapes=[pltpu.VMEM(s.shape, s.dtype) for s in state] + scratch(len(far)),
        compiler_params=PARAMS,
        cost_estimate=attend_cost(27),
        name="attend_far",
    )(need, stacked, *[k for k, _ in far], *[v for _, v in far], *held)

    other = lax.ppermute(send, "seq", [(s, s ^ 1) for s in range(seq_size)])
    keep, keep_sum, send = pl.pallas_call(
        merge_kernel,
        out_shape=(
            jax.ShapeDtypeStruct((1, width, TILE), jnp.float32),
            jax.ShapeDtypeStruct((1, 8, TILE), jnp.float32),
            jax.ShapeDtypeStruct((1, width + 2 * PART_ROWS, TILE), jnp.bfloat16),
        ),
        in_specs=vmem_specs(3),
        out_specs=tuple(vmem_specs(3)),
        compiler_params=PARAMS,
        name="merge",
    )(keep, keep_sum, other)
    other = lax.ppermute(send, "seq", [(s, s ^ 2) for s in range(seq_size)])
    attended = pl.pallas_call(
        finish_kernel,
        out_shape=jax.ShapeDtypeStruct((TILE, width), jnp.bfloat16),
        in_specs=vmem_specs(3),
        out_specs=pl.BlockSpec(memory_space=pltpu.VMEM),
        compiler_params=PARAMS,
        name="finish",
    )(keep, keep_sum, other)
    swap_side = [(h, h ^ 1) for h in range(head_size)]
    shares = pl.pallas_call(
        project_kernel,
        out_shape=jax.ShapeDtypeStruct((head_size // 2, TILE, width), jnp.bfloat16),
        in_specs=smem + vmem_specs(4),
        out_specs=pl.BlockSpec(memory_space=pltpu.VMEM),
        compiler_params=PARAMS,
        name="project",
    )(side[None], attended, lax.ppermute(attended, "head", swap_side), out_weight, other_weight)
    sides = [list(range(k, head_size, 2)) for k in range(2)]
    shares = lax.all_to_all(shares, "head", 0, 0, axis_index_groups=sides, tiled=True)
    return jnp.sum(shares.astype(jnp.float32), axis=0).astype(jnp.bfloat16)


def solution(mesh):
    return jax.shard_map(
        functools.partial(per_device, mesh.shape["seq"], mesh.shape["head"]),
        mesh=mesh,
        in_specs=(
            P("seq", "head"),
            P("seq", "head"),
            P("seq", "head"),
            P("seq", None),
            P(),
            P("head", None),
        ),
        out_specs=P("seq", "head"),
        check_vma=False,
    )
```

```python
import functools
import math

import jax
import jax.numpy as jnp
from jax import lax
from jax.experimental import pallas as pl
from jax.experimental.pallas import tpu as pltpu
from jax.sharding import PartitionSpec as P

HD = 128
TILE = 256
GROUP = 4
PART_ROWS = 16
LOWEST = -1e30
LOG2E = math.log2(math.e)


def pack_part(ref, index, outs, sums):
    heads = len(outs)
    for h in range(heads):
        ref[index, h * HD:(h + 1) * HD, :] = outs[h].astype(jnp.bfloat16)
    rows = jnp.concatenate(sums + [jnp.zeros((8 - heads, TILE), jnp.float32)], axis=0)
    high = rows.astype(jnp.bfloat16).astype(jnp.float32)
    middle = (rows - high).astype(jnp.bfloat16).astype(jnp.float32)
    low = rows - high - middle
    base = heads * HD
    ref[index, base:base + 16, :] = jnp.concatenate([high, middle], axis=0).astype(jnp.bfloat16)
    ref[index, base + 16:base + 32, :] = jnp.concatenate([low, jnp.zeros_like(low)], axis=0).astype(jnp.bfloat16)


def unpack_sums(ref, index, heads):
    base = heads * HD
    block = ref[index, base:base + 16, :].astype(jnp.float32)
    last = ref[index, base + 16:base + 32, :].astype(jnp.float32)
    return block[0:8] + block[8:16] + last[0:8]


def merged(mine_ref, mine_sum_ref, mine, other_ref, other, heads):
    others = unpack_sums(other_ref, other, heads)
    outs, sums = [], []
    for h in range(heads):
        rows = slice(h * HD, (h + 1) * HD)
        own_sum = mine_sum_ref[mine, h:h + 1, :]
        other_sum = others[h:h + 1]
        top = jnp.maximum(own_sum, other_sum)
        own_weight = jnp.exp2(own_sum - top)
        other_weight = jnp.exp2(other_sum - top)
        total = own_weight + other_weight
        outs.append(
            mine_ref[mine, rows, :] * (own_weight / total)
            + other_ref[other, rows, :].astype(jnp.float32) * (other_weight / total)
        )
        sums.append(top + jnp.log2(total))
    return outs, sums


def load_shards(need_ref, first, shards, k_ref, vt_ref):
    for j, (key, value) in enumerate(shards):
        wanted = need_ref[0, first + j]
        for t in range(1, need_ref.shape[0]):
            wanted = wanted + need_ref[t, first + j]

        @pl.when(wanted > 0)
        def _():
            k_ref[j] = key[...]
            for h in range(vt_ref.shape[1]):
                vt_ref[j, h] = value[:, h * HD:(h + 1) * HD].T


def visit_shards(factor, need_ref, first, count, q_ref, k_ref, vt_ref, state):
    acc_ref, peak_ref, total_ref = state
    heads = vt_ref.shape[1]

    def take(t, picks):
        def scores_of(h):
            cols = slice(h * HD, (h + 1) * HD)
            return [
                lax.dot_general(
                    k_ref[j, :, cols],
                    q_ref[t, :, cols],
                    (((1,), (1,)), ((), ())),
                    preferred_element_type=jnp.float32,
                )
                for j in picks
            ]

        following = scores_of(0)
        for h in range(heads):
            scores = following
            if h + 1 < heads:
                following = scores_of(h + 1)
            row = t * heads + h
            old = peak_ref[row]
            tops = [jnp.max(part, axis=0, keepdims=True) for part in scores]
            peak = jnp.maximum(old, functools.reduce(jnp.maximum, tops) * factor)
            weights = [jnp.exp2(part * factor - peak) for part in scores]
            shrink = jnp.exp2(old - peak)
            sums = [jnp.sum(w, axis=0, keepdims=True) for w in weights]
            dots = [
                jnp.dot(vt_ref[j, h], w.astype(jnp.bfloat16), preferred_element_type=jnp.float32)
                for j, w in zip(picks, weights)
            ]
            peak_ref[row] = peak
            total_ref[row] = total_ref[row] * shrink + sum(sums[1:], sums[0])
            acc_ref[row] = acc_ref[row] * shrink + sum(dots[1:], dots[0])

    def visit(t, carry):
        picks = [jnp.int32(0)] * count
        seen = jnp.int32(0)
        for j in range(count):
            wanted = need_ref[t, first + j]
            for i in range(j + 1):
                picks[i] = jnp.where((wanted > 0) & (seen == i), j, picks[i])
            seen = seen + wanted

        @pl.when(seen >= 3)
        def _():
            take(t, picks[:3])

        @pl.when((seen == 2) | (seen == 5))
        def _():
            take(t, [jnp.where(seen == 5, late, early) for late, early in zip(picks[-2:], picks[:2])])

        @pl.when((seen == 1) | (seen == 4))
        def _():
            take(t, [jnp.where(seen == 4, picks[min(3, count - 1)], picks[0])])

        return carry

    lax.fori_loop(0, q_ref.shape[0], visit, 0)


def list_wanted(seq_size, order, place_ref, text_ref, q_refs, need_ref):
    slots = [lax.rem(place_ref[0] + (GROUP * plane + seq_size), seq_size) for plane in order]
    for t, q_ref in enumerate(q_refs):
        row = q_ref[TILE:TILE + PART_ROWS, 0:HD].astype(jnp.float32)
        bits = jnp.zeros_like(row)
        for j, slot in enumerate(slots):
            bits = bits + jnp.where(row == slot.astype(jnp.float32), float(1 << j), 0.0)
        code = jnp.sum(bits).astype(jnp.int32)
        for j, slot in enumerate(slots):
            wanted = (code >> j) & 1
            for i in range(text_ref.shape[0]):
                wanted = jnp.where(slot == text_ref[i], 1, wanted)
            need_ref[t, j] = wanted


def near_kernel(factor, seq_size, order, place_ref, text_ref, *refs):
    q_refs, (k_own, v_own, k_low, k_high, v_low, v_high) = refs[:GROUP], refs[GROUP:GROUP + 6]
    need_ref, stacked_ref, acc_ref, peak_ref, total_ref, k_ref, vt_ref = refs[GROUP + 6:]
    list_wanted(seq_size, order, place_ref, text_ref, q_refs, need_ref)
    acc_ref[...] = jnp.zeros_like(acc_ref)
    peak_ref[...] = jnp.full_like(peak_ref, LOWEST)
    total_ref[...] = jnp.zeros_like(total_ref)
    for t, q_ref in enumerate(q_refs):
        stacked_ref[t] = q_ref[0:TILE, :]
    shards = [(k_own, v_own), (k_low, v_low), (k_high, v_high)]
    load_shards(need_ref, 0, shards, k_ref, vt_ref)
    visit_shards(factor, need_ref, 0, 3, stacked_ref, k_ref, vt_ref, (acc_ref, peak_ref, total_ref))


def far_kernel(factor, first, count, need_ref, stacked_ref, *refs):
    shards = list(zip(refs[:count], refs[count:2 * count]))
    held = refs[2 * count:2 * count + 3]
    keep_ref, keep_sum_ref, send_ref, *state, k_ref, vt_ref = refs[2 * count + 3:]
    heads = vt_ref.shape[1]
    for source, target in zip(held, state):
        target[...] = source[...]
    load_shards(need_ref, first, shards, k_ref, vt_ref)
    visit_shards(factor, need_ref, first, count, stacked_ref, k_ref, vt_ref, state)
    acc_ref, peak_ref, total_ref = state
    for t in range(GROUP):
        outs, sums = [], []
        for h in range(heads):
            row = t * heads + h
            total = total_ref[row]
            present = total > 0.0
            safe = jnp.where(present, total, 1.0)
            outs.append(acc_ref[row] * (1.0 / safe))
            sums.append(jnp.where(present, peak_ref[row] + jnp.log2(safe), LOWEST))
        if t % 2:
            pack_part(send_ref, t // 2, outs, sums)
        else:
            for h in range(heads):
                keep_ref[t // 2, h * HD:(h + 1) * HD, :] = outs[h]
                keep_sum_ref[t // 2, h:h + 1, :] = sums[h]


def merge_kernel(mine_ref, mine_sum_ref, other_ref, keep_ref, keep_sum_ref, send_ref):
    heads = mine_ref.shape[1] // HD
    outs, sums = merged(mine_ref, mine_sum_ref, 1, other_ref, 1, heads)
    pack_part(send_ref, 0, outs, sums)
    outs, sums = merged(mine_ref, mine_sum_ref, 0, other_ref, 0, heads)
    for h in range(heads):
        keep_ref[0, h * HD:(h + 1) * HD, :] = outs[h]
        keep_sum_ref[0, h:h + 1, :] = sums[h]


def finish_kernel(mine_ref, mine_sum_ref, other_ref, out_ref):
    heads = mine_ref.shape[1] // HD
    outs, _ = merged(mine_ref, mine_sum_ref, 0, other_ref, 0, heads)
    for h in range(heads):
        out_ref[:, h * HD:(h + 1) * HD] = outs[h].T.astype(jnp.bfloat16)


def project_kernel(side_ref, mine_ref, other_ref, weight_ref, other_weight_ref, out_ref):
    shares, _, width = out_ref.shape
    for j in range(shares):
        block = pl.ds(pl.multiple_of((2 * j + side_ref[0]) * width, HD), width)
        mixed = jnp.dot(mine_ref[...], weight_ref[:, block], preferred_element_type=jnp.float32)
        mixed = mixed + jnp.dot(other_ref[...], other_weight_ref[:, block], preferred_element_type=jnp.float32)
        out_ref[j] = mixed.astype(jnp.bfloat16)


def vmem_specs(count):
    return [pl.BlockSpec(memory_space=pltpu.VMEM)] * count


def attend_cost(blocks):
    return pl.CostEstimate(
        flops=blocks * 4 * TILE * TILE * HD, bytes_accessed=4 << 20, transcendentals=blocks * TILE * TILE
    )


PARAMS = pltpu.CompilerParams(vmem_limit_bytes=16 * 1024 * 1024)


def per_device(seq_size, head_size, queries, key_states, value_states, block_list, text_slots, out_weight):
    width = queries.shape[1]
    heads = width // HD
    planes = seq_size // GROUP
    me = lax.axis_index("seq")
    up = [(s, (s + GROUP) % seq_size) for s in range(seq_size)]
    down = [(s, (s - GROUP) % seq_size) for s in range(seq_size)]

    k_up, k_down, v_up, v_down = [key_states], [key_states], [value_states], [value_states]
    half = planes // 2
    for step in range(half):
        k_up.append(lax.ppermute(k_up[-1], "seq", up))
        if step < half - 1:
            k_down.append(lax.ppermute(k_down[-1], "seq", down))
            v_up.append(lax.ppermute(v_up[-1], "seq", up))
        v_down.append(lax.ppermute(v_down[-1], "seq", down))

    swap_side = [(h, h ^ 1) for h in range(head_size)]
    side = lax.axis_index("head") % 2
    other_weight = lax.ppermute(out_weight, "head", swap_side)

    listed = jnp.pad(
        block_list, ((0, PART_ROWS - 1), (0, width - block_list.shape[1])), constant_values=-1
    )
    packed = jnp.concatenate([queries, listed.astype(jnp.bfloat16)], axis=0)
    tiles = [packed] + [
        lax.ppermute(packed, "seq", [(s, s ^ k) for s in range(seq_size)]) for k in range(1, GROUP)
    ]
    order = (0, -1, 1, -3, 3, 4, -2, 2)

    rows = GROUP * heads
    state = (
        jax.ShapeDtypeStruct((rows, HD, TILE), jnp.float32),
        jax.ShapeDtypeStruct((rows, 1, TILE), jnp.float32),
        jax.ShapeDtypeStruct((rows, 1, TILE), jnp.float32),
    )
    factor = LOG2E / math.sqrt(HD)
    smem = [pl.BlockSpec(memory_space=pltpu.SMEM)]

    def scratch(count):
        return [
            pltpu.VMEM((count, TILE, width), jnp.bfloat16),
            pltpu.VMEM((count, heads, HD, TILE), jnp.bfloat16),
        ]

    need, stacked, *held = pl.pallas_call(
        functools.partial(near_kernel, factor, seq_size, order),
        out_shape=(
            jax.ShapeDtypeStruct((GROUP, len(order)), jnp.int32),
            jax.ShapeDtypeStruct((GROUP, TILE, width), jnp.bfloat16),
        )
        + state,
        in_specs=smem * 2 + vmem_specs(GROUP + 6),
        out_specs=tuple(smem + vmem_specs(4)),
        scratch_shapes=scratch(3),
        compiler_params=PARAMS,
        cost_estimate=attend_cost(27),
        name="attend_near",
    )(me[None], text_slots, *tiles, key_states, value_states, k_up[1], k_down[1], v_up[1], v_down[1])
    far = [(k_up[3], v_up[3]), (k_down[3], v_down[3]), (k_up[4], v_down[4]), (k_up[2], v_up[2]), (k_down[2], v_down[2])]
    keep, keep_sum, send = pl.pallas_call(
        functools.partial(far_kernel, factor, 3, len(far)),
        out_shape=(
            jax.ShapeDtypeStruct((2, width, TILE), jnp.float32),
            jax.ShapeDtypeStruct((2, 8, TILE), jnp.float32),
            jax.ShapeDtypeStruct((2, width + 2 * PART_ROWS, TILE), jnp.bfloat16),
        ),
        in_specs=smem + vmem_specs(1 + 2 * len(far) + 3),
        out_specs=tuple(vmem_specs(3)),
        scratch_shapes=[pltpu.VMEM(s.shape, s.dtype) for s in state] + scratch(len(far)),
        compiler_params=PARAMS,
        cost_estimate=attend_cost(27),
        name="attend_far",
    )(need, stacked, *[k for k, _ in far], *[v for _, v in far], *held)

    other = lax.ppermute(send, "seq", [(s, s ^ 1) for s in range(seq_size)])
    keep, keep_sum, send = pl.pallas_call(
        merge_kernel,
        out_shape=(
            jax.ShapeDtypeStruct((1, width, TILE), jnp.float32),
            jax.ShapeDtypeStruct((1, 8, TILE), jnp.float32),
            jax.ShapeDtypeStruct((1, width + 2 * PART_ROWS, TILE), jnp.bfloat16),
        ),
        in_specs=vmem_specs(3),
        out_specs=tuple(vmem_specs(3)),
        compiler_params=PARAMS,
        name="merge",
    )(keep, keep_sum, other)
    other = lax.ppermute(send, "seq", [(s, s ^ 2) for s in range(seq_size)])
    attended = pl.pallas_call(
        finish_kernel,
        out_shape=jax.ShapeDtypeStruct((TILE, width), jnp.bfloat16),
        in_specs=vmem_specs(3),
        out_specs=pl.BlockSpec(memory_space=pltpu.VMEM),
        compiler_params=PARAMS,
        name="finish",
    )(keep, keep_sum, other)
    shares = pl.pallas_call(
        project_kernel,
        out_shape=jax.ShapeDtypeStruct((head_size // 2, TILE, width), jnp.bfloat16),
        in_specs=smem + vmem_specs(4),
        out_specs=pl.BlockSpec(memory_space=pltpu.VMEM),
        compiler_params=PARAMS,
        name="project",
    )(side[None], attended, lax.ppermute(attended, "head", swap_side), out_weight, other_weight)
    sides = [list(range(k, head_size, 2)) for k in range(2)]
    shares = lax.all_to_all(shares, "head", 0, 0, axis_index_groups=sides, tiled=True)
    return jnp.sum(shares.astype(jnp.float32), axis=0).astype(jnp.bfloat16)


def solution(mesh):
    return jax.shard_map(
        functools.partial(per_device, mesh.shape["seq"], mesh.shape["head"]),
        mesh=mesh,
        in_specs=(
            P("seq", "head"),
            P("seq", "head"),
            P("seq", "head"),
            P("seq", None),
            P(),
            P("head", None),
        ),
        out_specs=P("seq", "head"),
        check_vma=False,
    )
```

```python
import functools
import math

import jax
import jax.numpy as jnp
from jax import lax
from jax.experimental import pallas as pl
from jax.experimental.pallas import tpu as pltpu
from jax.sharding import PartitionSpec as P

HD = 128
TILE = 256
GROUP = 4
PART_ROWS = 16
LOWEST = -1e30
LOG2E = math.log2(math.e)


def pack_part(ref, index, outs, sums):
    heads = len(outs)
    for h in range(heads):
        ref[index, h * HD:(h + 1) * HD, :] = outs[h].astype(jnp.bfloat16)
    rows = jnp.concatenate(sums + [jnp.zeros((8 - heads, TILE), jnp.float32)], axis=0)
    high = rows.astype(jnp.bfloat16).astype(jnp.float32)
    middle = (rows - high).astype(jnp.bfloat16).astype(jnp.float32)
    low = rows - high - middle
    base = heads * HD
    ref[index, base:base + 16, :] = jnp.concatenate([high, middle], axis=0).astype(jnp.bfloat16)
    ref[index, base + 16:base + 32, :] = jnp.concatenate([low, jnp.zeros_like(low)], axis=0).astype(jnp.bfloat16)


def unpack_sums(ref, index, heads):
    base = heads * HD
    block = ref[index, base:base + 16, :].astype(jnp.float32)
    last = ref[index, base + 16:base + 32, :].astype(jnp.float32)
    return block[0:8] + block[8:16] + last[0:8]


def merged(mine_ref, mine_sum_ref, mine, other_ref, other, heads):
    others = unpack_sums(other_ref, other, heads)
    outs, sums = [], []
    for h in range(heads):
        rows = slice(h * HD, (h + 1) * HD)
        own_sum = mine_sum_ref[mine, h:h + 1, :]
        other_sum = others[h:h + 1]
        top = jnp.maximum(own_sum, other_sum)
        own_weight = jnp.exp2(own_sum - top)
        other_weight = jnp.exp2(other_sum - top)
        total = own_weight + other_weight
        outs.append(
            mine_ref[mine, rows, :] * (own_weight / total)
            + other_ref[other, rows, :].astype(jnp.float32) * (other_weight / total)
        )
        sums.append(top + jnp.log2(total))
    return outs, sums


def load_shards(need_ref, first, shards, k_ref, vt_ref):
    for j, (key, value) in enumerate(shards):
        wanted = need_ref[0, first + j]
        for t in range(1, need_ref.shape[0]):
            wanted = wanted + need_ref[t, first + j]

        @pl.when(wanted > 0)
        def _():
            k_ref[j] = key[...]
            for h in range(vt_ref.shape[1]):
                vt_ref[j, h] = value[:, h * HD:(h + 1) * HD].T


def visit_shards(factor, need_ref, first, count, q_ref, k_ref, vt_ref, state):
    acc_ref, peak_ref, total_ref = state
    heads = vt_ref.shape[1]

    def take(t, picks):
        def scores_of(h):
            cols = slice(h * HD, (h + 1) * HD)
            return [
                lax.dot_general(
                    k_ref[j, :, cols],
                    q_ref[t, :, cols],
                    (((1,), (1,)), ((), ())),
                    preferred_element_type=jnp.float32,
                )
                for j in picks
            ]

        following = scores_of(0)
        for h in range(heads):
            scores = following
            if h + 1 < heads:
                following = scores_of(h + 1)
            row = t * heads + h
            old = peak_ref[row]
            tops = [jnp.max(part, axis=0, keepdims=True) for part in scores]
            peak = jnp.maximum(old, functools.reduce(jnp.maximum, tops) * factor)
            weights = [jnp.exp2(part * factor - peak) for part in scores]
            shrink = jnp.exp2(old - peak)
            sums = [jnp.sum(w, axis=0, keepdims=True) for w in weights]
            dots = [
                jnp.dot(vt_ref[j, h], w.astype(jnp.bfloat16), preferred_element_type=jnp.float32)
                for j, w in zip(picks, weights)
            ]
            peak_ref[row] = peak
            total_ref[row] = total_ref[row] * shrink + sum(sums[1:], sums[0])
            acc_ref[row] = acc_ref[row] * shrink + sum(dots[1:], dots[0])

    def visit(t, carry):
        picks = [jnp.int32(0)] * count
        seen = jnp.int32(0)
        for j in range(count):
            wanted = need_ref[t, first + j]
            for i in range(j + 1):
                picks[i] = jnp.where((wanted > 0) & (seen == i), j, picks[i])
            seen = seen + wanted

        @pl.when(seen >= 3)
        def _():
            take(t, picks[:3])

        @pl.when((seen == 2) | (seen == 5))
        def _():
            take(t, [jnp.where(seen == 5, late, early) for late, early in zip(picks[-2:], picks[:2])])

        @pl.when((seen == 1) | (seen == 4))
        def _():
            take(t, [jnp.where(seen == 4, picks[min(3, count - 1)], picks[0])])

        return carry

    lax.fori_loop(0, q_ref.shape[0], visit, 0)


def list_wanted(seq_size, order, text_ref, q_refs, need_ref):
    me = lax.axis_index("seq")
    slots = [lax.rem(me + (GROUP * plane + seq_size), seq_size) for plane in order]
    for t, q_ref in enumerate(q_refs):
        row = q_ref[TILE:TILE + PART_ROWS, 0:HD].astype(jnp.float32)
        bits = jnp.zeros_like(row)
        for j, slot in enumerate(slots):
            bits = bits + jnp.where(row == slot.astype(jnp.float32), float(1 << j), 0.0)
        code = jnp.sum(bits).astype(jnp.int32)
        for j, slot in enumerate(slots):
            wanted = (code >> j) & 1
            for i in range(text_ref.shape[0]):
                wanted = jnp.where(slot == text_ref[i], 1, wanted)
            need_ref[t, j] = wanted


def near_kernel(factor, seq_size, order, text_ref, *refs):
    q_refs, (k_own, v_own, k_low, k_high, v_low, v_high) = refs[:GROUP], refs[GROUP:GROUP + 6]
    need_ref, stacked_ref, acc_ref, peak_ref, total_ref, k_ref, vt_ref = refs[GROUP + 6:]
    list_wanted(seq_size, order, text_ref, q_refs, need_ref)
    acc_ref[...] = jnp.zeros_like(acc_ref)
    peak_ref[...] = jnp.full_like(peak_ref, LOWEST)
    total_ref[...] = jnp.zeros_like(total_ref)
    for t, q_ref in enumerate(q_refs):
        stacked_ref[t] = q_ref[0:TILE, :]
    shards = [(k_own, v_own), (k_low, v_low), (k_high, v_high)]
    load_shards(need_ref, 0, shards, k_ref, vt_ref)
    visit_shards(factor, need_ref, 0, 3, stacked_ref, k_ref, vt_ref, (acc_ref, peak_ref, total_ref))


def far_kernel(factor, first, count, need_ref, stacked_ref, *refs):
    shards = list(zip(refs[:count], refs[count:2 * count]))
    held = refs[2 * count:2 * count + 3]
    keep_ref, keep_sum_ref, send_ref, *state, k_ref, vt_ref = refs[2 * count + 3:]
    heads = vt_ref.shape[1]
    for source, target in zip(held, state):
        target[...] = source[...]
    load_shards(need_ref, first, shards, k_ref, vt_ref)
    visit_shards(factor, need_ref, first, count, stacked_ref, k_ref, vt_ref, state)
    acc_ref, peak_ref, total_ref = state
    for t in range(GROUP):
        outs, sums = [], []
        for h in range(heads):
            row = t * heads + h
            total = total_ref[row]
            present = total > 0.0
            safe = jnp.where(present, total, 1.0)
            outs.append(acc_ref[row] * (1.0 / safe))
            sums.append(jnp.where(present, peak_ref[row] + jnp.log2(safe), LOWEST))
        if t % 2:
            pack_part(send_ref, t // 2, outs, sums)
        else:
            for h in range(heads):
                keep_ref[t // 2, h * HD:(h + 1) * HD, :] = outs[h]
                keep_sum_ref[t // 2, h:h + 1, :] = sums[h]


def merge_kernel(mine_ref, mine_sum_ref, other_ref, keep_ref, keep_sum_ref, send_ref):
    heads = mine_ref.shape[1] // HD
    outs, sums = merged(mine_ref, mine_sum_ref, 1, other_ref, 1, heads)
    pack_part(send_ref, 0, outs, sums)
    outs, sums = merged(mine_ref, mine_sum_ref, 0, other_ref, 0, heads)
    for h in range(heads):
        keep_ref[0, h * HD:(h + 1) * HD, :] = outs[h]
        keep_sum_ref[0, h:h + 1, :] = sums[h]


def finish_kernel(mine_ref, mine_sum_ref, other_ref, out_ref):
    heads = mine_ref.shape[1] // HD
    outs, _ = merged(mine_ref, mine_sum_ref, 0, other_ref, 0, heads)
    for h in range(heads):
        out_ref[:, h * HD:(h + 1) * HD] = outs[h].T.astype(jnp.bfloat16)


def pick_kernel(weight_ref, out_ref):
    width = weight_ref.shape[0]
    side = lax.rem(lax.axis_index("head"), 2)
    for j in range(out_ref.shape[1] // width):
        begin = pl.multiple_of((2 * j + 1 - side) * width, HD)
        out_ref[:, j * width:(j + 1) * width] = weight_ref[:, pl.ds(begin, width)]


def project_kernel(mine_ref, other_ref, weight_ref, other_weight_ref, out_ref):
    shares, _, width = out_ref.shape
    side = lax.rem(lax.axis_index("head"), 2)
    for j in range(shares):
        begin = pl.multiple_of((2 * j + side) * width, HD)
        mixed = jnp.dot(mine_ref[...], weight_ref[:, pl.ds(begin, width)], preferred_element_type=jnp.float32)
        mixed = mixed + jnp.dot(
            other_ref[...], other_weight_ref[:, j * width:(j + 1) * width], preferred_element_type=jnp.float32
        )
        out_ref[j] = mixed.astype(jnp.bfloat16)


def vmem_specs(count):
    return [pl.BlockSpec(memory_space=pltpu.VMEM)] * count


def attend_cost(blocks):
    return pl.CostEstimate(
        flops=blocks * 4 * TILE * TILE * HD, bytes_accessed=4 << 20, transcendentals=blocks * TILE * TILE
    )


PARAMS = pltpu.CompilerParams(vmem_limit_bytes=16 * 1024 * 1024)


def per_device(seq_size, head_size, queries, key_states, value_states, block_list, text_slots, out_weight):
    width = queries.shape[1]
    heads = width // HD
    planes = seq_size // GROUP
    up = [(s, (s + GROUP) % seq_size) for s in range(seq_size)]
    down = [(s, (s - GROUP) % seq_size) for s in range(seq_size)]

    k_up, k_down, v_up, v_down = [key_states], [key_states], [value_states], [value_states]
    half = planes // 2
    for step in range(half):
        k_up.append(lax.ppermute(k_up[-1], "seq", up))
        if step < half - 1:
            k_down.append(lax.ppermute(k_down[-1], "seq", down))
            v_up.append(lax.ppermute(v_up[-1], "seq", up))
        v_down.append(lax.ppermute(v_down[-1], "seq", down))

    picked = pl.pallas_call(
        pick_kernel,
        out_shape=jax.ShapeDtypeStruct((width, head_size // 2 * width), out_weight.dtype),
        in_specs=vmem_specs(1),
        out_specs=pl.BlockSpec(memory_space=pltpu.VMEM),
        compiler_params=PARAMS,
        name="pick",
    )(out_weight)
    other_weight = lax.ppermute(picked, "head", [(h, h ^ 1) for h in range(head_size)])

    listed = jnp.pad(
        block_list, ((0, PART_ROWS - 1), (0, width - block_list.shape[1])), constant_values=-1
    )
    packed = jnp.concatenate([queries, listed.astype(jnp.bfloat16)], axis=0)
    tiles = [packed] + [
        lax.ppermute(packed, "seq", [(s, s ^ k) for s in range(seq_size)]) for k in range(1, GROUP)
    ]
    order = (0, -1, 1, -3, 3, 4, -2, 2)

    rows = GROUP * heads
    state = (
        jax.ShapeDtypeStruct((rows, HD, TILE), jnp.float32),
        jax.ShapeDtypeStruct((rows, 1, TILE), jnp.float32),
        jax.ShapeDtypeStruct((rows, 1, TILE), jnp.float32),
    )
    factor = LOG2E / math.sqrt(HD)
    smem = [pl.BlockSpec(memory_space=pltpu.SMEM)]

    def scratch(count):
        return [
            pltpu.VMEM((count, TILE, width), jnp.bfloat16),
            pltpu.VMEM((count, heads, HD, TILE), jnp.bfloat16),
        ]

    need, stacked, *held = pl.pallas_call(
        functools.partial(near_kernel, factor, seq_size, order),
        out_shape=(
            jax.ShapeDtypeStruct((GROUP, len(order)), jnp.int32),
            jax.ShapeDtypeStruct((GROUP, TILE, width), jnp.bfloat16),
        )
        + state,
        in_specs=smem + vmem_specs(GROUP + 6),
        out_specs=tuple(smem + vmem_specs(4)),
        scratch_shapes=scratch(3),
        compiler_params=PARAMS,
        cost_estimate=attend_cost(27),
        name="attend_near",
    )(text_slots, *tiles, key_states, value_states, k_up[1], k_down[1], v_up[1], v_down[1])
    far = [(k_up[3], v_up[3]), (k_down[3], v_down[3]), (k_up[4], v_down[4]), (k_up[2], v_up[2]), (k_down[2], v_down[2])]
    keep, keep_sum, send = pl.pallas_call(
        functools.partial(far_kernel, factor, 3, len(far)),
        out_shape=(
            jax.ShapeDtypeStruct((2, width, TILE), jnp.float32),
            jax.ShapeDtypeStruct((2, 8, TILE), jnp.float32),
            jax.ShapeDtypeStruct((2, width + 2 * PART_ROWS, TILE), jnp.bfloat16),
        ),
        in_specs=smem + vmem_specs(1 + 2 * len(far) + 3),
        out_specs=tuple(vmem_specs(3)),
        scratch_shapes=[pltpu.VMEM(s.shape, s.dtype) for s in state] + scratch(len(far)),
        compiler_params=PARAMS,
        cost_estimate=attend_cost(27),
        name="attend_far",
    )(need, stacked, *[k for k, _ in far], *[v for _, v in far], *held)

    other = lax.ppermute(send, "seq", [(s, s ^ 1) for s in range(seq_size)])
    keep, keep_sum, send = pl.pallas_call(
        merge_kernel,
        out_shape=(
            jax.ShapeDtypeStruct((1, width, TILE), jnp.float32),
            jax.ShapeDtypeStruct((1, 8, TILE), jnp.float32),
            jax.ShapeDtypeStruct((1, width + 2 * PART_ROWS, TILE), jnp.bfloat16),
        ),
        in_specs=vmem_specs(3),
        out_specs=tuple(vmem_specs(3)),
        compiler_params=PARAMS,
        name="merge",
    )(keep, keep_sum, other)
    other = lax.ppermute(send, "seq", [(s, s ^ 2) for s in range(seq_size)])
    attended = pl.pallas_call(
        finish_kernel,
        out_shape=jax.ShapeDtypeStruct((TILE, width), jnp.bfloat16),
        in_specs=vmem_specs(3),
        out_specs=pl.BlockSpec(memory_space=pltpu.VMEM),
        compiler_params=PARAMS,
        name="finish",
    )(keep, keep_sum, other)
    swap_side = [(h, h ^ 1) for h in range(head_size)]
    shares = pl.pallas_call(
        project_kernel,
        out_shape=jax.ShapeDtypeStruct((head_size // 2, TILE, width), jnp.bfloat16),
        in_specs=vmem_specs(4),
        out_specs=pl.BlockSpec(memory_space=pltpu.VMEM),
        compiler_params=PARAMS,
        name="project",
    )(attended, lax.ppermute(attended, "head", swap_side), out_weight, other_weight)
    sides = [list(range(k, head_size, 2)) for k in range(2)]
    shares = lax.all_to_all(shares, "head", 0, 0, axis_index_groups=sides, tiled=True)
    return jnp.sum(shares.astype(jnp.float32), axis=0).astype(jnp.bfloat16)


def solution(mesh):
    return jax.shard_map(
        functools.partial(per_device, mesh.shape["seq"], mesh.shape["head"]),
        mesh=mesh,
        in_specs=(
            P("seq", "head"),
            P("seq", "head"),
            P("seq", "head"),
            P("seq", None),
            P(),
            P("head", None),
        ),
        out_specs=P("seq", "head"),
        check_vma=False,
    )
```

```python
import functools
import math

import jax
import jax.numpy as jnp
from jax import lax
from jax.experimental import pallas as pl
from jax.experimental.pallas import tpu as pltpu
from jax.sharding import PartitionSpec as P

HD = 128
TILE = 256
GROUP = 4
PART_ROWS = 16
LOWEST = -1e30
LOG2E = math.log2(math.e)


def pack_part(ref, index, outs, sums):
    heads = len(outs)
    for h in range(heads):
        ref[index, h * HD:(h + 1) * HD, :] = outs[h].astype(jnp.bfloat16)
    rows = jnp.concatenate(sums + [jnp.zeros((8 - heads, TILE), jnp.float32)], axis=0)
    high = rows.astype(jnp.bfloat16).astype(jnp.float32)
    middle = (rows - high).astype(jnp.bfloat16).astype(jnp.float32)
    low = rows - high - middle
    base = heads * HD
    ref[index, base:base + 16, :] = jnp.concatenate([high, middle], axis=0).astype(jnp.bfloat16)
    ref[index, base + 16:base + 32, :] = jnp.concatenate([low, jnp.zeros_like(low)], axis=0).astype(jnp.bfloat16)


def unpack_sums(ref, index, heads):
    base = heads * HD
    block = ref[index, base:base + 16, :].astype(jnp.float32)
    last = ref[index, base + 16:base + 32, :].astype(jnp.float32)
    return block[0:8] + block[8:16] + last[0:8]


def merged(mine_ref, mine_sum_ref, mine, other_ref, other, heads):
    others = unpack_sums(other_ref, other, heads)
    outs, sums = [], []
    for h in range(heads):
        rows = slice(h * HD, (h + 1) * HD)
        own_sum = mine_sum_ref[mine, h:h + 1, :]
        other_sum = others[h:h + 1]
        top = jnp.maximum(own_sum, other_sum)
        own_weight = jnp.exp2(own_sum - top)
        other_weight = jnp.exp2(other_sum - top)
        total = own_weight + other_weight
        outs.append(
            mine_ref[mine, rows, :] * (own_weight / total)
            + other_ref[other, rows, :].astype(jnp.float32) * (other_weight / total)
        )
        sums.append(top + jnp.log2(total))
    return outs, sums


def load_shards(need_ref, first, shards, k_ref, vt_ref):
    for j, (key, value) in enumerate(shards):
        wanted = need_ref[0, first + j]
        for t in range(1, need_ref.shape[0]):
            wanted = wanted + need_ref[t, first + j]

        @pl.when(wanted > 0)
        def _():
            k_ref[j] = key[...]
            for h in range(vt_ref.shape[1]):
                vt_ref[j, h] = value[:, h * HD:(h + 1) * HD].T


def visit_shards(factor, need_ref, first, count, q_ref, k_ref, vt_ref, state):
    acc_ref, peak_ref, total_ref = state
    heads = vt_ref.shape[1]

    def take(t, picks):
        def scores_of(h):
            cols = slice(h * HD, (h + 1) * HD)
            return [
                lax.dot_general(
                    k_ref[j, :, cols],
                    q_ref[t, :, cols],
                    (((1,), (1,)), ((), ())),
                    preferred_element_type=jnp.float32,
                )
                for j in picks
            ]

        following = scores_of(0)
        for h in range(heads):
            scores = following
            if h + 1 < heads:
                following = scores_of(h + 1)
            row = t * heads + h
            old = peak_ref[row]
            tops = [jnp.max(part, axis=0, keepdims=True) for part in scores]
            peak = jnp.maximum(old, functools.reduce(jnp.maximum, tops) * factor)
            weights = [jnp.exp2(part * factor - peak) for part in scores]
            shrink = jnp.exp2(old - peak)
            sums = [jnp.sum(w, axis=0, keepdims=True) for w in weights]
            dots = [
                jnp.dot(vt_ref[j, h], w.astype(jnp.bfloat16), preferred_element_type=jnp.float32)
                for j, w in zip(picks, weights)
            ]
            peak_ref[row] = peak
            total_ref[row] = total_ref[row] * shrink + sum(sums[1:], sums[0])
            acc_ref[row] = acc_ref[row] * shrink + sum(dots[1:], dots[0])

    def visit(t, carry):
        picks = [jnp.int32(0)] * count
        seen = jnp.int32(0)
        for j in range(count):
            wanted = need_ref[t, first + j]
            for i in range(j + 1):
                picks[i] = jnp.where((wanted > 0) & (seen == i), j, picks[i])
            seen = seen + wanted

        @pl.when(seen >= 3)
        def _():
            take(t, picks[:3])

        @pl.when((seen == 2) | (seen == 5))
        def _():
            take(t, [jnp.where(seen == 5, late, early) for late, early in zip(picks[-2:], picks[:2])])

        @pl.when((seen == 1) | (seen == 4))
        def _():
            take(t, [jnp.where(seen == 4, picks[min(3, count - 1)], picks[0])])

        return carry

    lax.fori_loop(0, q_ref.shape[0], visit, 0)


def list_wanted(seq_size, order, text_ref, q_refs, need_ref):
    me = lax.axis_index("seq")
    slots = [lax.rem(me + (GROUP * plane + seq_size), seq_size) for plane in order]
    for t, q_ref in enumerate(q_refs):
        row = q_ref[TILE:TILE + PART_ROWS, 0:HD].astype(jnp.float32)
        bits = jnp.zeros_like(row)
        for j, slot in enumerate(slots):
            bits = bits + jnp.where(row == slot.astype(jnp.float32), float(1 << j), 0.0)
        code = jnp.sum(bits).astype(jnp.int32)
        for j, slot in enumerate(slots):
            wanted = (code >> j) & 1
            for i in range(text_ref.shape[0]):
                wanted = jnp.where(slot == text_ref[i], 1, wanted)
            need_ref[t, j] = wanted


def near_kernel(factor, seq_size, order, text_ref, *refs):
    q_refs, (k_own, v_own, k_low, k_high, v_low, v_high) = refs[:GROUP], refs[GROUP:GROUP + 6]
    need_ref, stacked_ref, acc_ref, peak_ref, total_ref, k_ref, vt_ref = refs[GROUP + 6:]
    list_wanted(seq_size, order, text_ref, q_refs, need_ref)
    acc_ref[...] = jnp.zeros_like(acc_ref)
    peak_ref[...] = jnp.full_like(peak_ref, LOWEST)
    total_ref[...] = jnp.zeros_like(total_ref)
    for t, q_ref in enumerate(q_refs):
        stacked_ref[t] = q_ref[0:TILE, :]
    shards = [(k_own, v_own), (k_low, v_low), (k_high, v_high)]
    load_shards(need_ref, 0, shards, k_ref, vt_ref)
    visit_shards(factor, need_ref, 0, 3, stacked_ref, k_ref, vt_ref, (acc_ref, peak_ref, total_ref))


def far_kernel(factor, first, count, need_ref, stacked_ref, *refs):
    shards = list(zip(refs[:count], refs[count:2 * count]))
    held = refs[2 * count:2 * count + 3]
    keep_ref, keep_sum_ref, send_ref, *state, k_ref, vt_ref = refs[2 * count + 3:]
    heads = vt_ref.shape[1]
    for source, target in zip(held, state):
        target[...] = source[...]
    load_shards(need_ref, first, shards, k_ref, vt_ref)
    visit_shards(factor, need_ref, first, count, stacked_ref, k_ref, vt_ref, state)
    acc_ref, peak_ref, total_ref = state
    for t in range(GROUP):
        outs, sums = [], []
        for h in range(heads):
            row = t * heads + h
            total = total_ref[row]
            present = total > 0.0
            safe = jnp.where(present, total, 1.0)
            outs.append(acc_ref[row] * (1.0 / safe))
            sums.append(jnp.where(present, peak_ref[row] + jnp.log2(safe), LOWEST))
        if t % 2:
            pack_part(send_ref, t // 2, outs, sums)
        else:
            for h in range(heads):
                keep_ref[t // 2, h * HD:(h + 1) * HD, :] = outs[h]
                keep_sum_ref[t // 2, h:h + 1, :] = sums[h]


def merge_kernel(mine_ref, mine_sum_ref, other_ref, keep_ref, keep_sum_ref, send_ref):
    heads = mine_ref.shape[1] // HD
    outs, sums = merged(mine_ref, mine_sum_ref, 1, other_ref, 1, heads)
    pack_part(send_ref, 0, outs, sums)
    outs, sums = merged(mine_ref, mine_sum_ref, 0, other_ref, 0, heads)
    for h in range(heads):
        keep_ref[0, h * HD:(h + 1) * HD, :] = outs[h]
        keep_sum_ref[0, h:h + 1, :] = sums[h]


def finish_kernel(mine_ref, mine_sum_ref, other_ref, out_ref):
    heads = mine_ref.shape[1] // HD
    outs, _ = merged(mine_ref, mine_sum_ref, 0, other_ref, 0, heads)
    for h in range(heads):
        out_ref[:, h * HD:(h + 1) * HD] = outs[h].T.astype(jnp.bfloat16)


def pick_kernel(weight_ref, out_ref):
    width = weight_ref.shape[0]
    count = out_ref.shape[1] // width
    side = lax.rem(lax.axis_index("head"), 2)
    core = lax.rem(lax.axis_index("seq"), 2)
    for j in range(count):
        begin = pl.multiple_of((2 * (core * count + j) + 1 - side) * width, HD)
        out_ref[:, j * width:(j + 1) * width] = weight_ref[:, pl.ds(begin, width)]


def project_kernel(mine_ref, other_ref, weight_ref, half_ref, swapped_ref, out_ref, blocks_ref):
    shares, _, width = out_ref.shape
    side = lax.rem(lax.axis_index("head"), 2)
    core = lax.rem(lax.axis_index("seq"), 2)
    half = half_ref.shape[1]
    blocks_ref[:, pl.ds(pl.multiple_of(core * half, HD), half)] = half_ref[...]
    blocks_ref[:, pl.ds(pl.multiple_of((1 - core) * half, HD), half)] = swapped_ref[...]
    for j in range(shares):
        begin = pl.multiple_of((2 * j + side) * width, HD)
        mixed = jnp.dot(mine_ref[...], weight_ref[:, pl.ds(begin, width)], preferred_element_type=jnp.float32)
        mixed = mixed + jnp.dot(
            other_ref[...], blocks_ref[:, j * width:(j + 1) * width], preferred_element_type=jnp.float32
        )
        out_ref[j] = mixed.astype(jnp.bfloat16)


def vmem_specs(count):
    return [pl.BlockSpec(memory_space=pltpu.VMEM)] * count


def attend_cost(blocks):
    return pl.CostEstimate(
        flops=blocks * 4 * TILE * TILE * HD, bytes_accessed=4 << 20, transcendentals=blocks * TILE * TILE
    )


PARAMS = pltpu.CompilerParams(vmem_limit_bytes=16 * 1024 * 1024)


def per_device(seq_size, head_size, queries, key_states, value_states, block_list, text_slots, out_weight):
    width = queries.shape[1]
    heads = width // HD
    planes = seq_size // GROUP
    up = [(s, (s + GROUP) % seq_size) for s in range(seq_size)]
    down = [(s, (s - GROUP) % seq_size) for s in range(seq_size)]

    k_up, k_down, v_up, v_down = [key_states], [key_states], [value_states], [value_states]
    half = planes // 2
    for step in range(half):
        k_up.append(lax.ppermute(k_up[-1], "seq", up))
        if step < half - 1:
            k_down.append(lax.ppermute(k_down[-1], "seq", down))
            v_up.append(lax.ppermute(v_up[-1], "seq", up))
        v_down.append(lax.ppermute(v_down[-1], "seq", down))

    picked = pl.pallas_call(
        pick_kernel,
        out_shape=jax.ShapeDtypeStruct((width, head_size // 4 * width), out_weight.dtype),
        in_specs=vmem_specs(1),
        out_specs=pl.BlockSpec(memory_space=pltpu.VMEM),
        compiler_params=PARAMS,
        name="pick",
    )(out_weight)
    other_half = lax.ppermute(picked, "head", [(h, h ^ 1) for h in range(head_size)])
    other_swapped = lax.ppermute(other_half, "seq", [(s, s ^ 1) for s in range(seq_size)])

    listed = jnp.pad(
        block_list, ((0, PART_ROWS - 1), (0, width - block_list.shape[1])), constant_values=-1
    )
    packed = jnp.concatenate([queries, listed.astype(jnp.bfloat16)], axis=0)
    tiles = [packed] + [
        lax.ppermute(packed, "seq", [(s, s ^ k) for s in range(seq_size)]) for k in range(1, GROUP)
    ]
    order = (0, -1, 1, -3, 3, 4, -2, 2)

    rows = GROUP * heads
    state = (
        jax.ShapeDtypeStruct((rows, HD, TILE), jnp.float32),
        jax.ShapeDtypeStruct((rows, 1, TILE), jnp.float32),
        jax.ShapeDtypeStruct((rows, 1, TILE), jnp.float32),
    )
    factor = LOG2E / math.sqrt(HD)
    smem = [pl.BlockSpec(memory_space=pltpu.SMEM)]

    def scratch(count):
        return [
            pltpu.VMEM((count, TILE, width), jnp.bfloat16),
            pltpu.VMEM((count, heads, HD, TILE), jnp.bfloat16),
        ]

    need, stacked, *held = pl.pallas_call(
        functools.partial(near_kernel, factor, seq_size, order),
        out_shape=(
            jax.ShapeDtypeStruct((GROUP, len(order)), jnp.int32),
            jax.ShapeDtypeStruct((GROUP, TILE, width), jnp.bfloat16),
        )
        + state,
        in_specs=smem + vmem_specs(GROUP + 6),
        out_specs=tuple(smem + vmem_specs(4)),
        scratch_shapes=scratch(3),
        compiler_params=PARAMS,
        cost_estimate=attend_cost(27),
        name="attend_near",
    )(text_slots, *tiles, key_states, value_states, k_up[1], k_down[1], v_up[1], v_down[1])
    far = [(k_up[3], v_up[3]), (k_down[3], v_down[3]), (k_up[4], v_down[4]), (k_up[2], v_up[2]), (k_down[2], v_down[2])]
    keep, keep_sum, send = pl.pallas_call(
        functools.partial(far_kernel, factor, 3, len(far)),
        out_shape=(
            jax.ShapeDtypeStruct((2, width, TILE), jnp.float32),
            jax.ShapeDtypeStruct((2, 8, TILE), jnp.float32),
            jax.ShapeDtypeStruct((2, width + 2 * PART_ROWS, TILE), jnp.bfloat16),
        ),
        in_specs=smem + vmem_specs(1 + 2 * len(far) + 3),
        out_specs=tuple(vmem_specs(3)),
        scratch_shapes=[pltpu.VMEM(s.shape, s.dtype) for s in state] + scratch(len(far)),
        compiler_params=PARAMS,
        cost_estimate=attend_cost(27),
        name="attend_far",
    )(need, stacked, *[k for k, _ in far], *[v for _, v in far], *held)

    other = lax.ppermute(send, "seq", [(s, s ^ 1) for s in range(seq_size)])
    keep, keep_sum, send = pl.pallas_call(
        merge_kernel,
        out_shape=(
            jax.ShapeDtypeStruct((1, width, TILE), jnp.float32),
            jax.ShapeDtypeStruct((1, 8, TILE), jnp.float32),
            jax.ShapeDtypeStruct((1, width + 2 * PART_ROWS, TILE), jnp.bfloat16),
        ),
        in_specs=vmem_specs(3),
        out_specs=tuple(vmem_specs(3)),
        compiler_params=PARAMS,
        name="merge",
    )(keep, keep_sum, other)
    other = lax.ppermute(send, "seq", [(s, s ^ 2) for s in range(seq_size)])
    attended = pl.pallas_call(
        finish_kernel,
        out_shape=jax.ShapeDtypeStruct((TILE, width), jnp.bfloat16),
        in_specs=vmem_specs(3),
        out_specs=pl.BlockSpec(memory_space=pltpu.VMEM),
        compiler_params=PARAMS,
        name="finish",
    )(keep, keep_sum, other)
    swap_side = [(h, h ^ 1) for h in range(head_size)]
    shares = pl.pallas_call(
        project_kernel,
        out_shape=jax.ShapeDtypeStruct((head_size // 2, TILE, width), jnp.bfloat16),
        in_specs=vmem_specs(5),
        out_specs=pl.BlockSpec(memory_space=pltpu.VMEM),
        scratch_shapes=[pltpu.VMEM((width, head_size // 2 * width), out_weight.dtype)],
        compiler_params=PARAMS,
        name="project",
    )(attended, lax.ppermute(attended, "head", swap_side), out_weight, other_half, other_swapped)
    sides = [list(range(k, head_size, 2)) for k in range(2)]
    shares = lax.all_to_all(shares, "head", 0, 0, axis_index_groups=sides, tiled=True)
    return jnp.sum(shares.astype(jnp.float32), axis=0).astype(jnp.bfloat16)


def solution(mesh):
    return jax.shard_map(
        functools.partial(per_device, mesh.shape["seq"], mesh.shape["head"]),
        mesh=mesh,
        in_specs=(
            P("seq", "head"),
            P("seq", "head"),
            P("seq", "head"),
            P("seq", None),
            P(),
            P("head", None),
        ),
        out_specs=P("seq", "head"),
        check_vma=False,
    )
```

```python
import functools
import math

import jax
import jax.numpy as jnp
from jax import lax
from jax.experimental import pallas as pl
from jax.experimental.pallas import tpu as pltpu
from jax.sharding import PartitionSpec as P

HD = 128
TILE = 256
GROUP = 4
PART_ROWS = 16
LOWEST = -1e30
LOG2E = math.log2(math.e)


def pack_part(ref, index, outs, sums):
    heads = len(outs)
    for h in range(heads):
        ref[index, h * HD:(h + 1) * HD, :] = outs[h].astype(jnp.bfloat16)
    rows = jnp.concatenate(sums + [jnp.zeros((8 - heads, TILE), jnp.float32)], axis=0)
    high = rows.astype(jnp.bfloat16).astype(jnp.float32)
    middle = (rows - high).astype(jnp.bfloat16).astype(jnp.float32)
    low = rows - high - middle
    base = heads * HD
    ref[index, base:base + 16, :] = jnp.concatenate([high, middle], axis=0).astype(jnp.bfloat16)
    ref[index, base + 16:base + 32, :] = jnp.concatenate([low, jnp.zeros_like(low)], axis=0).astype(jnp.bfloat16)


def unpack_sums(ref, index, heads):
    base = heads * HD
    block = ref[index, base:base + 16, :].astype(jnp.float32)
    last = ref[index, base + 16:base + 32, :].astype(jnp.float32)
    return block[0:8] + block[8:16] + last[0:8]


def merged(mine_ref, mine_sum_ref, mine, other_ref, other, heads):
    others = unpack_sums(other_ref, other, heads)
    outs, sums = [], []
    for h in range(heads):
        rows = slice(h * HD, (h + 1) * HD)
        own_sum = mine_sum_ref[mine, h:h + 1, :]
        other_sum = others[h:h + 1]
        top = jnp.maximum(own_sum, other_sum)
        own_weight = jnp.exp2(own_sum - top)
        other_weight = jnp.exp2(other_sum - top)
        total = own_weight + other_weight
        outs.append(
            mine_ref[mine, rows, :] * (own_weight / total)
            + other_ref[other, rows, :].astype(jnp.float32) * (other_weight / total)
        )
        sums.append(top + jnp.log2(total))
    return outs, sums


def load_shards(need_ref, first, shards, k_ref, vt_ref):
    for j, (key, value) in enumerate(shards):
        wanted = need_ref[0, first + j]
        for t in range(1, need_ref.shape[0]):
            wanted = wanted + need_ref[t, first + j]

        @pl.when(wanted > 0)
        def _():
            k_ref[j] = key[...]
            for h in range(vt_ref.shape[1]):
                vt_ref[j, h] = value[:, h * HD:(h + 1) * HD].T


def visit_shards(factor, need_ref, first, count, q_ref, k_ref, vt_ref, state):
    acc_ref, peak_ref, total_ref = state
    heads = vt_ref.shape[1]

    def take(t, picks):
        def scores_of(h):
            cols = slice(h * HD, (h + 1) * HD)
            return [
                lax.dot_general(
                    k_ref[j, :, cols],
                    q_ref[t, :, cols],
                    (((1,), (1,)), ((), ())),
                    preferred_element_type=jnp.float32,
                )
                for j in picks
            ]

        following = scores_of(0)
        for h in range(heads):
            scores = following
            if h + 1 < heads:
                following = scores_of(h + 1)
            row = t * heads + h
            old = peak_ref[row]
            tops = [jnp.max(part, axis=0, keepdims=True) for part in scores]
            peak = jnp.maximum(old, functools.reduce(jnp.maximum, tops) * factor)
            weights = [jnp.exp2(part * factor - peak) for part in scores]
            shrink = jnp.exp2(old - peak)
            sums = [jnp.sum(w, axis=0, keepdims=True) for w in weights]
            dots = [
                jnp.dot(vt_ref[j, h], w.astype(jnp.bfloat16), preferred_element_type=jnp.float32)
                for j, w in zip(picks, weights)
            ]
            peak_ref[row] = peak
            total_ref[row] = total_ref[row] * shrink + sum(sums[1:], sums[0])
            acc_ref[row] = acc_ref[row] * shrink + sum(dots[1:], dots[0])

    def visit(t, carry):
        picks = [jnp.int32(0)] * count
        seen = jnp.int32(0)
        for j in range(count):
            wanted = need_ref[t, first + j]
            for i in range(j + 1):
                picks[i] = jnp.where((wanted > 0) & (seen == i), j, picks[i])
            seen = seen + wanted

        @pl.when(seen >= 3)
        def _():
            take(t, picks[:3])

        @pl.when((seen == 2) | (seen == 5))
        def _():
            take(t, [jnp.where(seen == 5, late, early) for late, early in zip(picks[-2:], picks[:2])])

        @pl.when((seen == 1) | (seen == 4))
        def _():
            take(t, [jnp.where(seen == 4, picks[min(3, count - 1)], picks[0])])

        return carry

    lax.fori_loop(0, q_ref.shape[0], visit, 0)


def list_wanted(seq_size, order, text_ref, q_refs, need_ref):
    me = lax.axis_index("seq")
    slots = [lax.rem(me + (GROUP * plane + seq_size), seq_size) for plane in order]
    for t, q_ref in enumerate(q_refs):
        row = q_ref[TILE:TILE + PART_ROWS, 0:HD].astype(jnp.float32)
        bits = jnp.zeros_like(row)
        for j, slot in enumerate(slots):
            bits = bits + jnp.where(row == slot.astype(jnp.float32), float(1 << j), 0.0)
        code = jnp.sum(bits).astype(jnp.int32)
        for j, slot in enumerate(slots):
            wanted = (code >> j) & 1
            for i in range(text_ref.shape[0]):
                wanted = jnp.where(slot == text_ref[i], 1, wanted)
            need_ref[t, j] = wanted


def near_kernel(factor, seq_size, order, text_ref, *refs):
    q_refs, (k_own, v_own, k_low, k_high, v_low, v_high) = refs[:GROUP], refs[GROUP:GROUP + 6]
    need_ref, stacked_ref, acc_ref, peak_ref, total_ref, k_ref, vt_ref = refs[GROUP + 6:]
    list_wanted(seq_size, order, text_ref, q_refs, need_ref)
    acc_ref[...] = jnp.zeros_like(acc_ref)
    peak_ref[...] = jnp.full_like(peak_ref, LOWEST)
    total_ref[...] = jnp.zeros_like(total_ref)
    for t, q_ref in enumerate(q_refs):
        stacked_ref[t] = q_ref[0:TILE, :]
    shards = [(k_own, v_own), (k_low, v_low), (k_high, v_high)]
    load_shards(need_ref, 0, shards, k_ref, vt_ref)
    visit_shards(factor, need_ref, 0, 3, stacked_ref, k_ref, vt_ref, (acc_ref, peak_ref, total_ref))


def far_kernel(factor, first, count, need_ref, stacked_ref, *refs):
    shards = list(zip(refs[:count], refs[count:2 * count]))
    held = refs[2 * count:2 * count + 3]
    keep_ref, keep_sum_ref, send_ref, *state, k_ref, vt_ref = refs[2 * count + 3:]
    heads = vt_ref.shape[1]
    for source, target in zip(held, state):
        target[...] = source[...]
    load_shards(need_ref, first, shards, k_ref, vt_ref)
    visit_shards(factor, need_ref, first, count, stacked_ref, k_ref, vt_ref, state)
    acc_ref, peak_ref, total_ref = state
    for t in range(GROUP):
        outs, sums = [], []
        for h in range(heads):
            row = t * heads + h
            total = total_ref[row]
            present = total > 0.0
            safe = jnp.where(present, total, 1.0)
            outs.append(acc_ref[row] * (1.0 / safe))
            sums.append(jnp.where(present, peak_ref[row] + jnp.log2(safe), LOWEST))
        if t % 2:
            pack_part(send_ref, t // 2, outs, sums)
        else:
            for h in range(heads):
                keep_ref[t // 2, h * HD:(h + 1) * HD, :] = outs[h]
                keep_sum_ref[t // 2, h:h + 1, :] = sums[h]


def merge_kernel(mine_ref, mine_sum_ref, other_ref, keep_ref, keep_sum_ref, send_ref):
    heads = mine_ref.shape[1] // HD
    outs, sums = merged(mine_ref, mine_sum_ref, 1, other_ref, 1, heads)
    pack_part(send_ref, 0, outs, sums)
    outs, sums = merged(mine_ref, mine_sum_ref, 0, other_ref, 0, heads)
    for h in range(heads):
        keep_ref[0, h * HD:(h + 1) * HD, :] = outs[h]
        keep_sum_ref[0, h:h + 1, :] = sums[h]


def finish_kernel(mine_ref, mine_sum_ref, other_ref, out_ref):
    heads = mine_ref.shape[1] // HD
    outs, _ = merged(mine_ref, mine_sum_ref, 0, other_ref, 0, heads)
    for h in range(heads):
        out_ref[:, h * HD:(h + 1) * HD] = outs[h].T.astype(jnp.bfloat16)


def pick_kernel(weight_ref, out_ref):
    width = weight_ref.shape[0]
    count = out_ref.shape[1] // width
    side = lax.rem(lax.axis_index("head"), 2)
    core = lax.rem(lax.axis_index("seq"), 2)
    for j in range(count):
        begin = pl.multiple_of((2 * (core * count + j) + 1 - side) * width, HD)
        out_ref[:, j * width:(j + 1) * width] = weight_ref[:, pl.ds(begin, width)]


def project_own_kernel(mine_ref, weight_ref, half_ref, swapped_ref, sum_ref, blocks_ref):
    shares, _, width = sum_ref.shape
    side = lax.rem(lax.axis_index("head"), 2)
    core = lax.rem(lax.axis_index("seq"), 2)
    half = half_ref.shape[1]
    blocks_ref[:, pl.ds(pl.multiple_of(core * half, HD), half)] = half_ref[...]
    blocks_ref[:, pl.ds(pl.multiple_of((1 - core) * half, HD), half)] = swapped_ref[...]
    for j in range(shares):
        begin = pl.multiple_of((2 * j + side) * width, HD)
        sum_ref[j] = jnp.dot(mine_ref[...], weight_ref[:, pl.ds(begin, width)], preferred_element_type=jnp.float32)


def project_other_kernel(other_ref, sum_ref, blocks_ref, out_ref):
    shares, _, width = out_ref.shape
    for j in range(shares):
        mixed = sum_ref[j] + jnp.dot(
            other_ref[...], blocks_ref[:, j * width:(j + 1) * width], preferred_element_type=jnp.float32
        )
        out_ref[j] = mixed.astype(jnp.bfloat16)


def vmem_specs(count):
    return [pl.BlockSpec(memory_space=pltpu.VMEM)] * count


def attend_cost(blocks):
    return pl.CostEstimate(
        flops=blocks * 4 * TILE * TILE * HD, bytes_accessed=4 << 20, transcendentals=blocks * TILE * TILE
    )


PARAMS = pltpu.CompilerParams(vmem_limit_bytes=16 * 1024 * 1024)


def per_device(seq_size, head_size, queries, key_states, value_states, block_list, text_slots, out_weight):
    width = queries.shape[1]
    heads = width // HD
    planes = seq_size // GROUP
    up = [(s, (s + GROUP) % seq_size) for s in range(seq_size)]
    down = [(s, (s - GROUP) % seq_size) for s in range(seq_size)]

    k_up, k_down, v_up, v_down = [key_states], [key_states], [value_states], [value_states]
    half = planes // 2
    for step in range(half):
        k_up.append(lax.ppermute(k_up[-1], "seq", up))
        if step < half - 1:
            k_down.append(lax.ppermute(k_down[-1], "seq", down))
            v_up.append(lax.ppermute(v_up[-1], "seq", up))
        v_down.append(lax.ppermute(v_down[-1], "seq", down))

    picked = pl.pallas_call(
        pick_kernel,
        out_shape=jax.ShapeDtypeStruct((width, head_size // 4 * width), out_weight.dtype),
        in_specs=vmem_specs(1),
        out_specs=pl.BlockSpec(memory_space=pltpu.VMEM),
        compiler_params=PARAMS,
        name="pick",
    )(out_weight)
    other_half = lax.ppermute(picked, "head", [(h, h ^ 1) for h in range(head_size)])
    other_swapped = lax.ppermute(other_half, "seq", [(s, s ^ 1) for s in range(seq_size)])

    listed = jnp.pad(
        block_list, ((0, PART_ROWS - 1), (0, width - block_list.shape[1])), constant_values=-1
    )
    packed = jnp.concatenate([queries, listed.astype(jnp.bfloat16)], axis=0)
    tiles = [packed] + [
        lax.ppermute(packed, "seq", [(s, s ^ k) for s in range(seq_size)]) for k in range(1, GROUP)
    ]
    order = (0, -1, 1, -3, 3, 4, -2, 2)

    rows = GROUP * heads
    state = (
        jax.ShapeDtypeStruct((rows, HD, TILE), jnp.float32),
        jax.ShapeDtypeStruct((rows, 1, TILE), jnp.float32),
        jax.ShapeDtypeStruct((rows, 1, TILE), jnp.float32),
    )
    factor = LOG2E / math.sqrt(HD)
    smem = [pl.BlockSpec(memory_space=pltpu.SMEM)]

    def scratch(count):
        return [
            pltpu.VMEM((count, TILE, width), jnp.bfloat16),
            pltpu.VMEM((count, heads, HD, TILE), jnp.bfloat16),
        ]

    need, stacked, *held = pl.pallas_call(
        functools.partial(near_kernel, factor, seq_size, order),
        out_shape=(
            jax.ShapeDtypeStruct((GROUP, len(order)), jnp.int32),
            jax.ShapeDtypeStruct((GROUP, TILE, width), jnp.bfloat16),
        )
        + state,
        in_specs=smem + vmem_specs(GROUP + 6),
        out_specs=tuple(smem + vmem_specs(4)),
        scratch_shapes=scratch(3),
        compiler_params=PARAMS,
        cost_estimate=attend_cost(27),
        name="attend_near",
    )(text_slots, *tiles, key_states, value_states, k_up[1], k_down[1], v_up[1], v_down[1])
    far = [(k_up[3], v_up[3]), (k_down[3], v_down[3]), (k_up[4], v_down[4]), (k_up[2], v_up[2]), (k_down[2], v_down[2])]
    keep, keep_sum, send = pl.pallas_call(
        functools.partial(far_kernel, factor, 3, len(far)),
        out_shape=(
            jax.ShapeDtypeStruct((2, width, TILE), jnp.float32),
            jax.ShapeDtypeStruct((2, 8, TILE), jnp.float32),
            jax.ShapeDtypeStruct((2, width + 2 * PART_ROWS, TILE), jnp.bfloat16),
        ),
        in_specs=smem + vmem_specs(1 + 2 * len(far) + 3),
        out_specs=tuple(vmem_specs(3)),
        scratch_shapes=[pltpu.VMEM(s.shape, s.dtype) for s in state] + scratch(len(far)),
        compiler_params=PARAMS,
        cost_estimate=attend_cost(27),
        name="attend_far",
    )(need, stacked, *[k for k, _ in far], *[v for _, v in far], *held)

    other = lax.ppermute(send, "seq", [(s, s ^ 1) for s in range(seq_size)])
    keep, keep_sum, send = pl.pallas_call(
        merge_kernel,
        out_shape=(
            jax.ShapeDtypeStruct((1, width, TILE), jnp.float32),
            jax.ShapeDtypeStruct((1, 8, TILE), jnp.float32),
            jax.ShapeDtypeStruct((1, width + 2 * PART_ROWS, TILE), jnp.bfloat16),
        ),
        in_specs=vmem_specs(3),
        out_specs=tuple(vmem_specs(3)),
        compiler_params=PARAMS,
        name="merge",
    )(keep, keep_sum, other)
    other = lax.ppermute(send, "seq", [(s, s ^ 2) for s in range(seq_size)])
    attended = pl.pallas_call(
        finish_kernel,
        out_shape=jax.ShapeDtypeStruct((TILE, width), jnp.bfloat16),
        in_specs=vmem_specs(3),
        out_specs=pl.BlockSpec(memory_space=pltpu.VMEM),
        compiler_params=PARAMS,
        name="finish",
    )(keep, keep_sum, other)
    swap_side = [(h, h ^ 1) for h in range(head_size)]
    other = lax.ppermute(attended, "head", swap_side)
    sums, blocks = pl.pallas_call(
        project_own_kernel,
        out_shape=(
            jax.ShapeDtypeStruct((head_size // 2, TILE, width), jnp.float32),
            jax.ShapeDtypeStruct((width, head_size // 2 * width), out_weight.dtype),
        ),
        in_specs=vmem_specs(4),
        out_specs=tuple(vmem_specs(2)),
        compiler_params=PARAMS,
        name="project_own",
    )(attended, out_weight, other_half, other_swapped)
    shares = pl.pallas_call(
        project_other_kernel,
        out_shape=jax.ShapeDtypeStruct((head_size // 2, TILE, width), jnp.bfloat16),
        in_specs=vmem_specs(3),
        out_specs=pl.BlockSpec(memory_space=pltpu.VMEM),
        compiler_params=PARAMS,
        name="project_other",
    )(other, sums, blocks)
    sides = [list(range(k, head_size, 2)) for k in range(2)]
    shares = lax.all_to_all(shares, "head", 0, 0, axis_index_groups=sides, tiled=True)
    return jnp.sum(shares.astype(jnp.float32), axis=0).astype(jnp.bfloat16)


def solution(mesh):
    return jax.shard_map(
        functools.partial(per_device, mesh.shape["seq"], mesh.shape["head"]),
        mesh=mesh,
        in_specs=(
            P("seq", "head"),
            P("seq", "head"),
            P("seq", "head"),
            P("seq", None),
            P(),
            P("head", None),
        ),
        out_specs=P("seq", "head"),
        check_vma=False,
    )
```

```python
import functools
import math

import jax
import jax.numpy as jnp
from jax import lax
from jax.experimental import pallas as pl
from jax.experimental.pallas import tpu as pltpu
from jax.sharding import PartitionSpec as P

HD = 128
TILE = 256
GROUP = 4
PART_ROWS = 16
LOWEST = -1e30
LOG2E = math.log2(math.e)


def pack_part(ref, index, outs, sums):
    heads = len(outs)
    for h in range(heads):
        ref[index, h * HD:(h + 1) * HD, :] = outs[h].astype(jnp.bfloat16)
    rows = jnp.concatenate(sums, axis=0)
    high = rows.astype(jnp.bfloat16).astype(jnp.float32)
    middle = (rows - high).astype(jnp.bfloat16).astype(jnp.float32)
    low = rows - high - middle
    unused = jnp.zeros((PART_ROWS - 3 * heads, TILE), jnp.float32)
    base = heads * HD
    block = jnp.concatenate([high, middle, low, unused], axis=0)
    ref[index, base:base + PART_ROWS, :] = block.astype(jnp.bfloat16)


def unpack_sums(ref, index, heads):
    base = heads * HD
    block = ref[index, base:base + PART_ROWS, :].astype(jnp.float32)
    return block[0:heads] + block[heads:2 * heads] + block[2 * heads:3 * heads]


def merged(mine_ref, mine_sum_ref, mine, other_ref, other, heads):
    others = unpack_sums(other_ref, other, heads)
    outs, sums = [], []
    for h in range(heads):
        rows = slice(h * HD, (h + 1) * HD)
        own_sum = mine_sum_ref[mine, h:h + 1, :]
        other_sum = others[h:h + 1]
        top = jnp.maximum(own_sum, other_sum)
        own_weight = jnp.exp2(own_sum - top)
        other_weight = jnp.exp2(other_sum - top)
        total = own_weight + other_weight
        outs.append(
            mine_ref[mine, rows, :] * (own_weight / total)
            + other_ref[other, rows, :].astype(jnp.float32) * (other_weight / total)
        )
        sums.append(top + jnp.log2(total))
    return outs, sums


def load_shards(need_ref, first, shards, k_ref, vt_ref):
    for j, (key, value) in enumerate(shards):
        wanted = need_ref[0, first + j]
        for t in range(1, need_ref.shape[0]):
            wanted = wanted + need_ref[t, first + j]

        @pl.when(wanted > 0)
        def _():
            k_ref[j] = key[...]
            for h in range(vt_ref.shape[1]):
                vt_ref[j, h] = value[:, h * HD:(h + 1) * HD].T


def visit_shards(factor, need_ref, first, count, q_ref, k_ref, vt_ref, state):
    acc_ref, peak_ref, total_ref = state
    heads = vt_ref.shape[1]

    def take(t, picks):
        def scores_of(h):
            cols = slice(h * HD, (h + 1) * HD)
            return [
                lax.dot_general(
                    k_ref[j, :, cols],
                    q_ref[t, :, cols],
                    (((1,), (1,)), ((), ())),
                    preferred_element_type=jnp.float32,
                )
                for j in picks
            ]

        following = scores_of(0)
        for h in range(heads):
            scores = following
            if h + 1 < heads:
                following = scores_of(h + 1)
            row = t * heads + h
            old = peak_ref[row]
            tops = [jnp.max(part, axis=0, keepdims=True) for part in scores]
            peak = jnp.maximum(old, functools.reduce(jnp.maximum, tops) * factor)
            weights = [jnp.exp2(part * factor - peak) for part in scores]
            shrink = jnp.exp2(old - peak)
            sums = [jnp.sum(w, axis=0, keepdims=True) for w in weights]
            dots = [
                jnp.dot(vt_ref[j, h], w.astype(jnp.bfloat16), preferred_element_type=jnp.float32)
                for j, w in zip(picks, weights)
            ]
            peak_ref[row] = peak
            total_ref[row] = total_ref[row] * shrink + sum(sums[1:], sums[0])
            acc_ref[row] = acc_ref[row] * shrink + sum(dots[1:], dots[0])

    def visit(t, carry):
        picks = [jnp.int32(0)] * count
        seen = jnp.int32(0)
        for j in range(count):
            wanted = need_ref[t, first + j]
            for i in range(j + 1):
                picks[i] = jnp.where((wanted > 0) & (seen == i), j, picks[i])
            seen = seen + wanted

        @pl.when(seen >= 3)
        def _():
            take(t, picks[:3])

        @pl.when((seen == 2) | (seen == 5))
        def _():
            take(t, [jnp.where(seen == 5, late, early) for late, early in zip(picks[-2:], picks[:2])])

        @pl.when((seen == 1) | (seen == 4))
        def _():
            take(t, [jnp.where(seen == 4, picks[min(3, count - 1)], picks[0])])

        return carry

    lax.fori_loop(0, q_ref.shape[0], visit, 0)


def list_wanted(seq_size, order, text_ref, q_refs, need_ref):
    me = lax.axis_index("seq")
    slots = [lax.rem(me + (GROUP * plane + seq_size), seq_size) for plane in order]
    for t, q_ref in enumerate(q_refs):
        row = q_ref[TILE:TILE + PART_ROWS, 0:HD].astype(jnp.float32)
        bits = jnp.zeros_like(row)
        for j, slot in enumerate(slots):
            bits = bits + jnp.where(row == slot.astype(jnp.float32), float(1 << j), 0.0)
        code = jnp.sum(bits).astype(jnp.int32)
        for j, slot in enumerate(slots):
            wanted = (code >> j) & 1
            for i in range(text_ref.shape[0]):
                wanted = jnp.where(slot == text_ref[i], 1, wanted)
            need_ref[t, j] = wanted


def near_kernel(factor, seq_size, order, text_ref, *refs):
    q_refs, (k_own, v_own, k_low, k_high, v_low, v_high) = refs[:GROUP], refs[GROUP:GROUP + 6]
    need_ref, stacked_ref, acc_ref, peak_ref, total_ref, k_ref, vt_ref = refs[GROUP + 6:]
    list_wanted(seq_size, order, text_ref, q_refs, need_ref)
    acc_ref[...] = jnp.zeros_like(acc_ref)
    peak_ref[...] = jnp.full_like(peak_ref, LOWEST)
    total_ref[...] = jnp.zeros_like(total_ref)
    for t, q_ref in enumerate(q_refs):
        stacked_ref[t] = q_ref[0:TILE, :]
    shards = [(k_own, v_own), (k_low, v_low), (k_high, v_high)]
    load_shards(need_ref, 0, shards, k_ref, vt_ref)
    visit_shards(factor, need_ref, 0, 3, stacked_ref, k_ref, vt_ref, (acc_ref, peak_ref, total_ref))


def far_kernel(factor, first, count, need_ref, stacked_ref, *refs):
    shards = list(zip(refs[:count], refs[count:2 * count]))
    held = refs[2 * count:2 * count + 3]
    keep_ref, keep_sum_ref, send_ref, *state, k_ref, vt_ref = refs[2 * count + 3:]
    heads = vt_ref.shape[1]
    for source, target in zip(held, state):
        target[...] = source[...]
    load_shards(need_ref, first, shards, k_ref, vt_ref)
    visit_shards(factor, need_ref, first, count, stacked_ref, k_ref, vt_ref, state)
    acc_ref, peak_ref, total_ref = state
    for t in range(GROUP):
        outs, sums = [], []
        for h in range(heads):
            row = t * heads + h
            total = total_ref[row]
            present = total > 0.0
            safe = jnp.where(present, total, 1.0)
            outs.append(acc_ref[row] * (1.0 / safe))
            sums.append(jnp.where(present, peak_ref[row] + jnp.log2(safe), LOWEST))
        if t % 2:
            pack_part(send_ref, t // 2, outs, sums)
        else:
            for h in range(heads):
                keep_ref[t // 2, h * HD:(h + 1) * HD, :] = outs[h]
                keep_sum_ref[t // 2, h:h + 1, :] = sums[h]


def merge_kernel(mine_ref, mine_sum_ref, other_ref, keep_ref, keep_sum_ref, send_ref):
    heads = mine_ref.shape[1] // HD
    outs, sums = merged(mine_ref, mine_sum_ref, 1, other_ref, 1, heads)
    pack_part(send_ref, 0, outs, sums)
    outs, sums = merged(mine_ref, mine_sum_ref, 0, other_ref, 0, heads)
    for h in range(heads):
        keep_ref[0, h * HD:(h + 1) * HD, :] = outs[h]
        keep_sum_ref[0, h:h + 1, :] = sums[h]


def finish_kernel(mine_ref, mine_sum_ref, other_ref, out_ref):
    heads = mine_ref.shape[1] // HD
    outs, _ = merged(mine_ref, mine_sum_ref, 0, other_ref, 0, heads)
    for h in range(heads):
        out_ref[:, h * HD:(h + 1) * HD] = outs[h].T.astype(jnp.bfloat16)


def pick_kernel(weight_ref, out_ref):
    width = weight_ref.shape[0]
    count = out_ref.shape[1] // width
    side = lax.rem(lax.axis_index("head"), 2)
    core = lax.rem(lax.axis_index("seq"), 2)
    for j in range(count):
        begin = pl.multiple_of((2 * (core * count + j) + 1 - side) * width, HD)
        out_ref[:, j * width:(j + 1) * width] = weight_ref[:, pl.ds(begin, width)]


def project_own_kernel(mine_ref, weight_ref, half_ref, swapped_ref, sum_ref, blocks_ref):
    shares, _, width = sum_ref.shape
    side = lax.rem(lax.axis_index("head"), 2)
    core = lax.rem(lax.axis_index("seq"), 2)
    half = half_ref.shape[1]
    blocks_ref[:, pl.ds(pl.multiple_of(core * half, HD), half)] = half_ref[...]
    blocks_ref[:, pl.ds(pl.multiple_of((1 - core) * half, HD), half)] = swapped_ref[...]
    for j in range(shares):
        begin = pl.multiple_of((2 * j + side) * width, HD)
        sum_ref[j] = jnp.dot(mine_ref[...], weight_ref[:, pl.ds(begin, width)], preferred_element_type=jnp.float32)


def project_other_kernel(other_ref, sum_ref, blocks_ref, out_ref):
    shares, _, width = out_ref.shape
    for j in range(shares):
        mixed = sum_ref[j] + jnp.dot(
            other_ref[...], blocks_ref[:, j * width:(j + 1) * width], preferred_element_type=jnp.float32
        )
        out_ref[j] = mixed.astype(jnp.bfloat16)


def vmem_specs(count):
    return [pl.BlockSpec(memory_space=pltpu.VMEM)] * count


def attend_cost(blocks):
    return pl.CostEstimate(
        flops=blocks * 4 * TILE * TILE * HD, bytes_accessed=4 << 20, transcendentals=blocks * TILE * TILE
    )


PARAMS = pltpu.CompilerParams(vmem_limit_bytes=16 * 1024 * 1024)


def per_device(seq_size, head_size, queries, key_states, value_states, block_list, text_slots, out_weight):
    width = queries.shape[1]
    heads = width // HD
    planes = seq_size // GROUP
    up = [(s, (s + GROUP) % seq_size) for s in range(seq_size)]
    down = [(s, (s - GROUP) % seq_size) for s in range(seq_size)]

    k_up, k_down, v_up, v_down = [key_states], [key_states], [value_states], [value_states]
    half = planes // 2
    for step in range(half):
        k_up.append(lax.ppermute(k_up[-1], "seq", up))
        if step < half - 1:
            k_down.append(lax.ppermute(k_down[-1], "seq", down))
            v_up.append(lax.ppermute(v_up[-1], "seq", up))
        v_down.append(lax.ppermute(v_down[-1], "seq", down))

    picked = pl.pallas_call(
        pick_kernel,
        out_shape=jax.ShapeDtypeStruct((width, head_size // 4 * width), out_weight.dtype),
        in_specs=vmem_specs(1),
        out_specs=pl.BlockSpec(memory_space=pltpu.VMEM),
        compiler_params=PARAMS,
        name="pick",
    )(out_weight)
    other_half = lax.ppermute(picked, "head", [(h, h ^ 1) for h in range(head_size)])
    other_swapped = lax.ppermute(other_half, "seq", [(s, s ^ 1) for s in range(seq_size)])

    listed = jnp.pad(
        block_list, ((0, PART_ROWS - 1), (0, width - block_list.shape[1])), constant_values=-1
    )
    packed = jnp.concatenate([queries, listed.astype(jnp.bfloat16)], axis=0)
    tiles = [packed] + [
        lax.ppermute(packed, "seq", [(s, s ^ k) for s in range(seq_size)]) for k in range(1, GROUP)
    ]
    order = (0, -1, 1, -3, 3, 4, -2, 2)

    rows = GROUP * heads
    state = (
        jax.ShapeDtypeStruct((rows, HD, TILE), jnp.float32),
        jax.ShapeDtypeStruct((rows, 1, TILE), jnp.float32),
        jax.ShapeDtypeStruct((rows, 1, TILE), jnp.float32),
    )
    factor = LOG2E / math.sqrt(HD)
    smem = [pl.BlockSpec(memory_space=pltpu.SMEM)]

    def scratch(count):
        return [
            pltpu.VMEM((count, TILE, width), jnp.bfloat16),
            pltpu.VMEM((count, heads, HD, TILE), jnp.bfloat16),
        ]

    need, stacked, *held = pl.pallas_call(
        functools.partial(near_kernel, factor, seq_size, order),
        out_shape=(
            jax.ShapeDtypeStruct((GROUP, len(order)), jnp.int32),
            jax.ShapeDtypeStruct((GROUP, TILE, width), jnp.bfloat16),
        )
        + state,
        in_specs=smem + vmem_specs(GROUP + 6),
        out_specs=tuple(smem + vmem_specs(4)),
        scratch_shapes=scratch(3),
        compiler_params=PARAMS,
        cost_estimate=attend_cost(27),
        name="attend_near",
    )(text_slots, *tiles, key_states, value_states, k_up[1], k_down[1], v_up[1], v_down[1])
    far = [(k_up[3], v_up[3]), (k_down[3], v_down[3]), (k_up[4], v_down[4]), (k_up[2], v_up[2]), (k_down[2], v_down[2])]
    keep, keep_sum, send = pl.pallas_call(
        functools.partial(far_kernel, factor, 3, len(far)),
        out_shape=(
            jax.ShapeDtypeStruct((2, width, TILE), jnp.float32),
            jax.ShapeDtypeStruct((2, 8, TILE), jnp.float32),
            jax.ShapeDtypeStruct((2, width + PART_ROWS, TILE), jnp.bfloat16),
        ),
        in_specs=smem + vmem_specs(1 + 2 * len(far) + 3),
        out_specs=tuple(vmem_specs(3)),
        scratch_shapes=[pltpu.VMEM(s.shape, s.dtype) for s in state] + scratch(len(far)),
        compiler_params=PARAMS,
        cost_estimate=attend_cost(27),
        name="attend_far",
    )(need, stacked, *[k for k, _ in far], *[v for _, v in far], *held)

    other = lax.ppermute(send, "seq", [(s, s ^ 1) for s in range(seq_size)])
    keep, keep_sum, send = pl.pallas_call(
        merge_kernel,
        out_shape=(
            jax.ShapeDtypeStruct((1, width, TILE), jnp.float32),
            jax.ShapeDtypeStruct((1, 8, TILE), jnp.float32),
            jax.ShapeDtypeStruct((1, width + PART_ROWS, TILE), jnp.bfloat16),
        ),
        in_specs=vmem_specs(3),
        out_specs=tuple(vmem_specs(3)),
        compiler_params=PARAMS,
        name="merge",
    )(keep, keep_sum, other)
    other = lax.ppermute(send, "seq", [(s, s ^ 2) for s in range(seq_size)])
    attended = pl.pallas_call(
        finish_kernel,
        out_shape=jax.ShapeDtypeStruct((TILE, width), jnp.bfloat16),
        in_specs=vmem_specs(3),
        out_specs=pl.BlockSpec(memory_space=pltpu.VMEM),
        compiler_params=PARAMS,
        name="finish",
    )(keep, keep_sum, other)
    swap_side = [(h, h ^ 1) for h in range(head_size)]
    other = lax.ppermute(attended, "head", swap_side)
    sums, blocks = pl.pallas_call(
        project_own_kernel,
        out_shape=(
            jax.ShapeDtypeStruct((head_size // 2, TILE, width), jnp.float32),
            jax.ShapeDtypeStruct((width, head_size // 2 * width), out_weight.dtype),
        ),
        in_specs=vmem_specs(4),
        out_specs=tuple(vmem_specs(2)),
        compiler_params=PARAMS,
        name="project_own",
    )(attended, out_weight, other_half, other_swapped)
    shares = pl.pallas_call(
        project_other_kernel,
        out_shape=jax.ShapeDtypeStruct((head_size // 2, TILE, width), jnp.bfloat16),
        in_specs=vmem_specs(3),
        out_specs=pl.BlockSpec(memory_space=pltpu.VMEM),
        compiler_params=PARAMS,
        name="project_other",
    )(other, sums, blocks)
    sides = [list(range(k, head_size, 2)) for k in range(2)]
    shares = lax.all_to_all(shares, "head", 0, 0, axis_index_groups=sides, tiled=True)
    return jnp.sum(shares.astype(jnp.float32), axis=0).astype(jnp.bfloat16)


def solution(mesh):
    return jax.shard_map(
        functools.partial(per_device, mesh.shape["seq"], mesh.shape["head"]),
        mesh=mesh,
        in_specs=(
            P("seq", "head"),
            P("seq", "head"),
            P("seq", "head"),
            P("seq", None),
            P(),
            P("head", None),
        ),
        out_specs=P("seq", "head"),
        check_vma=False,
    )
```
